32 devices in a mesh: rows: 16 (over z, y, core), heads: 2 (over x).
Axes of the slice: x: 2, y: 2, z: 4, core: 2. Of those that a mesh axis runs over, the one named last changes fastest.
Arguments:
- tokens: bfloat16 [4096, 2048], P('rows', 'heads'), may hold values from -6 to 6
- cotangent: bfloat16 [4, 4096, 2048], P(None, 'rows', 'heads'), may hold values from -6 to 6
- doc_lengths: int32 [16], replicated, may hold values from 1 to 3976, as said below
- input_gain: float32 [2048], replicated, may hold values from 0.1 to 1.9
- input_weight: bfloat16 [2048, 32, 256], P('rows', None, 'heads'), may hold values from -0.125 to 0.125
- step_weight: bfloat16 [2048, 2, 32], P('rows', 'heads'), may hold values from -0.125 to 0.125
- state_weight: bfloat16 [2048, 256], replicated, may hold values from -0.125 to 0.125
- conv_inner: float32 [4, 4096], replicated, may hold values from -3 to 3
- conv_inner_bias: float32 [4096], replicated, may hold values from -1.5 to 1.5
- conv_state: float32 [4, 256], replicated, may hold values from -3 to 3
- conv_state_bias: float32 [256], replicated, may hold values from -1.5 to 1.5
- step_bias: float32 [64], replicated, may hold values from -12 to -3, as said below
- decay_log: float32 [64], replicated, may hold values from -6 to 1, as said below
- skip_gain: float32 [64], replicated, may hold values from 0.5 to 1.5
- gated_gain: float32 [4096], replicated, may hold values from 0.1 to 1.9
- output_weight: bfloat16 [32, 128, 2048], P(None, 'heads', 'rows'), may hold values from -0.125 to 0.125
Outputs:
- mixed: bfloat16 [4, 4096, 2048], P(None, 'rows', 'heads')
- tokens_grad: float32 [4096, 2048], P('rows', 'heads')
- input_gain_grad: float32 [2048], replicated
- input_weight_grad: float32 [2048, 32, 256], P('rows', None, 'heads')
- step_weight_grad: float32 [2048, 2, 32], P('rows', 'heads')
- state_weight_grad: float32 [2048, 256], replicated
- conv_inner_grad: float32 [4, 4096], replicated
- conv_inner_bias_grad: float32 [4096], replicated
- conv_state_grad: float32 [4, 256], replicated
- conv_state_bias_grad: float32 [256], replicated
- step_bias_grad: float32 [64], replicated
- decay_log_grad: float32 [64], replicated
- skip_gain_grad: float32 [64], replicated
- gated_gain_grad: float32 [4096], replicated
- output_weight_grad: float32 [32, 128, 2048], P(None, 'heads', 'rows')
The draws below stay inside these ranges and needn't reach their ends.
Inputs may be any that keep to these rules, and one draw needn't show every extreme that they name: `doc_lengths`: the lengths add up to 4096. One document, at a place drawn from the seed, is exactly as long as the stated most; it starts among the first 256 tokens and ends among the last 256. Every other document has at most 16 tokens, and one of them has exactly 1. `step_bias`: A value for each head. `decay_log`: A value for each head.
All inputs are finite; a program needn't handle non-finite values.
Results may differ from the reference program's by a relative error of at most 0.011.
The reference program's roundings to bfloat16 on the way count: a program that leaves them out, or rounds other values in their place, can miss the bound.
Values may be sent and summed in bfloat16 or wider, within the bound.
No kernel may reach another device: no remote copies, remote signals or barrier semaphores. Data moves between devices by JAX's collectives and lax.ppermute only.
A program may use at most 256 MiB of HBM per device.

```python
import jax
import jax.numpy as jnp
from jax import lax

D = 2048
H = 64
P_SIZE = 64
STATE = 128
KERNEL = 4
SPAN = 256
DOCS = 16
TOK_DEV = 256
INNER = 4096
GROUPS = 32
LENGTH = 4096
N_HEADS = 2


def rate_pair(key, slow_share):
    first_key, second_key, third_key = jax.random.split(key, 3)
    slow = jax.random.uniform(first_key, (H,), minval=jnp.log(0.2 / LENGTH), maxval=jnp.log(1.0 / LENGTH))
    fast = jax.random.uniform(second_key, (H,), minval=jnp.log(1.0 / LENGTH), maxval=jnp.log(0.04))
    chosen = jax.random.uniform(third_key, (H,)) < slow_share
    rate = jnp.exp(jnp.where(chosen, slow, fast))
    step_size = 0.15 * jnp.sqrt(rate)
    return (rate, step_size)


def draw_step_bias(key, part):
    rate, step_size = rate_pair(key, 0.5)
    return jnp.log(jnp.expm1(step_size)).astype(jnp.float32)


def draw_decay_log(key, part):
    rate, step_size = rate_pair(key, 0.5)
    return (jnp.log(rate) - jnp.log(step_size)).astype(jnp.float32)


def draw_doc_lengths(key, part):
    key = jax.random.fold_in(key, 7)
    first_key, second_key, third_key = jax.random.split(key, 3)
    short_most = TOK_DEV // DOCS
    pair_count = (DOCS - 2) // 2
    halves = jax.random.randint(first_key, (pair_count,), 1, short_most + 1)
    others = jnp.concatenate([halves, short_most + 1 - halves, jnp.ones((1,), jnp.int32)])
    others = jax.random.permutation(third_key, others)
    longest = jax.random.randint(second_key, (), 0, DOCS)
    index = jnp.arange(DOCS)
    is_long = index == longest
    source = jnp.clip(index - (index > longest).astype(jnp.int32), 0, DOCS - 2)
    long_length = LENGTH - pair_count * (short_most + 1) - 1
    return jnp.where(is_long, long_length, others[source]).astype(jnp.int32)


def spiked(drawn, own_key, source, target, blocks, factor):
    def block_of(axis_at):
        return (jnp.arange(drawn.shape[axis_at]) // (drawn.shape[axis_at] // blocks)).reshape((-1,) + (1,) * (drawn.ndim - 1 - axis_at))

    first = jax.random.permutation(own_key, blocks)[block_of(target)]
    far = (block_of(target) + blocks // 2) % blocks
    return jnp.where((block_of(source) == first) | (block_of(source) == far), factor * drawn, drawn)


def block_scale(rng, shape, cuts, least, high):
    def one(axis_at, shards_of):
        heights = jax.random.uniform(jax.random.fold_in(jax.random.fold_in(rng, 6), axis_at), (shards_of,), jnp.float32, least / len(cuts), high / len(cuts))
        return jnp.repeat(jnp.exp(heights), shape[axis_at] // shards_of).reshape((-1,) + (1,) * (len(shape) - axis_at - 1))

    loudness = one(*cuts[0])
    for cut in cuts[1:]:
        loudness = loudness * one(*cut)
    return loudness


def bell_draw(own_key, extent, width, limit, pieces=(), kind=jnp.bfloat16):
    values = jax.random.normal(own_key, extent, jnp.float32) * width
    if len(pieces) > 0:
        values = block_scale(own_key, extent, pieces, -0.22, 0.18) * values
    return jnp.clip(values, min=-limit, max=limit).astype(kind)


def gaussian_with(rng, dims, width, limit, cuts, heavy, kind=jnp.bfloat16):
    entries = width * jax.random.normal(rng, dims, jnp.float32)
    if cuts:
        entries = entries * block_scale(rng, dims, cuts, -0.22, 0.18)
    return jnp.clip(spiked(entries, jax.random.fold_in(rng, 3), *heavy), -limit, limit).astype(kind)


def setup_inputs(seed: int = 0) -> dict:
    key_of = jax.random.split(jax.random.key(seed), 17)
    return {
        "tokens": bell_draw(key_of[0], (LENGTH, D), 1.0, 6.0, ((0, 16), (1, 2))),
        "cotangent": bell_draw(key_of[1], (4, LENGTH, D), 1.0, 6.0, ((1, 16), (2, 2))),
        "doc_lengths": draw_doc_lengths(jax.random.fold_in(key_of[16], 71), 0),
        "input_gain": jnp.clip(1.0 + 0.18 * jax.random.normal(key_of[3], (D,), jnp.float32), 0.1, 1.9),
        "input_weight": bell_draw(key_of[4], (D, GROUPS, N_HEADS * 2 * P_SIZE), D ** -0.5, 0.125, ((0, 16), (2, 2))),
        "step_weight": bell_draw(key_of[5], (D, N_HEADS, GROUPS), D ** -0.5, 0.125, ((0, 16), (1, 2))),
        "state_weight": bell_draw(key_of[6], (D, 2 * STATE), D ** -0.5, 0.125),
        "conv_inner": bell_draw(key_of[7], (KERNEL, INNER), KERNEL ** -0.5, 3.0, (), jnp.float32),
        "conv_inner_bias": bell_draw(key_of[8], (INNER,), 0.3, 1.5, (), jnp.float32),
        "conv_state": bell_draw(key_of[9], (KERNEL, 2 * STATE), KERNEL ** -0.5, 3.0, (), jnp.float32),
        "conv_state_bias": bell_draw(key_of[10], (2 * STATE,), 0.3, 1.5, (), jnp.float32),
        "step_bias": draw_step_bias(jax.random.fold_in(key_of[16], 71), 0),
        "decay_log": draw_decay_log(jax.random.fold_in(key_of[16], 71), 0),
        "skip_gain": jnp.clip(jax.random.uniform(key_of[13], (H,), jnp.float32, 0.5, 1.5), 0.5, 1.5),
        "gated_gain": jnp.clip(1.0 + 0.18 * jax.random.normal(key_of[14], (INNER,), jnp.float32), 0.1, 1.9),
        "output_weight": gaussian_with(key_of[15], (GROUPS, N_HEADS * P_SIZE, D), INNER ** -0.5, 0.125, ((1, 2), (2, 16)), (1, 2, 16, 2.0)),
    }


eps = 1e-05
highest = lax.Precision.HIGHEST

@jax.custom_vjp
def low(v):
    return lax.optimization_barrier(v.astype(jnp.bfloat16)).astype(jnp.float32)

@jax.custom_vjp
def low_back(v):
    return v

def low_keep(v):
    return (low(v), None)

def low_pass(kept, grad):
    return (grad,)

def back_keep(v):
    return (v, None)

def back_low(kept, grad):
    return (low(grad),)
low.defvjp(low_keep, low_pass)
low_back.defvjp(back_keep, back_low)

def doc_matches(positions, starts, tap_count):
    doc_index = lax.optimization_barrier(jnp.sum((positions[:, None] >= starts[None, :]).astype(jnp.int32), axis=1))
    row_count = positions.shape[0] - tap_count + 1
    compared = [(doc_index[offset:offset + row_count] == doc_index[tap_count - 1:]).astype(jnp.float32) for offset in range(tap_count)]
    return jnp.stack(compared)

def conv_apply(extended, kernel, bias_row, matches):
    row_count = matches.shape[1]
    summed = bias_row[None, :] + jnp.zeros((row_count, kernel.shape[1]), jnp.float32)
    for offset in range(kernel.shape[0]):
        summed = summed + kernel[offset][None, :] * extended[offset:offset + row_count] * matches[offset][:, None]
    return jax.nn.silu(summed)

def span_terms(inner_block, in_block, step_block, decay_block, reset_block):
    cumulative = jnp.cumsum(decay_block, axis=0)
    segment = jnp.cumsum(reset_block)
    to_end = jnp.where((segment == segment[-1])[:, None], jnp.exp(cumulative[-1][None, :] - cumulative), 0.0)
    local_state = jnp.einsum('jh,jh,jhp,jn->hpn', to_end, step_block, inner_block, in_block, precision=highest)
    span_decay = jnp.where(segment[-1] == 0, jnp.exp(cumulative[-1]), 0.0)
    return (local_state, span_decay)

def span_output(inner_block, in_block, out_block, step_block, decay_block, reset_block, entering):
    cumulative = jnp.cumsum(decay_block, axis=0)
    segment = jnp.cumsum(reset_block)
    position = jnp.arange(inner_block.shape[0])
    allowed = (segment[:, None] == segment[None, :]) & (position[:, None] >= position[None, :])
    spread = cumulative[:, None, :] - cumulative[None, :, :]
    weights = jnp.where(allowed[:, :, None], jnp.exp(jnp.where(allowed[:, :, None], spread, 0.0)), 0.0)
    scores = jnp.dot(out_block, in_block.T, precision=highest)
    within = jnp.einsum('ijh,ij,jh,jhp->ihp', weights, scores, step_block, inner_block, precision=highest)
    entry_weight = jnp.where((segment == 0)[:, None], jnp.exp(cumulative), 0.0)
    carried = jnp.einsum('in,hpn->ihp', out_block, entering, precision=highest) * entry_weight[:, :, None]
    return within + carried

def state_scan(inner_heads, in_vec, out_vec, step_size, decay, resets):
    span_total = inner_heads.shape[0] // SPAN

    def to_blocks(values):
        return values.reshape((span_total, SPAN) + values.shape[1:])

    def advance(state, element):
        inner_block, in_block, out_block, step_block, decay_block, reset_block = element
        result = span_output(inner_block, in_block, out_block, step_block, decay_block, reset_block, state)
        local_state, span_decay = span_terms(inner_block, in_block, step_block, decay_block, reset_block)
        return (span_decay[:, None, None] * state + local_state, result)
    initial = jnp.zeros((H, P_SIZE, STATE), jnp.float32)
    elements = (to_blocks(inner_heads), to_blocks(in_vec), to_blocks(out_vec), to_blocks(step_size), to_blocks(decay), to_blocks(resets))
    final_state, outputs = lax.scan(jax.checkpoint(advance), initial, elements)
    return outputs.reshape(inner_heads.shape)

def forward_layer(tokens, input_gain, input_weight, step_weight, state_weight, conv_inner, conv_inner_bias, conv_state, conv_state_bias, step_bias, decay_log, skip_gain, gated_gain, output_weight, matches, resets):
    length_all = tokens.shape[0]
    pad_rows = KERNEL - 1
    mean_square = lax.optimization_barrier(jnp.mean(tokens * tokens, axis=1, keepdims=True))
    normed = low(tokens * lax.rsqrt(mean_square + eps) * input_gain[None, :])
    input_view = input_weight.reshape(D, H * 2 * P_SIZE)
    projected = low_back(low(jnp.dot(normed, input_view, precision=highest))).reshape(length_all, H, 2, P_SIZE)
    gate_z = projected[:, :, 0, :]
    inner_pre = projected[:, :, 1, :].reshape(length_all, INNER)
    step_view = jnp.transpose(step_weight, (0, 2, 1)).reshape(D, H)
    step_raw = low_back(jnp.dot(normed, step_view, precision=highest))
    state_pre = low_back(low(jnp.dot(normed, state_weight, precision=highest)))
    inner_act = low(conv_apply(jnp.pad(inner_pre, ((pad_rows, 0), (0, 0))), conv_inner, conv_inner_bias, matches))
    state_act = low(conv_apply(jnp.pad(state_pre, ((pad_rows, 0), (0, 0))), conv_state, conv_state_bias, matches))
    inner_heads = inner_act.reshape(length_all, H, P_SIZE)
    step_size = jax.nn.softplus(step_raw + step_bias[None, :])
    decay = -step_size * jnp.exp(decay_log)[None, :]
    scanned = state_scan(inner_heads, state_act[:, :STATE], state_act[:, STATE:], step_size, decay, resets)
    gated = (scanned + skip_gain[None, :, None] * inner_heads) * jax.nn.silu(gate_z)
    squares = lax.optimization_barrier(jnp.sum(gated * gated, axis=2))
    scaled_u = low(gated.reshape(length_all, INNER) * gated_gain[None, :])
    output_view = output_weight.reshape(INNER, D)
    results = []
    for level_index in range(4):
        heads_kept = H >> level_index
        width_kept = heads_kept * P_SIZE
        factor = lax.rsqrt(lax.optimization_barrier(jnp.sum(squares[:, :heads_kept], axis=1)) / width_kept + eps)
        product = low_back(jnp.dot(scaled_u[:, :width_kept], output_view[:width_kept], precision=highest))
        results.append(tokens + factor[:, None] * product)
    return jnp.stack(results)

def reference(tokens, cotangent, doc_lengths, input_gain, input_weight, step_weight, state_weight, conv_inner, conv_inner_bias, conv_state, conv_state_bias, step_bias, decay_log, skip_gain, gated_gain, output_weight):
    starts = (jnp.cumsum(doc_lengths) - doc_lengths).astype(jnp.int32)
    positions = jnp.arange(-(KERNEL - 1), LENGTH, dtype=jnp.int32)
    matches = doc_matches(positions, starts, KERNEL)
    resets = jnp.any(positions[KERNEL - 1:, None] == starts[None, :], axis=1).astype(jnp.int32)
    values_in = (tokens.astype(jnp.float32), input_gain, input_weight.astype(jnp.float32), step_weight.astype(jnp.float32), state_weight.astype(jnp.float32), conv_inner, conv_inner_bias, conv_state, conv_state_bias, step_bias, decay_log, skip_gain, gated_gain, output_weight.astype(jnp.float32))

    def wrapped(*values):
        return forward_layer(*values, matches, resets)
    mixed, pullback = jax.vjp(wrapped, *values_in)
    grads = pullback(cotangent.astype(jnp.float32))
    return (mixed.astype(jnp.bfloat16), grads[0], grads[1], grads[2], grads[3], grads[4], grads[5], grads[6], grads[7], grads[8], grads[9], grads[10], grads[11], grads[12], grads[13])
```

```python
from functools import partial

import jax
import jax.numpy as jnp
from jax import lax
from jax.experimental import pallas as pl
from jax.experimental.pallas import tpu as pltpu
from jax.sharding import Mesh
from jax.sharding import PartitionSpec as P

D = 2048
P_SIZE = 64
STATE = 128
KERNEL = 4
INNER = 4096
CHUNK = 128
PLANE = 4

HALF_TOP = 16384.0

eps = 1e-05
bf16 = jnp.bfloat16
f32 = jnp.float32
high = lax.Precision.HIGHEST
PARAMS = pltpu.CompilerParams(
    vmem_limit_bytes=48 * 1024 * 1024, dimension_semantics=("arbitrary",)
)


def swap(block, axis, bit):
    return lax.ppermute(block, axis, [(a, a ^ bit) for a in range(lax.axis_size(axis))])


def shifted(block, axis, distance):
    devices = range(lax.axis_size(axis))
    route = [(a - distance, a) for a in devices if a - distance in devices]
    return lax.ppermute(block, axis, route)


def bits_of(axis):
    count = lax.axis_size(axis)
    return [1 << b for b in range(count.bit_length() - 1)]


def take(values, index, axis=0):
    return lax.dynamic_index_in_dim(values, index, axis, keepdims=False)


def put(buffer, piece, index):
    return lax.dynamic_update_index_in_dim(buffer, piece, index, 0)


def add_all(value, axes):
    for axis in axes:
        for bit in bits_of(axis):
            value = value + swap(value, axis, bit)
    return value


def stack_all(value, axes):
    whole = value[None]
    for axis in reversed(axes):
        place = lax.axis_index(axis)
        for bit in bits_of(axis):
            other = swap(whole, axis, bit)
            upper = (place & bit) != 0
            whole = jnp.where(
                upper,
                jnp.concatenate([other, whole], axis=0),
                jnp.concatenate([whole, other], axis=0),
            )
    return whole


def gather_inner(block):
    place = lax.axis_index("i")
    core = swap(block, "i", 1)
    across = swap(block, "i", 2)
    both = swap(across, "i", 1)
    out = jnp.zeros((PLANE,) + block.shape, block.dtype)
    for bit, piece in ((0, block), (1, core), (2, across), (3, both)):
        out = put(out, piece, place ^ bit)
    return out


def exchange_inner(blocks):
    place = lax.axis_index("i")
    out = blocks
    for bit in range(1, PLANE):
        out = put(out, swap(take(blocks, place ^ bit), "i", bit), place ^ bit)
    return out


def scatter_inner(parts):
    place = lax.axis_index("i")
    core, row = place & 1, place >> 1
    shaped = parts.reshape((2, 2) + parts.shape[1:])
    got = swap(take(shaped, 1 - core, 1).astype(bf16), "i", 1)
    half = take(shaped, core, 1) + got.astype(f32)
    got = swap(take(half, 1 - row).astype(bf16), "i", 2)
    return take(half, row) + got.astype(f32)


def gather_heads(block, axis):
    if lax.axis_size("h") != 2:
        return lax.all_gather(block, "h", axis=axis, tiled=True)
    other = swap(block, "h", 1)
    upper = lax.axis_index("h") != 0
    return jnp.where(
        upper,
        jnp.concatenate([other, block], axis=axis),
        jnp.concatenate([block, other], axis=axis),
    )


def scatter_heads(values, axis):
    count = lax.axis_size("h")
    if count != 2:
        return lax.psum_scatter(values, "h", scatter_dimension=axis, tiled=True)
    place = lax.axis_index("h")
    width = values.shape[axis] // 2
    sent = lax.dynamic_slice_in_dim(values, (1 - place) * width, width, axis)
    kept = lax.dynamic_slice_in_dim(values, place * width, width, axis)
    return kept + swap(sent.astype(bf16), "h", 1).astype(f32)


def to_half(values, largest):
    safe = jnp.maximum(largest, 1e-30)
    return (values * (HALF_TOP / safe)).astype(jnp.float16)


def from_half(values, largest):
    return values.astype(f32) * (jnp.maximum(largest, 1e-30) / HALF_TOP)


def chain(state, decay_wide, direction):
    count = lax.axis_size("o")
    largest = jnp.max(jnp.abs(state), axis=0, keepdims=True)
    sent = to_half(state, largest)
    rows = jnp.concatenate([largest, decay_wide, jnp.zeros((6, state.shape[1]), f32)], axis=0)
    total = None
    for distance in range(count - 1, 0, -1):
        got = shifted(rows, "o", direction * distance)
        own = from_half(shifted(sent, "o", direction * distance), got[0:1])
        total = own if total is None else own + got[1:2] * total
    return total


def mm(a, b):
    return jnp.dot(a, b, preferred_element_type=f32)


def mm_two(a, b):
    upper, lower = split_two(b)
    return mm(a, upper) + mm(a, lower)


def mm_three(a, b):
    a_up, a_low = split_two(a)
    b_up, b_low = split_two(b)
    return mm_t(a_up, b_up) + mm_t(a_up, b_low) + mm_t(a_low, b_up)


def mm_t(a, b):
    return lax.dot_general(a, b, (((1,), (1,)), ((), ())), preferred_element_type=f32)


def t_mm(a, b):
    return lax.dot_general(a, b, (((0,), (0,)), ((), ())), preferred_element_type=f32)


def head_mask(groups, width):
    head = lax.broadcasted_iota(jnp.int32, (groups, width), 0)
    lane = lax.broadcasted_iota(jnp.int32, (groups, width), 1)
    return (lane // P_SIZE == head).astype(f32).astype(bf16)


def split_two(values):
    upper = values.astype(bf16)
    return upper, (values - upper.astype(f32)).astype(bf16)


def widen(values, mask):
    upper, lower = split_two(values)
    return mm(upper, mask) + mm(lower, mask)


def fold(values, mask):
    upper, lower = split_two(values)
    return mm_t(upper, mask) + mm_t(lower, mask)


def pair_masks():
    lane = lax.broadcasted_iota(jnp.int32, (1, 2 * P_SIZE), 1)
    lower = (lane < P_SIZE).astype(f32)
    return lower.astype(bf16), (1.0 - lower).astype(bf16)


def rows_cols():
    row = lax.broadcasted_iota(jnp.int32, (CHUNK, CHUNK), 0)
    col = lax.broadcasted_iota(jnp.int32, (CHUNK, CHUNK), 1)
    return row, col


def within_kernel(groups, x_ref, st_ref, col_ref, row_ref, y_ref):
    b_in = st_ref[:, :STATE]
    c_out = st_ref[:, STATE:]
    scores = mm_t(c_out, b_in)
    doc_col = col_ref[:, 3 * groups : 3 * groups + 1]
    doc_row = row_ref[2 * groups : 2 * groups + 1, :]
    row, col = rows_cols()
    bias = jnp.where((doc_col == doc_row) & (row >= col), 0.0, -1e30)
    masks = pair_masks()
    for pair in range(groups // 2):
        lanes = slice(pair * 2 * P_SIZE, (pair + 1) * 2 * P_SIZE)
        x_pair = x_ref[:, lanes]
        weights, values = [], []
        for side in range(2):
            h = 2 * pair + side
            spread = jnp.exp(col_ref[:, h : h + 1] - row_ref[h : h + 1, :] + bias)
            weights.append(split_two(scores * spread * row_ref[groups + h : groups + h + 1, :]))
            values.append(x_pair * masks[side])
        value = jnp.concatenate(values, axis=0)
        y_ref[:, lanes] = mm(
            jnp.concatenate([weights[0][0], weights[1][0]], axis=1), value
        ) + mm(jnp.concatenate([weights[0][1], weights[1][1]], axis=1), value)


def carry_kernel(
    groups,
    x_ref,
    st_ref,
    stt_ref,
    col_ref,
    yl_ref,
    gz_ref,
    inc_ref,
    wide_ref,
    level_ref,
    v_ref,
    u_ref,
    sq_ref,
    enter_ref,
    state,
):
    @pl.when(pl.program_id(0) == 0)
    def _():
        state[...] = inc_ref[...]

    width = x_ref.shape[1]
    mask = head_mask(groups, width)
    cum = col_ref[:, :groups]
    step = col_ref[:, groups : 2 * groups]
    from_start = col_ref[:, 3 * groups + 1 : 3 * groups + 2]
    to_end = col_ref[:, 3 * groups + 2 : 3 * groups + 3]
    cum_last = cum[CHUNK - 1 : CHUNK, :]
    entry = jnp.exp(cum) * from_start
    ending = jnp.exp(cum_last - cum) * to_end * step
    entry_wide = widen(entry, mask)
    ending_wide = widen(ending, mask)
    held = state[...]
    enter_ref[...] = held
    carried = mm_two(st_ref[:, STATE:], held)
    x_wide = x_ref[...].astype(f32)
    v = yl_ref[...] + entry_wide * carried + wide_ref[0:1, :] * x_wide
    v_ref[...] = v
    z = gz_ref[...].astype(f32)
    gated = v * (z * jax.nn.sigmoid(z))
    u_ref[...] = (gated * wide_ref[1:2, :]).astype(bf16)
    upper, lower = split_two(gated * gated)
    sq_ref[...] = mm_t(level_ref[...], upper) + mm_t(level_ref[...], lower)
    added = mm_two(stt_ref[:STATE, :], x_wide * ending_wide)
    state[...] = entry_wide[CHUNK - 1 : CHUNK, :] * held + added


def gate_back_kernel(
    groups,
    ug_ref,
    v_ref,
    gz_ref,
    x_ref,
    stt_ref,
    col_ref,
    stat_ref,
    wide_ref,
    level_ref,
    yg_ref,
    zg_ref,
    acc_ref,
    lam_ref,
):
    @pl.when(pl.program_id(0) == 0)
    def _():
        acc_ref[...] = jnp.zeros_like(acc_ref)
        lam_ref[...] = jnp.zeros_like(lam_ref)

    mask = head_mask(groups, x_ref.shape[1])
    v = v_ref[...]
    z = gz_ref[...].astype(f32)
    sig = jax.nn.sigmoid(z)
    silu = z * sig
    gated = v * silu
    ug = ug_ref[...]
    upper, lower = split_two(stat_ref[...])
    stat = t_mm(upper, level_ref[...]) + t_mm(lower, level_ref[...])
    gated_grad = ug * wide_ref[1:2, :] + 2.0 * gated * stat
    y_grad = gated_grad * silu
    yg_ref[...] = y_grad
    zg_ref[...] = (gated_grad * v * (sig * (1.0 + z * (1.0 - sig)))).astype(bf16)
    acc_ref[0:1, :] += jnp.sum(ug * gated, axis=0, keepdims=True)
    acc_ref[1:2, :] += jnp.sum(y_grad * x_ref[...].astype(f32), axis=0, keepdims=True)
    whole_entry = widen(col_ref[:, 2 * groups : 3 * groups], mask)
    lam_ref[...] += mm_two(stt_ref[STATE:, :], y_grad * whole_entry)


def within_back_kernel(groups, x_ref, st_ref, col_ref, row_ref, yg_ref, dx_ref, dbc_ref, ds_ref):
    b_in = st_ref[:, :STATE]
    c_out = st_ref[:, STATE:]
    scores = mm_t(b_in, c_out)
    doc_col = col_ref[:, 3 * groups : 3 * groups + 1]
    doc_row = row_ref[2 * groups : 2 * groups + 1, :]
    row, col = rows_cols()
    same = doc_col == doc_row
    bias = jnp.where(same & (row <= col), 0.0, -1e30)
    masks = pair_masks()
    total = jnp.zeros((CHUNK, CHUNK), f32)
    head_lane = lax.broadcasted_iota(jnp.int32, (CHUNK, groups), 1)
    head_row = lax.broadcasted_iota(jnp.int32, (groups, CHUNK), 0)
    size_part = jnp.zeros((CHUNK, groups), f32)
    out_part = jnp.zeros((groups, CHUNK), f32)
    for pair in range(groups // 2):
        lanes = slice(pair * 2 * P_SIZE, (pair + 1) * 2 * P_SIZE)
        x_pair = x_ref[:, lanes]
        y_pair, y_rest = split_two(yg_ref[:, lanes])
        weights, values = [], []
        for side in range(2):
            h = 2 * pair + side
            step = col_ref[:, groups + h : groups + h + 1]
            spread = jnp.exp(row_ref[h : h + 1, :] - col_ref[:, h : h + 1] + bias)
            y_side = y_pair * masks[side]
            paired = spread * (mm_t(x_pair, y_side) + mm_t(x_pair, y_rest * masks[side]))
            total = total + step * paired
            product = scores * paired
            size_part = jnp.where(
                head_lane == h, jnp.sum(product, axis=1, keepdims=True), size_part
            )
            out_part = jnp.where(
                head_row == h, jnp.sum(step * product, axis=0, keepdims=True), out_part
            )
            weights.append((scores * spread).astype(bf16))
            values.append(y_side)
        dx_ref[:, lanes] = mm(jnp.concatenate(weights, axis=1), jnp.concatenate(values, axis=0))
    upper, lower = split_two(total)
    dbc_ref[:, :STATE] = mm(upper, c_out) + mm(lower, c_out)
    dbc_ref[:, STATE:] = t_mm(upper, b_in) + t_mm(lower, b_in)
    later = (same & (row <= col)).astype(f32)
    step_all = col_ref[:, groups : 2 * groups]
    ds_ref[:, :groups] = size_part
    ds_ref[:, groups:] = lax.dot_general(
        later, out_part, (((1,), (1,)), ((), ())), precision=high, preferred_element_type=f32
    ) - jnp.dot(later, step_all * size_part, precision=high, preferred_element_type=f32)


def conv_back_step(act_grad, pre, value, taps_ref, match, next_ref, sum_ref):
    sig = jax.nn.sigmoid(pre)
    slope = act_grad * (sig * (1.0 + pre * (1.0 - sig)))
    sum_ref[4:5, :] += jnp.sum(slope, axis=0, keepdims=True)
    sum_ref[3:4, :] += jnp.sum(slope * value, axis=0, keepdims=True)
    grad = taps_ref[3:4, :] * slope
    row = lax.broadcasted_iota(jnp.int32, (8, pre.shape[1]), 0)
    for k in range(KERNEL - 1):
        reach = KERNEL - 1 - k
        rolled = pltpu.roll(slope * match[k], CHUNK - reach, 0)
        last = rolled[CHUNK - 8 :]
        keep = row < 8 - reach
        after = next_ref[k * 8 : k * 8 + 8, :]
        moved = jnp.concatenate([rolled[: CHUNK - 8], jnp.where(keep, last, after)], axis=0)
        next_ref[k * 8 : k * 8 + 8, :] = jnp.where(keep, 0.0, last)
        grad = grad + taps_ref[k : k + 1, :] * moved
        sum_ref[k : k + 1, :] += jnp.sum(value * moved, axis=0, keepdims=True)
    return grad


def conv_back_edge(halo_ref, taps_ref, next_ref, sum_ref, edge_ref):
    value = halo_ref[...].astype(f32)[8:]
    edge = 0.0
    for k in range(KERNEL - 1):
        after = next_ref[k * 8 : k * 8 + 8, :]
        edge = edge + taps_ref[k : k + 1, :] * after
        sum_ref[k : k + 1, :] += jnp.sum(value * after, axis=0, keepdims=True)
    edge_ref[...] = edge


def carry_back_kernel(
    groups,
    x_ref,
    st_ref,
    stt_ref,
    col_ref,
    row_ref,
    yg_ref,
    dxl_ref,
    dbcl_ref,
    dsl_ref,
    enter_ref,
    lam_ref,
    wide_ref,
    pre_ref,
    value_ref,
    halo_ref,
    taps_ref,
    pre_state_ref,
    value_state_ref,
    halo_state_ref,
    taps_state_ref,
    grad_ref,
    tail_ref,
    edge_ref,
    sum_ref,
    grad_state_ref,
    edge_state_ref,
    sum_state_ref,
    ds_ref,
    adjoint,
    next_ref,
    next_state_ref,
):
    step_index = pl.program_id(0)

    @pl.when(step_index == 0)
    def _():
        adjoint[...] = lam_ref[...]
        next_ref[...] = jnp.zeros_like(next_ref)
        next_state_ref[...] = jnp.zeros_like(next_state_ref)
        sum_ref[...] = jnp.zeros_like(sum_ref)
        sum_state_ref[...] = jnp.zeros_like(sum_state_ref)

    width = x_ref.shape[1]
    mask = head_mask(groups, width)
    cum = col_ref[:, :groups]
    step = col_ref[:, groups : 2 * groups]
    from_start = col_ref[:, 3 * groups + 1 : 3 * groups + 2]
    to_end = col_ref[:, 3 * groups + 2 : 3 * groups + 3]
    inside = col_ref[:, 3 * groups + 3 : 3 * groups + 4]
    match = [col_ref[:, 3 * groups + 4 + k : 3 * groups + 5 + k] for k in range(KERNEL - 1)]
    cum_last = cum[CHUNK - 1 : CHUNK, :]
    entry = jnp.exp(cum) * from_start
    ending = jnp.exp(cum_last - cum) * to_end
    entry_wide = widen(entry, mask)
    ending_wide = widen(ending, mask)
    step_wide = widen(step, mask)
    y_grad = yg_ref[...]
    entered = enter_ref[...]
    held = adjoint[...]
    y_entry = y_grad * entry_wide
    out_grad = dbcl_ref[:, STATE:] + mm_three(y_entry, entered)
    out_carry = fold(y_entry * mm_two(st_ref[:, STATE:], entered), mask)
    x_wide = x_ref[...].astype(f32)
    back = ending_wide * mm_two(st_ref[:, :STATE], held)
    act_grad = step_wide * (dxl_ref[...] + back) + wide_ref[0:1, :] * y_grad
    in_grad = dbcl_ref[:, :STATE] + mm_three(x_wide * ending_wide * step_wide, held)
    size_carry = fold(x_wide * back, mask)
    both = jnp.sum(held * entered, axis=0, keepdims=True)
    crossing = fold(jnp.broadcast_to(both, (8, width)), mask)[0:1, :] * entry[CHUNK - 1 : CHUNK, :]
    doc_col = col_ref[:, 3 * groups : 3 * groups + 1]
    doc_row = row_ref[2 * groups : 2 * groups + 1, :]
    row, col = rows_cols()
    same = doc_col == doc_row
    later = (same & (row <= col)).astype(f32)
    earlier = (same & (row > col)).astype(f32)
    decayed = (
        dsl_ref[:, groups:]
        + jnp.dot(later, out_carry, precision=high, preferred_element_type=f32)
        + jnp.dot(earlier, step * size_carry, precision=high, preferred_element_type=f32)
        + crossing
    )
    ds_ref[:, :groups] = dsl_ref[:, :groups] + size_carry
    ds_ref[:, groups:] = decayed * inside
    adjoint[...] = entry_wide[CHUNK - 1 : CHUNK, :] * held + mm_two(stt_ref[STATE:, :], y_entry)

    grad = conv_back_step(
        act_grad, pre_ref[...], value_ref[...].astype(f32), taps_ref, match, next_ref, sum_ref
    )
    grad_ref[...] = grad.astype(bf16)
    grad_state_ref[...] = conv_back_step(
        jnp.concatenate([in_grad, out_grad], axis=1),
        pre_state_ref[...],
        value_state_ref[...].astype(f32),
        taps_state_ref,
        match,
        next_state_ref,
        sum_state_ref,
    )

    @pl.when(step_index == 0)
    def _():
        tail_ref[...] = grad[CHUNK - 16 :]

    @pl.when(step_index == pl.num_programs(0) - 1)
    def _():
        conv_back_edge(halo_ref, taps_ref, next_ref, sum_ref, edge_ref)
        conv_back_edge(halo_state_ref, taps_state_ref, next_state_ref, sum_state_ref, edge_state_ref)


def norm_kernel(count, cols, planes_each, place_ref, gain_ref, *refs):
    pieces = refs[: PLANE * count]
    out_ref, share_ref = refs[PLANE * count :]
    place = place_ref[0]
    head = place_ref[1]
    share = pieces[0].shape[1]
    for r in range(PLANE):

        @pl.when(pl.program_id(0) == r)
        def _():
            wide = [pieces[r * count + q][...].astype(f32) for q in range(count)]
            total = 0.0
            for q in range(count):
                total = total + jnp.sum(wide[q] * wide[q], axis=1, keepdims=True)
            inverse = lax.rsqrt(total / D + eps)
            for q in range(count):
                lanes = pl.ds(pl.multiple_of((head ^ q) * share, 128), share)
                out_ref[:, lanes] = (wide[q] * inverse * gain_ref[:, lanes]).astype(bf16)
            for t in range(PLANE):

                @pl.when(place == t)
                def _():
                    for z in range(planes_each):
                        share_ref[0, :, z * cols : (z + 1) * cols] = pieces[r * count][
                            :, (z * PLANE + t) * cols : (z * PLANE + t + 1) * cols
                        ]


def project_kernel(
    groups,
    normed_ref,
    halo_ref,
    weight_ref,
    stt_ref,
    col_ref,
    taps_ref,
    value_ref,
    pre_ref,
    x_ref,
    state_ref,
    halo_out_ref,
    last_ref,
):
    @pl.when(pl.program_id(0) == 0)
    def _():
        halo = mm(halo_ref[...], weight_ref[...]).astype(bf16)
        halo_out_ref[...] = halo
        last_ref[...] = halo.astype(f32)[8:]
        state_ref[...] = jnp.zeros_like(state_ref)

    width = x_ref.shape[1]
    rows = x_ref.shape[0]
    value_low = mm(normed_ref[...], weight_ref[...]).astype(bf16)
    value_ref[...] = value_low
    value = value_low.astype(f32)
    row = lax.broadcasted_iota(jnp.int32, (8, width), 0)
    last = last_ref[...]
    pre = taps_ref[4:5, :] + taps_ref[3:4, :] * value
    for k in range(KERNEL - 1):
        reach = KERNEL - 1 - k
        rolled = pltpu.roll(value, reach, 0)
        top = jnp.where(row < reach, pltpu.roll(last, reach, 0), rolled[:8])
        moved = jnp.concatenate([top, rolled[8:]], axis=0)
        pre = pre + taps_ref[k : k + 1, :] * moved * col_ref[:, 3 * groups + 4 + k : 3 * groups + 5 + k]
    last_ref[...] = value[rows - 8 :]
    pre_ref[...] = pre
    x_low = (pre * jax.nn.sigmoid(pre)).astype(bf16)
    x_ref[...] = x_low
    ending = widen(col_ref[:, 3 * groups + 7 : 4 * groups + 7], head_mask(groups, width))
    state_ref[...] += mm_two(stt_ref[:STATE, :], x_low.astype(f32) * ending)


def normed_back_kernel(z_ref, inner_ref, step_ref, state_ref, wg_ref, wi_ref, ws_ref, wt_ref, *out_refs):
    total = (
        mm_t(z_ref[...], wg_ref[...])
        + mm_t(inner_ref[...], wi_ref[...])
        + mm_t(step_ref[...], ws_ref[...])
        + mm_t(state_ref[...], wt_ref[...])
    )
    for r in range(PLANE):

        @pl.when(pl.program_id(0) == r)
        def _():
            out_refs[r][...] = total.astype(out_refs[r].dtype)


def level_of(place, half):
    return jnp.where(place == 0, 3 - half, jnp.where(place == 1, 1, 0))


def split_kernel(count, cols, place_ref, whole_ref, *out_refs):
    place = place_ref[0]
    for r in range(PLANE):
        for t in range(PLANE):

            @pl.when(place == t ^ r)
            def _():
                for z in range(count):
                    out_refs[r][0, :, z * cols : (z + 1) * cols] = whole_ref[
                        0, :, (z * PLANE + t) * cols : (z * PLANE + t + 1) * cols
                    ]


def join_kernel(count, cols, place_ref, *refs):
    place = place_ref[0]
    out_ref = refs[PLANE]
    for r in range(PLANE):
        for t in range(PLANE):

            @pl.when(place == t ^ r)
            def _():
                for z in range(count):
                    out_ref[0, :, (z * PLANE + t) * cols : (z * PLANE + t + 1) * cols] = refs[r][
                        0, :, z * cols : (z + 1) * cols
                    ]


def out_back_kernel(count, place_ref, scale_ref, weight_ref, *refs):
    cot_refs = refs[:count]
    part_refs = refs[count : count + PLANE]
    sum_ref = refs[count + PLANE]
    top_ref = refs[count + PLANE + 1]
    low_ref = refs[count + PLANE + 2]
    place = place_ref[0]

    @pl.when(pl.program_id(0) == 0)
    def _():
        top_ref[...] = jnp.zeros_like(top_ref)

    half = cot_refs[0].shape[3]
    for q in range(count):
        lanes = slice(q * half, (q + 1) * half)
        total = None
        for m in range(4):
            grad = (scale_ref[:, m : m + 1] * cot_refs[q][0, m].astype(f32)).astype(bf16)
            total = grad.astype(f32) if m == 0 else total + grad.astype(f32)
            upper, lower = split_two(total)
            sum_ref[m, :, lanes] = upper
            low_ref[m, :, lanes] = lower
    rows = weight_ref.shape[2] // 2
    for r in range(PLANE):
        owner = place ^ r
        for side in range(2):
            level = level_of(owner, side)
            span = slice(side * rows, (side + 1) * rows)
            weight = weight_ref[owner, :, span]
            part = mm(sum_ref[level], weight)
            out_ref = part_refs[r]

            @pl.when(owner < 2)
            def _():
                out_ref[:, span] = (part + mm(low_ref[level], weight)).astype(out_ref.dtype)

            @pl.when(owner >= 2)
            def _():
                out_ref[:, span] = part.astype(out_ref.dtype)

        if r % 2 == 0 or r == 3:
            bound = jnp.max(jnp.abs(out_ref[...]), axis=0, keepdims=True)
            top_ref[r : r + 1, :] = jnp.maximum(top_ref[r : r + 1, :], bound)


def product_kernel(count, place_ref, weight_ref, *refs):
    u_refs = refs[:PLANE]
    cot_refs = refs[PLANE : PLANE + count]
    dot_ref, own_ref = refs[PLANE + count : PLANE + count + 2]
    send_refs = refs[PLANE + count + 2 : PLANE + 2 * count + 1]
    block_ref = refs[PLANE + 2 * count + 1]
    place = place_ref[0]
    half = cot_refs[0].shape[3]
    rows = weight_ref.shape[1] // 2
    block_ref[...] = jnp.zeros_like(block_ref)
    for r in range(PLANE):
        owner = place ^ r
        for side in range(2):
            span = slice(side * rows, (side + 1) * rows)
            block_ref[level_of(owner, side)] += mm(u_refs[r][:, span], weight_ref[owner, span, :])
    running = None
    ones = jnp.ones((8, half), bf16)
    dot_ref[4:8, :] = jnp.zeros((4, dot_ref.shape[1]), f32)
    for m in (3, 2, 1, 0):
        running = block_ref[m] if running is None else running + block_ref[m]
        dots = 0.0
        for q in range(count):
            part = running[:, q * half : (q + 1) * half]
            dots = dots + cot_refs[q][0, m].astype(f32) * part
            if q == 0:
                own_ref[0, m] = part
            else:
                send_refs[q - 1][0, m] = part.astype(bf16)
        upper, lower = split_two(dots)
        dot_ref[m : m + 1, :] = (mm_t(ones, upper) + mm_t(ones, lower))[0:1, :]


def mix_kernel(count, scale_ref, tok_ref, own_ref, *refs):
    got_refs = refs[: count - 1]
    out_refs = refs[count - 1 :]
    for r in range(PLANE):

        @pl.when(pl.program_id(0) == r)
        def _():
            for m in range(4):
                total = own_ref[0, m]
                for got in got_refs:
                    total = total + got[0, m].astype(f32)
                out_refs[r][m] = (
                    tok_ref[0].astype(f32) + scale_ref[:, m : m + 1] * total
                ).astype(bf16)


def out_weight_kernel(count, planes_each, cols, place_ref, sum_ref, *refs):
    u_refs = refs[:PLANE]
    out_ref = refs[PLANE]
    place = place_ref[0]
    head = place_ref[1]
    rows = u_refs[0].shape[1] // 2
    for r in range(PLANE):

        @pl.when(pl.program_id(0) == r)
        def _():
            owner = place ^ r
            for side in range(2):
                span = slice(side * rows, (side + 1) * rows)
                grad = t_mm(u_refs[r][:, span], sum_ref[level_of(owner, side)])
                for q in range(count):
                    for z in range(planes_each):
                        lanes = slice((q * planes_each + z) * cols, (q * planes_each + z + 1) * cols)
                        out_ref[(head ^ q) * planes_each + z, span, :] = grad[:, lanes].astype(bf16)


def per_chunk(width):
    return pl.BlockSpec((CHUNK, width), lambda c: (c, 0))


def across(height):
    return pl.BlockSpec((height, CHUNK), lambda c: (0, c))


def fixed(*shape):
    return pl.BlockSpec(shape, lambda c: (0,) * len(shape))


def back_chunk(width, steps):
    return pl.BlockSpec((CHUNK, width), lambda c: (steps - 1 - c, 0))


def back_across(height, steps):
    return pl.BlockSpec((height, CHUNK), lambda c: (0, steps - 1 - c))


def shaped(shape, kind=f32):
    return jax.ShapeDtypeStruct(shape, kind)


def contract(left_side, right_side, left_dim, right_dim):
    return lax.dot_general(
        left_side,
        right_side,
        (((left_dim,), (right_dim,)), ((), ())),
        preferred_element_type=f32,
    )


def own_heads(values, heads):
    shape = values.shape[:-1]
    shaped_values = values.reshape(shape + (PLANE, -1, lax.axis_size("h"), heads))
    mine = take(shaped_values, lax.axis_index("i"), len(shape))
    mine = take(mine, lax.axis_index("h"), len(shape) + 1)
    return mine.reshape(shape + (-1,))


def shards(
    tokens,
    cotangent,
    doc_lengths,
    input_gain,
    input_weight,
    step_weight,
    state_weight,
    conv_inner,
    conv_inner_bias,
    conv_state,
    conv_state_bias,
    step_bias,
    decay_log,
    skip_gain,
    gated_gain,
    output_weight,
):
    planes = lax.axis_size("o")
    head_count = lax.axis_size("h")
    plane = lax.axis_index("o")
    inner = lax.axis_index("i")
    head = lax.axis_index("h")
    here = jnp.stack([inner, head]).astype(jnp.int32)
    tok_rows, share = tokens.shape
    span = tok_rows * PLANE
    steps = span // CHUNK
    weight_rows, groups_all = input_weight.shape[:2]
    groups = groups_all // PLANE
    width = groups * P_SIZE
    wide_rows = groups_all * P_SIZE
    cols = output_weight.shape[2]
    own_planes = planes // head_count
    half = own_planes * cols
    pad = KERNEL - 1
    halo = 16
    fence = lax.optimization_barrier

    def token_block(*rest):
        return pl.BlockSpec((tok_rows,) + rest, lambda r, place: (r ^ place[0],) + (0,) * len(rest))

    def part_block(*rest):
        return pl.BlockSpec((1,) + rest, lambda r, place: (r,) + (0,) * len(rest))

    def whole_block(*shape):
        return pl.BlockSpec(shape, lambda r, place: (0,) * len(shape))

    def placed_call(kernel, in_specs, out_specs, out_shape, scratch, name):
        return pl.pallas_call(
            kernel,
            grid_spec=pltpu.PrefetchScalarGridSpec(
                num_scalar_prefetch=1,
                grid=(PLANE,),
                in_specs=in_specs,
                out_specs=out_specs,
                scratch_shapes=scratch,
            ),
            out_shape=out_shape,
            compiler_params=PARAMS,
            name=name,
        )

    def unplaced(kernel):
        return lambda place_ref, *refs: kernel(*refs)

    def chunk_call(kernel, in_specs, out_specs, out_shape, scratch, name):
        return pl.pallas_call(
            kernel,
            grid=(steps,),
            in_specs=in_specs,
            out_specs=out_specs,
            out_shape=out_shape,
            scratch_shapes=scratch,
            compiler_params=PARAMS,
            name=name,
        )

    pieces = input_weight.reshape(weight_rows, PLANE, groups, 2, P_SIZE)

    def head_pieces(side):
        return jnp.transpose(pieces[:, :, :, side, :], (1, 0, 2, 3)).reshape(
            PLANE, weight_rows, width
        )

    inner_pieces = exchange_inner(head_pieces(1))
    weight_inner = lax.all_gather(
        inner_pieces.reshape(PLANE * weight_rows, width), "o", axis=0, tiled=True
    )

    near = [swap(tokens, "h", q) if q else tokens for q in range(head_count)]
    far = swap(tokens, "i", 2)
    far = [swap(far, "h", q) if q else far for q in range(head_count)]
    blocks = [near, [swap(b, "i", 1) for b in near], far, [swap(b, "i", 1) for b in far]]
    normed, tok_share = placed_call(
        partial(norm_kernel, head_count, cols, own_planes),
        [whole_block(1, D)] + [whole_block(tok_rows, share)] * (PLANE * head_count),
        [token_block(D), part_block(tok_rows, half)],
        [shaped((span, D), bf16), shaped((PLANE, tok_rows, half), bf16)],
        [],
        "norm",
    )(here, input_gain[None], *[b for row in blocks for b in row])
    normed_halo = shifted(normed[span - halo :], "o", 1)

    gate_pieces, inner_pieces = fence((head_pieces(0), inner_pieces))
    weight_gate = lax.all_gather(
        exchange_inner(gate_pieces).reshape(PLANE * weight_rows, width), "o", axis=0, tiled=True
    )
    weight_out = lax.all_gather(output_weight.reshape(wide_rows, cols), "o")
    weight_out = jnp.concatenate(
        [
            take(weight_out, (head ^ q) * own_planes + z)
            for q in range(head_count)
            for z in range(own_planes)
        ],
        axis=1,
    ).reshape(PLANE, width, head_count * half)
    weight_out_t = jnp.transpose(weight_out, (0, 2, 1))
    weight_step = stack_all(step_weight.reshape(weight_rows, groups_all), ("o", "i")).reshape(
        D, groups_all
    )
    weight_step = lax.dynamic_slice_in_dim(weight_step, inner * groups, groups, 1)

    cot_parts = pl.pallas_call(
        partial(split_kernel, own_planes, cols),
        grid_spec=pltpu.PrefetchScalarGridSpec(
            num_scalar_prefetch=1,
            grid=(4,),
            in_specs=[pl.BlockSpec((1, tok_rows, share), lambda m, place: (m, 0, 0))],
            out_specs=[pl.BlockSpec((1, tok_rows, half), lambda m, place: (m, 0, 0))] * PLANE,
        ),
        out_shape=[shaped((4, tok_rows, half), bf16)] * PLANE,
        compiler_params=PARAMS,
        name="split",
    )(here, cotangent)
    cot_parts = [cot_parts[0]] + [swap(cot_parts[r], "i", r) for r in range(1, PLANE)]
    normed, normed_halo, cot_parts = fence((normed, normed_halo, cot_parts))
    cots = [
        [swap(part, "h", q) if q else part for part in cot_parts] for q in range(head_count)
    ]

    starts = jnp.cumsum(doc_lengths) - doc_lengths
    positions = plane * span + jnp.arange(-pad, span, dtype=jnp.int32)
    docs_ext = jnp.sum((positions[:, None] >= starts[None, :]).astype(jnp.int32), axis=1)
    docs = docs_ext[pad:]
    matches = [(docs_ext[k : k + span] == docs).astype(f32) for k in range(pad)]

    def taps_of(kernel, bias):
        return jnp.concatenate([kernel, bias[None], jnp.zeros((3, bias.shape[0]), f32)], axis=0)

    taps_inner = taps_of(own_heads(conv_inner, P_SIZE), own_heads(conv_inner_bias, P_SIZE))
    taps_state = taps_of(conv_state, conv_state_bias)
    gain_wide = own_heads(gated_gain, P_SIZE)
    step_shift = own_heads(step_bias, 1)
    rate_log = own_heads(decay_log, 1)
    skip_wide = jnp.repeat(own_heads(skip_gain, 1), P_SIZE)
    wide = jnp.concatenate([skip_wide[None], gain_wide[None], jnp.zeros((6, width), f32)], axis=0)
    group_number = inner * groups + jnp.arange(groups)
    level_limit = jnp.array([groups_all >> m for m in range(4)] + [0] * 4)
    level_mask = jnp.repeat(
        (group_number[None, :] < level_limit[:, None]).astype(bf16), P_SIZE, axis=1
    )

    state_halo, state_value = fence(
        (
            jnp.dot(normed_halo, state_weight, preferred_element_type=f32).astype(bf16),
            jnp.dot(normed, state_weight, preferred_element_type=f32).astype(bf16),
        )
    )
    extended = jnp.concatenate([state_halo[halo - pad :], state_value], axis=0).astype(f32)
    pre_state = conv_state_bias[None, :] + conv_state[pad][None, :] * extended[pad:]
    for k in range(pad):
        pre_state = pre_state + (
            conv_state[k][None, :] * extended[k : k + span] * matches[k][:, None]
        )
    state_act = jax.nn.silu(pre_state).astype(bf16)
    state_act_t = jnp.transpose(state_act)

    step_raw = jnp.dot(normed, weight_step, preferred_element_type=f32)
    step = jax.nn.softplus(step_raw + step_shift[None, :])
    rate = jnp.exp(rate_log)
    decay = -step * rate[None, :]
    lower = jnp.tril(jnp.ones((CHUNK, CHUNK), f32))
    cum = jnp.einsum("ts,csh->cth", lower, decay.reshape(steps, CHUNK, groups), precision=high)
    sums = cum[:, -1]
    before = jnp.cumsum(sums, axis=0) - sums
    cum_whole = (cum + before[:, None, :]).reshape(span, groups)
    cum = cum.reshape(span, groups)
    docs_f = docs.astype(f32)
    prior_doc = docs_ext[pad - 1 : pad - 1 + span]
    by_chunk = docs.reshape(steps, CHUNK)
    prior = prior_doc.reshape(steps, CHUNK)[:, :1]
    from_start = (by_chunk == prior).astype(f32).reshape(span)
    to_end = (by_chunk == by_chunk[:, -1:]).astype(f32).reshape(span)
    inside = (docs == prior_doc).astype(f32)
    whole_start = (docs == docs_ext[pad - 1]).astype(f32)
    whole_end = (docs == docs[-1]).astype(f32)
    entry_whole = jnp.exp(cum_whole) * whole_start[:, None]
    end_whole = jnp.exp(cum_whole[-1:] - cum_whole) * whole_end[:, None] * step
    decay_whole = jnp.repeat(entry_whole[-1:], P_SIZE, axis=1)
    col_pack = jnp.concatenate(
        [
            cum,
            step,
            entry_whole,
            jnp.stack([docs_f, from_start, to_end, inside] + matches, axis=1),
            end_whole,
        ],
        axis=1,
    )
    col_width = col_pack.shape[1]
    row_pack = jnp.concatenate([cum.T, step.T, docs_f[None]], axis=0)
    row_height = row_pack.shape[0]

    wide_out = shaped((span, width))
    value, pre_inner, x, own_state, inner_halo = chunk_call(
        partial(project_kernel, groups),
        [
            per_chunk(D),
            fixed(halo, D),
            fixed(D, width),
            across(2 * STATE),
            per_chunk(col_width),
            fixed(8, width),
        ],
        [per_chunk(width)] * 3 + [fixed(STATE, width), fixed(halo, width)],
        [
            shaped((span, width), bf16),
            wide_out,
            shaped((span, width), bf16),
            shaped((STATE, width)),
            shaped((halo, width), bf16),
        ],
        [pltpu.VMEM((8, width), f32)],
        "project",
    )(normed, normed_halo, weight_inner, state_act_t, col_pack, taps_inner)
    incoming = chain(own_state, decay_whole, 1)
    y_local = chunk_call(
        partial(within_kernel, groups),
        [per_chunk(width), per_chunk(2 * STATE), per_chunk(col_width), across(row_height)],
        per_chunk(width),
        wide_out,
        [],
        "within",
    )(x, state_act, col_pack, row_pack)
    y_local, cots = fence((y_local, cots))
    cots = [jnp.stack(parts) for parts in cots]
    gate_z = jnp.dot(normed, weight_gate, preferred_element_type=f32).astype(bf16)
    v, scaled_u, squares, entering = chunk_call(
        partial(carry_kernel, groups),
        [
            per_chunk(width),
            per_chunk(2 * STATE),
            across(2 * STATE),
            per_chunk(col_width),
            per_chunk(width),
            per_chunk(width),
            fixed(STATE, width),
            fixed(8, width),
            fixed(8, width),
        ],
        [per_chunk(width), per_chunk(width), across(8), per_chunk(width)],
        [
            wide_out,
            shaped((span, width), bf16),
            shaped((8, span)),
            shaped((steps * STATE, width)),
        ],
        [pltpu.VMEM((STATE, width), f32)],
        "carry",
    )(x, state_act, state_act_t, col_pack, y_local, gate_z, incoming, wide, level_mask)

    u_far = swap(scaled_u, "i", 2)
    u_parts = [scaled_u, swap(scaled_u, "i", 1), u_far, swap(u_far, "i", 1)]
    squares = add_all(squares[:4], ("i", "h"))
    widths = jnp.array([INNER >> m for m in range(4)], f32)
    scales_row = lax.rsqrt(squares / widths[:, None] + eps)
    scales = jnp.transpose(jnp.concatenate([scales_row, jnp.zeros_like(scales_row)], axis=0))
    cot_block = part_block(4, tok_rows, half)
    cot_shape = shaped((PLANE, 4, tok_rows, half), bf16)
    *parts, sums, tops = placed_call(
        partial(out_back_kernel, head_count),
        [token_block(8), whole_block(PLANE, head_count * half, width)] + [cot_block] * head_count,
        [token_block(width)] * PLANE
        + [
            pl.BlockSpec((4, tok_rows, head_count * half), lambda r, place: (0, r ^ place[0], 0)),
            whole_block(8, width),
        ],
        [wide_out] * PLANE + [shaped((4, span, head_count * half), bf16), shaped((8, width))],
        [pltpu.VMEM((4, tok_rows, head_count * half), bf16)],
        "out_back",
    )(here, scales, weight_out_t, *cots)
    top = tops[2:3] + swap(tops, "i", 1)[3:4]
    top_across = swap(jnp.broadcast_to(top, tops.shape), "i", 2)[:1]
    got_across = swap(to_half(parts[2] + swap(parts[3], "i", 1), top), "i", 2)
    got_near = swap(parts[1], "i", 1)
    u_grad = parts[0] + got_near + from_half(got_across, top_across)
    dots, own_product, *sent_products = placed_call(
        partial(product_kernel, head_count),
        [whole_block(PLANE, width, head_count * half)]
        + [token_block(width)] * PLANE
        + [cot_block] * head_count,
        [pl.BlockSpec((8, tok_rows), lambda r, place: (0, r ^ place[0]))]
        + [cot_block] * head_count,
        [shaped((8, span)), shaped(cot_shape.shape)] + [cot_shape] * (head_count - 1),
        [pltpu.VMEM((4, tok_rows, head_count * half), f32)],
        "products",
    )(here, weight_out, *u_parts, *cots)
    dots = add_all(dots[:4], ("i", "h"))
    out_grad = placed_call(
        partial(out_weight_kernel, head_count, own_planes, cols),
        [whole_block(4, span, head_count * half)] + [whole_block(span, width)] * PLANE,
        pl.BlockSpec((planes, width, cols), lambda r, place: (0, r ^ place[0], 0)),
        shaped((planes, wide_rows, cols), bf16),
        [],
        "out_weight_back",
    )(here, sums, *u_parts)
    out_grad = lax.psum_scatter(out_grad, "o", scatter_dimension=0, tiled=False)
    output_weight_grad = out_grad.astype(f32).reshape(groups_all, P_SIZE, cols)

    stat = dots * -0.5 * scales_row * scales_row * scales_row / widths[:, None]
    stat = jnp.concatenate([stat, jnp.zeros_like(stat)], axis=0)
    y_grad, z_grad, wide_sums, leaving = chunk_call(
        partial(gate_back_kernel, groups),
        [
            per_chunk(width),
            per_chunk(width),
            per_chunk(width),
            per_chunk(width),
            across(2 * STATE),
            per_chunk(col_width),
            across(8),
            fixed(8, width),
            fixed(8, width),
        ],
        [per_chunk(width), per_chunk(width), fixed(8, width), fixed(STATE, width)],
        [wide_out, shaped((span, width), bf16), shaped((8, width)), shaped((STATE, width))],
        [],
        "gate_back",
    )(u_grad, v, gate_z, x, state_act_t, col_pack, stat, wide, level_mask)
    lam = chain(leaving, decay_whole, -1)
    gate_grad = contract(normed, z_grad, 0, 0).astype(bf16)
    gate_grad, y_grad = fence((gate_grad, y_grad))
    gate_grad = lax.psum_scatter(gate_grad, "o", scatter_dimension=0, tiled=True)

    dx_local, dbc_local, ds_local = chunk_call(
        partial(within_back_kernel, groups),
        [
            per_chunk(width),
            per_chunk(2 * STATE),
            per_chunk(col_width),
            across(row_height),
            per_chunk(width),
        ],
        [per_chunk(width), per_chunk(2 * STATE), per_chunk(2 * groups)],
        [wide_out, shaped((span, 2 * STATE)), shaped((span, 2 * groups))],
        [],
        "within_back",
    )(x, state_act, col_pack, row_pack, y_grad)
    back_wide = back_chunk(width, steps)
    back_state = back_chunk(2 * STATE, steps)
    back_step = back_chunk(2 * groups, steps)
    (
        inner_grad,
        inner_tail,
        inner_edge,
        inner_sums,
        state_grad,
        state_edge,
        state_sums,
        step_pair,
    ) = chunk_call(
        partial(carry_back_kernel, groups),
        [
            back_wide,
            back_state,
            back_across(2 * STATE, steps),
            back_chunk(col_width, steps),
            back_across(row_height, steps),
            back_wide,
            back_wide,
            back_state,
            back_step,
            back_wide,
            fixed(STATE, width),
            fixed(8, width),
            back_wide,
            back_wide,
            fixed(halo, width),
            fixed(8, width),
            back_state,
            back_state,
            fixed(halo, 2 * STATE),
            fixed(8, 2 * STATE),
        ],
        [
            back_wide,
            fixed(16, width),
            fixed(8, width),
            fixed(8, width),
            back_state,
            fixed(8, 2 * STATE),
            fixed(8, 2 * STATE),
            back_step,
        ],
        [
            shaped((span, width), bf16),
            shaped((16, width)),
            shaped((8, width)),
            shaped((8, width)),
            shaped((span, 2 * STATE)),
            shaped((8, 2 * STATE)),
            shaped((8, 2 * STATE)),
            shaped((span, 2 * groups)),
        ],
        [
            pltpu.VMEM((STATE, width), f32),
            pltpu.VMEM((24, width), f32),
            pltpu.VMEM((24, 2 * STATE), f32),
        ],
        "carry_back",
    )(
        x,
        state_act,
        state_act_t,
        col_pack,
        row_pack,
        y_grad,
        dx_local,
        dbc_local,
        ds_local,
        entering,
        lam,
        wide,
        pre_inner,
        value,
        inner_halo,
        taps_inner,
        pre_state,
        state_value,
        state_halo,
        taps_state,
    )
    size_grad = step_pair[:, :groups]
    decay_grad = step_pair[:, groups:]
    step_raw_grad = (size_grad - rate[None, :] * decay_grad) * jax.nn.sigmoid(
        step_raw + step_shift[None, :]
    )
    edges = shifted(jnp.concatenate([inner_edge, state_edge], axis=1), "o", -1)
    tail = inner_tail + jnp.pad(edges[:, :width], ((8, 0), (0, 0)))
    inner_grad = lax.dynamic_update_slice_in_dim(inner_grad, tail.astype(bf16), span - 16, 0)
    state_grad = state_grad + jnp.pad(edges[:, width:], ((span - 8, 0), (0, 0)))

    inner_part = contract(normed, inner_grad, 0, 0).astype(bf16)
    inner_part, inner_grad = fence((inner_part, inner_grad))
    inner_part = lax.psum_scatter(inner_part, "o", scatter_dimension=0, tiled=True)
    step_grad_low = step_raw_grad.astype(bf16)
    state_grad_low = state_grad.astype(bf16)
    normed_parts = placed_call(
        unplaced(normed_back_kernel),
        [
            token_block(width),
            token_block(width),
            token_block(groups),
            token_block(2 * STATE),
            whole_block(D, width),
            whole_block(D, width),
            whole_block(D, groups),
            whole_block(D, 2 * STATE),
        ],
        [whole_block(tok_rows, D)] * PLANE,
        [shaped((tok_rows, D), f32 if r % 2 == 0 else bf16) for r in range(PLANE)],
        [],
        "normed_back",
    )(
        here,
        z_grad,
        inner_grad,
        step_grad_low,
        state_grad_low,
        weight_gate,
        weight_inner,
        weight_step,
        state_weight,
    )
    got_across = swap(
        (normed_parts[2] + swap(normed_parts[3], "i", 1).astype(f32)).astype(bf16), "i", 2
    )
    full_grad = scatter_heads(
        normed_parts[0] + swap(normed_parts[1], "i", 1).astype(f32) + got_across.astype(f32), 1
    )

    got_products = [swap(sent_products[q - 1], "h", q) for q in range(1, head_count)]
    mixed_parts = placed_call(
        unplaced(partial(mix_kernel, head_count)),
        [token_block(8), part_block(tok_rows, half)] + [cot_block] * head_count,
        [whole_block(4, tok_rows, half)] * PLANE,
        [shaped((4, tok_rows, half), bf16)] * PLANE,
        [],
        "mix",
    )(here, scales, tok_share, own_product, *got_products)
    mixed_parts = [mixed_parts[0]] + [swap(mixed_parts[r], "i", r) for r in range(1, PLANE)]
    mixed = placed_call(
        partial(join_kernel, own_planes, cols),
        [part_block(tok_rows, half)] * PLANE,
        part_block(tok_rows, share),
        shaped((4, tok_rows, share), bf16),
        [],
        "join",
    )(here, *mixed_parts)

    gate_back = exchange_inner(gate_grad.reshape(PLANE, weight_rows, width))
    inner_back = exchange_inner(inner_part.reshape(PLANE, weight_rows, width))

    def by_group(values):
        return jnp.transpose(
            values.reshape(PLANE, weight_rows, groups, P_SIZE), (1, 0, 2, 3)
        ).reshape(weight_rows, groups_all, P_SIZE)

    input_weight_grad = jnp.concatenate(
        [by_group(gate_back), by_group(inner_back)], axis=2
    ).astype(f32)
    step_part = add_all(contract(step_grad_low, normed, 0, 0), ("o",))
    step_part = lax.dynamic_slice_in_dim(
        stack_all(step_part, ("i",)).reshape(groups_all, planes * PLANE, weight_rows),
        plane * PLANE + inner,
        1,
        1,
    )
    step_weight_grad = jnp.transpose(step_part, (2, 1, 0))

    state_sum = state_grad
    for axis in ("i", "h"):
        for bit in bits_of(axis):
            kind = f32 if axis == "i" and bit == 1 else bf16
            state_sum = state_sum + swap(state_sum.astype(kind), axis, bit).astype(f32)
    part_rows = D // (PLANE * head_count)
    normed_part = lax.dynamic_slice_in_dim(
        normed, (inner * head_count + head) * part_rows, part_rows, 1
    )
    state_part = contract(normed_part, state_sum.astype(bf16), 0, 0)
    state_part = add_all(state_part, ("o",)).astype(bf16)
    state_weight_grad = stack_all(state_part, ("i", "h")).reshape(D, 2 * STATE).astype(f32)

    own_wide = [near[q].astype(f32) for q in range(head_count)]
    square = sum(jnp.sum(a * a, axis=1, keepdims=True) for a in own_wide)
    inverse = lax.rsqrt(square / D + eps)
    gain_share = lax.dynamic_slice_in_dim(input_gain, head * share, share, 0)
    unit = own_wide[0] * inverse
    weighted = full_grad * gain_share[None, :]
    row_sum = add_all(jnp.sum(weighted * unit, axis=1).reshape(-1, CHUNK), ("h",)).reshape(-1, 1)
    resid = jnp.sum(cotangent.astype(f32), axis=0)
    tokens_grad = resid + inverse * (weighted - unit * (row_sum / D))
    gain_part = add_all(jnp.sum(full_grad * unit, axis=0).reshape(-1, CHUNK), ("o", "i"))
    input_gain_grad = stack_all(gain_part, ("h",)).reshape(D)

    per_head = jnp.stack(
        [
            jnp.sum(step_raw_grad, axis=0),
            jnp.sum(decay_grad * decay, axis=0),
            jnp.sum(wide_sums[1].reshape(groups, P_SIZE), axis=1),
        ]
    )
    per_head = jnp.pad(per_head, ((0, 0), (0, width - groups)))
    flat = state_sums[: KERNEL + 1].reshape(-1)
    flat = jnp.pad(flat, (0, -flat.shape[0] % width)).reshape(-1, width)
    small = jnp.concatenate([inner_sums[: KERNEL + 1], wide_sums[:1], per_head, flat], axis=0)
    small = stack_all(add_all(small, ("o",)), ("i", "h"))
    small = small.reshape(PLANE, head_count, -1, width)
    shared = jnp.sum(small[:, :, 9:], axis=(0, 1)).reshape(-1)[: (KERNEL + 1) * 2 * STATE]
    shared = shared.reshape(KERNEL + 1, 2 * STATE)

    def all_heads(values, size):
        values = values.reshape(PLANE, head_count, -1, groups, size)
        return jnp.transpose(values, (2, 0, 3, 1, 4)).reshape(values.shape[2], -1)

    wide_total = all_heads(small[:, :, :6], P_SIZE)
    head_total = all_heads(small[:, :, 6:9, :groups], 1)
    return (
        mixed,
        tokens_grad,
        input_gain_grad,
        input_weight_grad,
        step_weight_grad,
        state_weight_grad,
        wide_total[:4],
        wide_total[4],
        shared[:4],
        shared[4],
        head_total[0],
        head_total[1],
        head_total[2],
        wide_total[5],
        output_weight_grad,
    )


def solution(mesh):
    rows, heads = mesh.devices.shape
    cut = Mesh(mesh.devices.reshape(rows // PLANE, PLANE, heads), ("o", "i", "h"))
    both = ("o", "i")
    placed = (
        P(both, "h"),
        P(None, both, "h"),
        P(),
        P(),
        P(both, None, "h"),
        P(both, "h", None),
        P(),
        P(),
        P(),
        P(),
        P(),
        P(),
        P(),
        P(),
        P(),
        P(None, "h", both),
    )
    return jax.shard_map(
        shards,
        mesh=cut,
        in_specs=placed,
        out_specs=(
            P(None, both, "h"),
            P(both, "h"),
            P(),
            P(both, None, "h"),
            P(both, "h", None),
            P(),
            P(),
            P(),
            P(),
            P(),
            P(),
            P(),
            P(),
            P(),
            P(None, "h", both),
        ),
        check_vma=False,
    )
```

```python
from functools import partial

import jax
import jax.numpy as jnp
from jax import lax
from jax.experimental import pallas as pl
from jax.experimental.pallas import tpu as pltpu
from jax.sharding import Mesh
from jax.sharding import PartitionSpec as P

D = 2048
P_SIZE = 64
STATE = 128
KERNEL = 4
INNER = 4096
CHUNK = 128
SUB = 2
PLANE = 4

HALF_TOP = 16384.0

eps = 1e-05
bf16 = jnp.bfloat16
f32 = jnp.float32
high = lax.Precision.HIGHEST
PARAMS = pltpu.CompilerParams(
    vmem_limit_bytes=58 * 1024 * 1024, dimension_semantics=("arbitrary",)
)


def swap(block, axis, bit):
    return lax.ppermute(block, axis, [(a, a ^ bit) for a in range(lax.axis_size(axis))])


def shifted(block, axis, distance):
    devices = range(lax.axis_size(axis))
    route = [(a - distance, a) for a in devices if a - distance in devices]
    return lax.ppermute(block, axis, route)


def scattered_inner(blocks):
    place = lax.axis_index("i")
    got = {0: take(blocks, place)}
    for bit in (2, 3, 1):
        got[bit] = swap(take(blocks, place ^ bit), "i", bit)
    return [got[r] for r in range(PLANE)]


def bits_of(axis):
    count = lax.axis_size(axis)
    return [1 << b for b in range(count.bit_length() - 1)]


def take(values, index, axis=0):
    return lax.dynamic_index_in_dim(values, index, axis, keepdims=False)


def put(buffer, piece, index):
    return lax.dynamic_update_index_in_dim(buffer, piece, index, 0)


def add_all(value, axes):
    for axis in axes:
        for bit in bits_of(axis):
            value = value + swap(value, axis, bit)
    return value


def add_inner(value, bit):
    return value + swap(value, "i", bit)


def stack_over(value, axis, bit, at):
    other = swap(value, axis, bit)
    upper = (lax.axis_index(axis) & bit) != 0
    return jnp.where(
        upper, jnp.stack([other, value], axis=at), jnp.stack([value, other], axis=at)
    )


def stack_plane(value):
    shape = value.shape
    count = lax.axis_size("h")
    for bit in bits_of("h"):
        value = stack_over(value, "h", bit, 0)
        value = value.reshape((-1,) + shape) if bit > 1 else value
    value = value.reshape((count,) + shape)
    value = stack_over(value, "i", 2, 0)
    value = stack_over(value, "i", 1, 1)
    return value.reshape((PLANE, count) + shape)


def stack_planes(value):
    shape = value.shape
    for bit in bits_of("o"):
        value = stack_over(value, "o", bit, 0)
        value = value.reshape((-1,) + shape)
    return value


def stack_inner(value):
    shape = value.shape
    value = stack_over(value, "i", 2, 0)
    return stack_over(value, "i", 1, 1).reshape((PLANE,) + shape)


def exchange_inner(blocks):
    place = lax.axis_index("i")
    out = blocks
    for bit in (2, 3, 1):
        out = put(out, swap(take(blocks, place ^ bit), "i", bit), place ^ bit)
    return out


def scatter_heads(values, axis):
    count = lax.axis_size("h")
    if count != 2:
        return lax.psum_scatter(values, "h", scatter_dimension=axis, tiled=True)
    place = lax.axis_index("h")
    width = values.shape[axis] // 2
    sent = lax.dynamic_slice_in_dim(values, (1 - place) * width, width, axis)
    kept = lax.dynamic_slice_in_dim(values, place * width, width, axis)
    return kept + swap(sent.astype(bf16), "h", 1).astype(f32)


def column_power(values):
    largest = jnp.max(jnp.abs(values), axis=0, keepdims=True)
    exponent = jnp.ceil(jnp.log2(jnp.clip(largest, 1e-30, 1e30)))
    return jnp.exp2(exponent), exponent


def split_rows(values):
    upper = lax.reduce_precision(values, 8, 7)
    return upper.astype(bf16), (values - upper).astype(bf16)


def pack_half(values, extra=()):
    power, exponent = column_power(values)
    rows = [exponent]
    for row in extra:
        first = lax.reduce_precision(row, 5, 10)
        rows += [first, (row - first) * 2048.0]
    rows.append(jnp.zeros((16 - len(rows), values.shape[1]), f32))
    return jnp.concatenate([values * (HALF_TOP / power)] + rows, axis=0).astype(jnp.float16)


def unpack_half(packed):
    rows = packed.shape[0] - 16
    tail = packed[rows:].astype(f32)
    values = packed[:rows].astype(f32) * (jnp.exp2(tail[0:1]) / HALF_TOP)
    return values, tail[1:2] + tail[2:3] / 2048.0


def chain(state, decay_wide, direction):
    packed = pack_half(state, (decay_wide,))
    total = None
    for distance in range(lax.axis_size("o") - 1, 0, -1):
        own, decay = unpack_half(shifted(packed, "o", direction * distance))
        total = own if total is None else own + decay * total
    return total


def mm(a, b):
    return jnp.dot(a, b, preferred_element_type=f32)


def mm_two(a, b):
    upper, lower = split_two(b)
    return mm(a, upper) + mm(a, lower)


def mm_three(a, b):
    a_up, a_low = split_two(a)
    b_up, b_low = split_two(b)
    return mm_t(a_up, b_up) + mm_t(a_up, b_low) + mm_t(a_low, b_up)


def mm_t(a, b):
    return lax.dot_general(a, b, (((1,), (1,)), ((), ())), preferred_element_type=f32)


def t_mm(a, b):
    return lax.dot_general(a, b, (((0,), (0,)), ((), ())), preferred_element_type=f32)


def head_mask(groups, width):
    head = lax.broadcasted_iota(jnp.int32, (groups, width), 0)
    lane = lax.broadcasted_iota(jnp.int32, (groups, width), 1)
    return (lane // P_SIZE == head).astype(f32).astype(bf16)


def split_two(values):
    upper = values.astype(bf16)
    return upper, (values - upper.astype(f32)).astype(bf16)


def widen(values, mask):
    upper, lower = split_two(values)
    return mm(upper, mask) + mm(lower, mask)


def fold(values, mask):
    upper, lower = split_two(values)
    return mm_t(upper, mask) + mm_t(lower, mask)


def pair_masks():
    lane = lax.broadcasted_iota(jnp.int32, (1, 2 * P_SIZE), 1)
    lower = (lane < P_SIZE).astype(f32)
    return lower.astype(bf16), (1.0 - lower).astype(bf16)


def rows_cols():
    row = lax.broadcasted_iota(jnp.int32, (CHUNK, CHUNK), 0)
    col = lax.broadcasted_iota(jnp.int32, (CHUNK, CHUNK), 1)
    return row, col


def within_kernel(groups, turn, x_ref, st_ref, col_ref, row_ref, y_ref):
    b_in = st_ref[:, :STATE]
    c_out = st_ref[:, STATE:]
    scores = mm_t(c_out, b_in)
    doc_col = col_ref[:, 3 * groups : 3 * groups + 1]
    doc_row = row_ref[2 * groups : 2 * groups + 1, :]
    row, col = rows_cols()
    bias = jnp.where((doc_col == doc_row) & (row >= col), 0.0, -1e30)
    masks = pair_masks()
    for pair in range(groups // 2):
        lanes = slice(pair * 2 * P_SIZE, (pair + 1) * 2 * P_SIZE)
        x_pair = x_ref[:, lanes]
        weights, values = [], []
        for side in range(2):
            h = 2 * pair + side
            spread = jnp.exp(col_ref[:, h : h + 1] - row_ref[h : h + 1, :] + bias)
            weights.append(split_two(scores * spread * row_ref[groups + h : groups + h + 1, :]))
            values.append(x_pair * masks[side])
        value = jnp.concatenate(values, axis=0)
        y_ref[:, lanes] = mm(
            jnp.concatenate([weights[0][0], weights[1][0]], axis=1), value
        ) + mm(jnp.concatenate([weights[0][1], weights[1][1]], axis=1), value)


def carry_kernel(
    groups, turn,
    x_ref,
    st_ref,
    stt_ref,
    col_ref,
    yl_ref,
    gz_ref,
    inc_ref,
    wide_ref,
    level_ref,
    v_ref,
    u_ref,
    sq_ref,
    enter_ref,
    state,
):
    @pl.when(turn == 0)
    def _():
        state[...] = inc_ref[...]

    width = x_ref.shape[1]
    mask = head_mask(groups, width)
    cum = col_ref[:, :groups]
    step = col_ref[:, groups : 2 * groups]
    from_start = col_ref[:, 3 * groups + 1 : 3 * groups + 2]
    to_end = col_ref[:, 3 * groups + 2 : 3 * groups + 3]
    cum_last = cum[CHUNK - 1 : CHUNK, :]
    entry = jnp.exp(cum) * from_start
    ending = jnp.exp(cum_last - cum) * to_end * step
    entry_wide = widen(entry, mask)
    ending_wide = widen(ending, mask)
    held = state[...]
    enter_ref[...] = held
    carried = mm_two(st_ref[:, STATE:], held)
    x_wide = x_ref[...].astype(f32)
    v = yl_ref[...] + entry_wide * carried + wide_ref[0:1, :] * x_wide
    v_ref[...] = v
    z = gz_ref[...].astype(f32)
    gated = v * (z * jax.nn.sigmoid(z))
    u_ref[...] = (gated * wide_ref[1:2, :]).astype(bf16)
    upper, lower = split_two(gated * gated)
    sq_ref[...] = mm_t(level_ref[...], upper) + mm_t(level_ref[...], lower)
    added = mm_two(stt_ref[:STATE, :], x_wide * ending_wide)
    state[...] = entry_wide[CHUNK - 1 : CHUNK, :] * held + added


def gate_back_kernel(
    groups, turn,
    ug_ref,
    v_ref,
    gz_ref,
    x_ref,
    stt_ref,
    col_ref,
    dot_ref,
    scale_ref,
    wide_ref,
    level_ref,
    yg_ref,
    zg_ref,
    acc_ref,
    lam_ref,
):
    @pl.when(turn == 0)
    def _():
        acc_ref[...] = jnp.zeros_like(acc_ref)
        lam_ref[...] = jnp.zeros_like(lam_ref)

    mask = head_mask(groups, x_ref.shape[1])
    v = v_ref[...]
    z = gz_ref[...].astype(f32)
    sig = jax.nn.sigmoid(z)
    silu = z * sig
    gated = v * silu
    ug = ug_ref[...]
    level = lax.broadcasted_iota(jnp.int32, dot_ref.shape, 0)
    factor = jnp.zeros(dot_ref.shape, f32)
    for m in range(4):
        factor = jnp.where(level == m, -0.5 / (INNER >> m), factor)
    scale = scale_ref[...]
    upper, lower = split_two(dot_ref[...] * scale * scale * scale * factor)
    stat = t_mm(upper, level_ref[...]) + t_mm(lower, level_ref[...])
    gated_grad = ug * wide_ref[1:2, :] + 2.0 * gated * stat
    y_grad = gated_grad * silu
    yg_ref[...] = y_grad
    zg_ref[...] = (gated_grad * v * (sig * (1.0 + z * (1.0 - sig)))).astype(bf16)
    acc_ref[0:1, :] += jnp.sum(ug * gated, axis=0, keepdims=True)
    acc_ref[1:2, :] += jnp.sum(y_grad * x_ref[...].astype(f32), axis=0, keepdims=True)
    whole_entry = widen(col_ref[:, 2 * groups : 3 * groups], mask)
    lam_ref[...] += mm_two(stt_ref[STATE:, :], y_grad * whole_entry)


def within_back_kernel(groups, turn, x_ref, st_ref, col_ref, row_ref, yg_ref, dx_ref, dbc_ref, ds_ref):
    b_in = st_ref[:, :STATE]
    c_out = st_ref[:, STATE:]
    scores = mm_t(b_in, c_out)
    doc_col = col_ref[:, 3 * groups : 3 * groups + 1]
    doc_row = row_ref[2 * groups : 2 * groups + 1, :]
    row, col = rows_cols()
    same = doc_col == doc_row
    bias = jnp.where(same & (row <= col), 0.0, -1e30)
    masks = pair_masks()
    total = jnp.zeros((CHUNK, CHUNK), f32)
    head_lane = lax.broadcasted_iota(jnp.int32, (CHUNK, groups), 1)
    head_row = lax.broadcasted_iota(jnp.int32, (groups, CHUNK), 0)
    size_part = jnp.zeros((CHUNK, groups), f32)
    out_part = jnp.zeros((groups, CHUNK), f32)
    for pair in range(groups // 2):
        lanes = slice(pair * 2 * P_SIZE, (pair + 1) * 2 * P_SIZE)
        x_pair = x_ref[:, lanes]
        y_pair, y_rest = split_two(yg_ref[:, lanes])
        weights, values = [], []
        for side in range(2):
            h = 2 * pair + side
            step = col_ref[:, groups + h : groups + h + 1]
            spread = jnp.exp(row_ref[h : h + 1, :] - col_ref[:, h : h + 1] + bias)
            y_side = y_pair * masks[side]
            paired = spread * (mm_t(x_pair, y_side) + mm_t(x_pair, y_rest * masks[side]))
            total = total + step * paired
            product = scores * paired
            size_part = jnp.where(
                head_lane == h, jnp.sum(product, axis=1, keepdims=True), size_part
            )
            out_part = jnp.where(
                head_row == h, jnp.sum(step * product, axis=0, keepdims=True), out_part
            )
            weights.append((scores * spread).astype(bf16))
            values.append(y_side)
        dx_ref[:, lanes] = mm(jnp.concatenate(weights, axis=1), jnp.concatenate(values, axis=0))
    upper, lower = split_two(total)
    dbc_ref[:, :STATE] = mm(upper, c_out) + mm(lower, c_out)
    dbc_ref[:, STATE:] = t_mm(upper, b_in) + t_mm(lower, b_in)
    later = (same & (row <= col)).astype(f32)
    step_all = col_ref[:, groups : 2 * groups]
    ds_ref[:, :groups] = size_part
    ds_ref[:, groups:] = lax.dot_general(
        later, out_part, (((1,), (1,)), ((), ())), precision=high, preferred_element_type=f32
    ) - jnp.dot(later, step_all * size_part, precision=high, preferred_element_type=f32)


def conv_back_step(act_grad, pre, value, taps_ref, match, next_ref, sum_ref):
    sig = jax.nn.sigmoid(pre)
    slope = act_grad * (sig * (1.0 + pre * (1.0 - sig)))
    sum_ref[4:5, :] += jnp.sum(slope, axis=0, keepdims=True)
    sum_ref[3:4, :] += jnp.sum(slope * value, axis=0, keepdims=True)
    grad = taps_ref[3:4, :] * slope
    row = lax.broadcasted_iota(jnp.int32, (8, pre.shape[1]), 0)
    for k in range(KERNEL - 1):
        reach = KERNEL - 1 - k
        rolled = pltpu.roll(slope * match[k], CHUNK - reach, 0)
        last = rolled[CHUNK - 8 :]
        keep = row < 8 - reach
        after = next_ref[k * 8 : k * 8 + 8, :]
        moved = jnp.concatenate([rolled[: CHUNK - 8], jnp.where(keep, last, after)], axis=0)
        next_ref[k * 8 : k * 8 + 8, :] = jnp.where(keep, 0.0, last)
        grad = grad + taps_ref[k : k + 1, :] * moved
        sum_ref[k : k + 1, :] += jnp.sum(value * moved, axis=0, keepdims=True)
    return grad


def conv_back_edge(halo_ref, taps_ref, next_ref, sum_ref, edge_ref):
    value = halo_ref[...].astype(f32)[8:]
    edge = 0.0
    for k in range(KERNEL - 1):
        after = next_ref[k * 8 : k * 8 + 8, :]
        edge = edge + taps_ref[k : k + 1, :] * after
        sum_ref[k : k + 1, :] += jnp.sum(value * after, axis=0, keepdims=True)
    edge_ref[...] = edge


def carry_back_kernel(
    groups,
    turns,
    step_index,
    x_ref,
    st_ref,
    stt_ref,
    col_ref,
    row_ref,
    yg_ref,
    dxl_ref,
    dbcl_ref,
    dsl_ref,
    enter_ref,
    lam_ref,
    wide_ref,
    pre_ref,
    value_ref,
    halo_ref,
    taps_ref,
    pre_state_ref,
    value_state_ref,
    halo_state_ref,
    taps_state_ref,
    rate_ref,
    wide_sum_ref,
    grad_ref,
    tail_ref,
    edge_ref,
    sum_ref,
    grad_state_ref,
    grad_state_t_ref,
    step_grad_ref,
    adjoint,
    next_ref,
    next_state_ref,
):
    width = x_ref.shape[1]
    state_at = 2 * width
    step_at = state_at + 2 * STATE
    sum_inner_ref = sum_ref.at[:, :width]
    sum_state_ref = sum_ref.at[:, state_at:step_at]

    @pl.when(step_index == turns)
    def _():
        sum_ref[:, width:state_at] = wide_sum_ref[...]
        conv_back_edge(halo_ref, taps_ref, next_ref, sum_inner_ref, edge_ref.at[:, :width])
        edge_state_ref = edge_ref.at[:, width:]
        conv_back_edge(halo_state_ref, taps_state_ref, next_state_ref, sum_state_ref, edge_state_ref)
        edge = edge_state_ref[...]
        edge = jnp.concatenate([edge, jnp.zeros((CHUNK - 8, edge.shape[1]), f32)], axis=0)
        grad_state_t_ref[...] = jnp.transpose(edge)

    @pl.when(step_index == 0)
    def _():
        adjoint[...] = lam_ref[...]
        next_ref[...] = jnp.zeros_like(next_ref)
        next_state_ref[...] = jnp.zeros_like(next_state_ref)
        sum_ref[...] = jnp.zeros_like(sum_ref)

    @pl.when(step_index < turns)
    def _():
        mask = head_mask(groups, width)
        cum = col_ref[:, :groups]
        step = col_ref[:, groups : 2 * groups]
        from_start = col_ref[:, 3 * groups + 1 : 3 * groups + 2]
        to_end = col_ref[:, 3 * groups + 2 : 3 * groups + 3]
        inside = col_ref[:, 3 * groups + 3 : 3 * groups + 4]
        match = [col_ref[:, 3 * groups + 4 + k : 3 * groups + 5 + k] for k in range(KERNEL - 1)]
        cum_last = cum[CHUNK - 1 : CHUNK, :]
        entry = jnp.exp(cum) * from_start
        ending = jnp.exp(cum_last - cum) * to_end
        entry_wide = widen(entry, mask)
        ending_wide = widen(ending, mask)
        step_wide = widen(step, mask)
        y_grad = yg_ref[...]
        entered = enter_ref[...]
        held = adjoint[...]
        y_entry = y_grad * entry_wide
        out_grad = dbcl_ref[:, STATE:] + mm_three(y_entry, entered)
        out_carry = fold(y_entry * mm_two(st_ref[:, STATE:], entered), mask)
        x_wide = x_ref[...].astype(f32)
        back = ending_wide * mm_two(st_ref[:, :STATE], held)
        act_grad = step_wide * (dxl_ref[...] + back) + wide_ref[0:1, :] * y_grad
        in_grad = dbcl_ref[:, :STATE] + mm_three(x_wide * ending_wide * step_wide, held)
        size_carry = fold(x_wide * back, mask)
        both = jnp.sum(held * entered, axis=0, keepdims=True)
        crossing = fold(jnp.broadcast_to(both, (8, width)), mask)[0:1, :] * entry[CHUNK - 1 : CHUNK, :]
        doc_col = col_ref[:, 3 * groups : 3 * groups + 1]
        doc_row = row_ref[2 * groups : 2 * groups + 1, :]
        row, col = rows_cols()
        same = doc_col == doc_row
        later = (same & (row <= col)).astype(f32)
        earlier = (same & (row > col)).astype(f32)
        decayed = (
            dsl_ref[:, groups:]
            + jnp.dot(later, out_carry, precision=high, preferred_element_type=f32)
            + jnp.dot(earlier, step * size_carry, precision=high, preferred_element_type=f32)
            + crossing
        )
        decay_grad = decayed * inside
        size_grad = dsl_ref[:, :groups] + size_carry
        rate = rate_ref[1:2, :]
        step_grad = (size_grad - rate * decay_grad) * col_ref[:, 3 * groups + 7 :]
        step_grad_ref[...] = step_grad.astype(bf16)
        sum_ref[0:1, step_at : step_at + groups] += jnp.sum(step_grad, axis=0, keepdims=True)
        sum_ref[0:1, step_at + groups : step_at + 2 * groups] -= jnp.sum(
            decay_grad * step * rate, axis=0, keepdims=True
        )
        adjoint[...] = entry_wide[CHUNK - 1 : CHUNK, :] * held + mm_two(stt_ref[STATE:, :], y_entry)

        grad = conv_back_step(
            act_grad, pre_ref[...], value_ref[...].astype(f32), taps_ref, match, next_ref, sum_inner_ref
        )
        grad_ref[...] = grad.astype(bf16)
        grad_state = conv_back_step(
            jnp.concatenate([in_grad, out_grad], axis=1),
            pre_state_ref[...],
            value_state_ref[...].astype(f32),
            taps_state_ref,
            match,
            next_state_ref,
            sum_state_ref,
        )
        grad_state_ref[...] = grad_state.astype(bf16)
        grad_state_t_ref[...] = jnp.transpose(grad_state)

        @pl.when(step_index == 0)
        def _():
            tail_ref[:, :width] = grad[CHUNK - 16 :]
            tail_ref[:, width:] = grad_state[CHUNK - 16 :]


def norm_kernel(count, cols, planes_each, place_ref, gain_ref, wt_ref, ws_ref, ws_t_ref, *refs):
    pieces = refs[: PLANE * count]
    before_refs = refs[PLANE * count : (PLANE + 1) * count]
    out_ref, share_ref, value_ref, raw_ref, raw_row_ref, halo_ref, halo_value_ref = refs[
        (PLANE + 1) * count :
    ]
    place = place_ref[0]
    head = place_ref[1]
    share = pieces[0].shape[1]

    @pl.when(pl.program_id(0) == 0)
    def _():
        wide = [ref[...].astype(f32) for ref in before_refs]
        total = 0.0
        for q in range(count):
            total = total + jnp.sum(wide[q] * wide[q], axis=1, keepdims=True)
        inverse = lax.rsqrt(total / D + eps)
        for q in range(count):
            lanes = pl.ds(pl.multiple_of((head ^ q) * share, 128), share)
            halo_ref[:, lanes] = (wide[q] * inverse * gain_ref[:, lanes]).astype(bf16)
        halo_value_ref[...] = mm(halo_ref[...], wt_ref[...]).astype(bf16)

    for r in range(PLANE):

        @pl.when(pl.program_id(0) == r)
        def _():
            wide = [pieces[r * count + q][...].astype(f32) for q in range(count)]
            total = 0.0
            for q in range(count):
                total = total + jnp.sum(wide[q] * wide[q], axis=1, keepdims=True)
            inverse = lax.rsqrt(total / D + eps)
            for q in range(count):
                lanes = pl.ds(pl.multiple_of((head ^ q) * share, 128), share)
                out_ref[:, lanes] = (wide[q] * inverse * gain_ref[:, lanes]).astype(bf16)
            for t in range(PLANE):

                @pl.when(place == t)
                def _():
                    for z in range(planes_each):
                        share_ref[0, :, z * cols : (z + 1) * cols] = pieces[r * count][
                            :, (z * PLANE + t) * cols : (z * PLANE + t + 1) * cols
                        ]

    normed = out_ref[...]
    value_ref[...] = mm(normed, wt_ref[...]).astype(bf16)
    raw_ref[...] = mm(normed, ws_ref[...])
    raw_row_ref[...] = mm_t(ws_t_ref[...], normed)


def shift_in(value, last, reach, row):
    rolled = pltpu.roll(value, reach, 0)
    top = jnp.where(row < reach, pltpu.roll(last, reach, 0), rolled[:8])
    return jnp.concatenate([top, rolled[8:]], axis=0)


def conv_step(value, last_ref, taps_ref, match):
    row = lax.broadcasted_iota(jnp.int32, (8, value.shape[1]), 0)
    last = last_ref[...]
    pre = taps_ref[4:5, :] + taps_ref[3:4, :] * value
    for k in range(KERNEL - 1):
        moved = shift_in(value, last, KERNEL - 1 - k, row)
        pre = pre + taps_ref[k : k + 1, :] * moved * match[k]
    last_ref[...] = value[value.shape[0] - 8 :]
    return pre


def softplus(a):
    return jnp.maximum(a, 0.0) + jnp.log1p(jnp.exp(-jnp.abs(a)))


def vectors_kernel(
    groups, turn,
    base_ref,
    value_ref,
    halo_ref,
    raw_ref,
    raw_row_ref,
    taps_ref,
    starts_ref,
    starts_t_ref,
    head_row_ref,
    head_col_ref,
    pre_ref,
    act_ref,
    act_t_ref,
    col_ref,
    row_ref,
    decay_ref,
    last_ref,
    total_ref,
):
    chunk = turn

    @pl.when(chunk == 0)
    def _():
        last_ref[...] = halo_ref[...].astype(f32)[8:]
        total_ref[...] = jnp.zeros_like(total_ref)

    base = base_ref[0]
    first = base + chunk * CHUNK

    def doc_of(position):
        return jnp.sum((position >= starts_ref[...]).astype(f32), axis=1, keepdims=True)

    place = first + lax.broadcasted_iota(jnp.int32, (CHUNK, 1), 0)
    corner = jnp.zeros((1, 1), jnp.int32)
    doc = doc_of(place)
    match = [(doc_of(place - (KERNEL - 1) + k) == doc).astype(f32) for k in range(KERNEL - 1)]
    from_start = (doc == doc_of(corner + (first - 1))).astype(f32)
    to_end = (doc == doc_of(corner + (first + CHUNK - 1))).astype(f32)
    whole_start = (doc == doc_of(corner + (base - 1))).astype(f32)
    place_row = first + lax.broadcasted_iota(jnp.int32, (1, CHUNK), 1)
    row_ref[2 * groups : 2 * groups + 1, :] = jnp.sum(
        (place_row >= starts_t_ref[...]).astype(f32), axis=0, keepdims=True
    )

    pre = conv_step(value_ref[...].astype(f32), last_ref, taps_ref, match)
    pre_ref[...] = pre
    act = pre * jax.nn.sigmoid(pre)
    act_ref[...] = act.astype(bf16)
    act_t_ref[...] = jnp.transpose(act).astype(bf16)

    shifted_raw = raw_ref[...] + head_row_ref[0:1, :]
    step = softplus(shifted_raw)
    col_ref[:, 3 * groups + 7 :] = jax.nn.sigmoid(shifted_raw)
    row, col = rows_cols()
    lower = (row >= col).astype(f32)
    cum = jnp.dot(
        lower, -step * head_row_ref[1:2, :], precision=high, preferred_element_type=f32
    )
    whole = cum + total_ref[0:1, :]
    total_ref[...] = jnp.broadcast_to(whole[CHUNK - 1 : CHUNK, :], total_ref.shape)
    entry_whole = jnp.exp(whole) * whole_start
    col_ref[:, :groups] = cum
    col_ref[:, groups : 2 * groups] = step
    col_ref[:, 2 * groups : 3 * groups] = entry_whole
    for n, column in enumerate([doc, from_start, to_end, match[2]] + match):
        col_ref[:, 3 * groups + n : 3 * groups + n + 1] = column
    step_row = softplus(raw_row_ref[:groups, :] + head_col_ref[:, 0:1])
    row_ref[:groups, :] = lax.dot_general(
        -step_row * head_col_ref[:, 1:2],
        lower,
        (((1,), (1,)), ((), ())),
        precision=high,
        preferred_element_type=f32,
    )
    row_ref[groups : 2 * groups, :] = step_row
    decay_ref[...] = widen(
        jnp.broadcast_to(entry_whole[CHUNK - 1 : CHUNK, :], (8, groups)),
        head_mask(groups, decay_ref.shape[1]),
    )


def convolve_kernel(
    groups, turn, value_ref, halo_ref, stt_ref, col_ref, taps_ref, pre_ref, x_ref, state_ref, last_ref
):
    @pl.when(turn == 0)
    def _():
        last_ref[...] = halo_ref[...].astype(f32)[8:]
        state_ref[...] = jnp.zeros_like(state_ref)

    mask = head_mask(groups, x_ref.shape[1])
    match = [col_ref[:, 3 * groups + 4 + k : 3 * groups + 5 + k] for k in range(KERNEL - 1)]
    pre = conv_step(value_ref[...].astype(f32), last_ref, taps_ref, match)
    pre_ref[...] = pre
    x_low = (pre * jax.nn.sigmoid(pre)).astype(bf16)
    x_ref[...] = x_low
    cum = col_ref[:, :groups]
    cum_last = cum[CHUNK - 1 : CHUNK, :]
    from_start = col_ref[CHUNK - 1 : CHUNK, 3 * groups + 1 : 3 * groups + 2]
    to_end = col_ref[:, 3 * groups + 2 : 3 * groups + 3]
    ending = widen(jnp.exp(cum_last - cum) * to_end * col_ref[:, groups : 2 * groups], mask)
    kept = widen(jnp.broadcast_to(jnp.exp(cum_last) * from_start, (8, groups)), mask)
    state_ref[...] = kept[0:1, :] * state_ref[...] + mm_two(
        stt_ref[:STATE, :], x_low.astype(f32) * ending
    )


def weight_kernel(groups, *refs):
    refs = refs[1:]
    out_ref = refs[2 * PLANE]
    for r in range(PLANE):

        @pl.when(pl.program_id(0) == r)
        def _():
            for g in range(groups):
                lanes = slice(g * P_SIZE, (g + 1) * P_SIZE)
                both = [refs[r][:, lanes].astype(f32), refs[PLANE + r][:, lanes].astype(f32)]
                out_ref[:, g, :] = jnp.concatenate(both, axis=1)


def unpack_kernel(groups, state_rows, place_ref, *refs):
    small_refs = refs[:2]
    (
        state_ref,
        taps_ref,
        bias_ref,
        gated_ref,
        state_taps_ref,
        state_bias_ref,
        shift_ref,
        rate_ref,
        skip_ref,
        step_ref,
        total_ref,
    ) = refs[2:]
    head = place_ref[1]
    core = place_ref[0] & 1
    width = groups * P_SIZE
    sums = 8 + groups
    heads = small_refs[0].shape[1]
    state_at = 2 * width
    step_at = state_at + 2 * STATE
    total_ref[...] = jnp.zeros_like(total_ref)
    for side in range(2):
        for near in range(2):

            @pl.when(core == side ^ near)
            def _():
                for y in range(2):
                    for h in range(heads):
                        rows = small_refs[near]
                        state = rows[y, h, :state_rows, :].astype(f32)
                        at = (side * 2 + y) * (STATE // 2) + h * state_rows
                        state_ref[:, at : at + state_rows] = jnp.transpose(state)
                        value = (
                            rows[y, h, state_rows : state_rows + sums, :].astype(f32)
                            + rows[y, h, state_rows + sums :, :].astype(f32)
                        )
                        total_ref[...] += value[:8]
                        inner = y * 2 + side
                        for g in range(groups):
                            number = (inner * groups + g) * heads + h
                            here = slice(number * P_SIZE, (number + 1) * P_SIZE)
                            lanes = slice(g * P_SIZE, (g + 1) * P_SIZE)
                            taps_ref[:, here] = value[:KERNEL, lanes]
                            bias_ref[:, here] = value[KERNEL : KERNEL + 1, lanes]
                            lanes = slice(width + g * P_SIZE, width + (g + 1) * P_SIZE)
                            gated_ref[:, here] = value[0:1, lanes]
                            skip_ref[:, number : number + 1] = jnp.sum(
                                value[1:2, lanes], axis=1, keepdims=True
                            )
                            lane = step_at + g
                            shift_ref[:, number : number + 1] = value[0:1, lane : lane + 1]
                            lane = step_at + groups + g
                            rate_ref[:, number : number + 1] = value[0:1, lane : lane + 1]

                        @pl.when(head == h)
                        def _():
                            step_ref[inner * groups : (inner + 1) * groups, :] = value[8:]

    state_taps_ref[...] = total_ref[:KERNEL, state_at:step_at]
    state_bias_ref[...] = total_ref[KERNEL : KERNEL + 1, state_at:step_at]


def normed_back_kernel(
    place_ref,
    z_ref,
    inner_ref,
    step_ref,
    state_ref,
    normed_ref,
    wg_ref,
    wi_ref,
    ws_ref,
    wt_ref,
    own_ref,
    across_ref,
    core_ref,
    gain_ref,
    total_ref,
):
    total = (
        mm_t(z_ref[...], wg_ref[...])
        + mm_t(inner_ref[...], wi_ref[...])
        + mm_t(step_ref[...], ws_ref[...])
        + mm_t(state_ref[...], wt_ref[...])
    )
    total_ref[...] = total
    gain = jnp.sum(total * normed_ref[...].astype(f32), axis=0, keepdims=True)
    gain_ref[...] = jnp.broadcast_to(gain, gain_ref.shape)
    rows = own_ref.shape[0]
    place = place_ref[0]

    def block(r):
        return total_ref[pl.ds(pl.multiple_of((place ^ r) * rows, rows), rows), :]

    own_ref[...] = block(0)
    core_ref[0] = block(1).astype(bf16)
    across_ref[...] = block(2)
    core_ref[1] = block(3).astype(bf16)


def level_of(place, half):
    return jnp.where(place == 0, 3 - half, jnp.where(place == 1, 1, 0))


def split_kernel(count, cols, place_ref, whole_ref, *out_refs):
    place = place_ref[0]
    for r in range(PLANE):
        for t in range(PLANE):

            @pl.when(place == t ^ r)
            def _():
                for z in range(count):
                    out_refs[r][0, :, z * cols : (z + 1) * cols] = whole_ref[
                        0, :, (z * PLANE + t) * cols : (z * PLANE + t + 1) * cols
                    ]


def join_kernel(count, cols, place_ref, *refs):
    place = place_ref[0]
    out_ref = refs[PLANE]
    for r in range(PLANE):
        for t in range(PLANE):

            @pl.when(place == t ^ r)
            def _():
                for z in range(count):
                    out_ref[0, :, (z * PLANE + t) * cols : (z * PLANE + t + 1) * cols] = refs[r][
                        0, :, z * cols : (z + 1) * cols
                    ]


def pick_part(near_refs, first_refs, second_refs, cot_ref):
    step = pl.program_id(0)

    @pl.when(step < 2)
    def _():
        for q, near in enumerate(near_refs):
            cot_ref[q] = near[0]

    @pl.when(step == 2)
    def _():
        for q, first in enumerate(first_refs):
            cot_ref[q] = first[...]

    @pl.when(step == 3)
    def _():
        for q, second in enumerate(second_refs):
            cot_ref[q] = second[...]


def weight_rows_of(weight_ref, count, head, owner, span):
    each = weight_ref.shape[0] // count
    return jnp.concatenate(
        [weight_ref[(head ^ q) * each + z, owner, span, :] for q in range(count) for z in range(each)],
        axis=1,
    )


def scale_kernel(sum_ref, row_ref, col_ref):
    level = lax.broadcasted_iota(jnp.int32, sum_ref.shape, 0)
    width = jnp.zeros(sum_ref.shape, f32) + 1.0
    for m in range(4):
        width = jnp.where(level == m, float(INNER >> m), width)
    scale = lax.rsqrt(sum_ref[...] / width + eps)
    row_ref[...] = scale
    col_ref[...] = jnp.transpose(scale)


def out_back_kernel(count, place_ref, scale_ref, weight_ref, *refs):
    part_refs = refs[3 * count : 3 * count + PLANE]
    sum_ref, low_ref, cot_ref = refs[3 * count + PLANE :]
    pick_part(refs[:count], refs[count : 2 * count], refs[2 * count : 3 * count], cot_ref)
    place = place_ref[0]
    half = cot_ref.shape[3]
    for q in range(count):
        lanes = slice(q * half, (q + 1) * half)
        total = None
        for m in range(4):
            grad = (scale_ref[:, m : m + 1] * cot_ref[q, m].astype(f32)).astype(bf16)
            total = grad.astype(f32) if m == 0 else total + grad.astype(f32)
            upper, lower = split_two(total)
            sum_ref[m, :, lanes] = upper
            low_ref[m, :, lanes] = lower
    rows = weight_ref.shape[2] // 2
    for r in range(PLANE):
        owner = place ^ r
        for side in range(2):
            level = level_of(owner, side)
            span = slice(side * rows, (side + 1) * rows)
            weight = weight_rows_of(weight_ref, count, place_ref[1], owner, span)
            part = mm_t(sum_ref[level], weight)
            out_ref = part_refs[r]

            @pl.when(owner < 2)
            def _():
                out_ref[:, span] = (part + mm_t(low_ref[level], weight)).astype(out_ref.dtype)

            @pl.when(owner >= 2)
            def _():
                out_ref[:, span] = part.astype(out_ref.dtype)


def product_kernel(count, place_ref, weight_ref, *refs):
    u_refs = refs[:PLANE]
    cot_refs = refs[PLANE : PLANE + 3 * count]
    refs = refs[PLANE + 3 * count :]
    dot_ref, own_ref = refs[:2]
    send_refs = refs[2 : count + 1]
    block_ref, cot_ref = refs[count + 1 :]
    pick_part(cot_refs[:count], cot_refs[count : 2 * count], cot_refs[2 * count :], cot_ref)
    place = place_ref[0]
    half = cot_ref.shape[3]
    rows = weight_ref.shape[2] // 2
    block_ref[...] = jnp.zeros_like(block_ref)
    for r in range(PLANE):
        owner = place ^ r
        for side in range(2):
            span = slice(side * rows, (side + 1) * rows)
            weight = weight_rows_of(weight_ref, count, place_ref[1], owner, span)
            block_ref[level_of(owner, side)] += mm(u_refs[r][:, span], weight)
    running = None
    ones = jnp.ones((8, half), bf16)
    dot_ref[4:8, :] = jnp.zeros((4, dot_ref.shape[1]), f32)
    for m in (3, 2, 1, 0):
        running = block_ref[m] if running is None else running + block_ref[m]
        dots = 0.0
        for q in range(count):
            part = running[:, q * half : (q + 1) * half]
            dots = dots + cot_ref[q, m].astype(f32) * part
            if q == 0:
                own_ref[0, m] = part
            else:
                send_refs[q - 1][0, m] = part.astype(bf16)
        upper, lower = split_two(dots)
        dot_ref[m : m + 1, :] = (mm_t(ones, upper) + mm_t(ones, lower))[0:1, :]


def mix_kernel(count, scale_ref, tok_ref, own_ref, *refs):
    got_refs = refs[: count - 1]
    out_refs = refs[count - 1 :]
    for r in range(PLANE):

        @pl.when(pl.program_id(0) == r)
        def _():
            for m in range(4):
                total = own_ref[0, m]
                for got in got_refs:
                    total = total + got[0, m].astype(f32)
                out_refs[r][m] = (
                    tok_ref[0].astype(f32) + scale_ref[:, m : m + 1] * total
                ).astype(bf16)


def out_weight_kernel(count, planes_each, cols, place_ref, sum_ref, *refs):
    u_refs = refs[:PLANE]
    out_ref = refs[PLANE]
    place = place_ref[0]
    head = place_ref[1]
    rows = u_refs[0].shape[1] // 2
    for r in range(PLANE):

        @pl.when(pl.program_id(0) == r)
        def _():
            owner = place ^ r
            for side in range(2):
                span = slice(side * rows, (side + 1) * rows)
                grad = t_mm(u_refs[r][:, span], sum_ref[level_of(owner, side)])
                for q in range(count):
                    for z in range(planes_each):
                        lanes = slice((q * planes_each + z) * cols, (q * planes_each + z + 1) * cols)
                        out_ref[(head ^ q) * planes_each + z, span, :] = grad[:, lanes].astype(bf16)


def per_chunk(width):
    return "rows", pl.BlockSpec((SUB * CHUNK, width), lambda c, *rest: (c, 0))


def across(height):
    return "cols", pl.BlockSpec((height, SUB * CHUNK), lambda c, *rest: (0, c))


def fixed(*shape):
    return "fixed", pl.BlockSpec(shape, lambda c, *rest: (0,) * len(shape))


def spread(kernel, specs, reverse=False, ahead=0):
    def view(kind, ref, sub):
        part = pl.ds(sub * CHUNK, CHUNK)
        if kind == "rows":
            return ref.at[part, :]
        return ref.at[:, part] if kind == "cols" else ref

    def run(*refs):
        first, refs = refs[:ahead], refs[ahead:]
        for n in range(SUB):
            sub = SUB - 1 - n if reverse else n
            views = [view(kind, ref, sub) for (kind, _), ref in zip(specs, refs)]
            kernel(pl.program_id(0) * SUB + n, *first, *views, *refs[len(specs) :])

    return run


def shaped(shape, kind=f32):
    return jax.ShapeDtypeStruct(shape, kind)


def contract(left_side, right_side, left_dim, right_dim):
    return lax.dot_general(
        left_side,
        right_side,
        (((left_dim,), (right_dim,)), ((), ())),
        preferred_element_type=f32,
    )


def own_heads(values, heads):
    shape = values.shape[:-1]
    shaped_values = values.reshape(shape + (PLANE, -1, lax.axis_size("h"), heads))
    mine = take(shaped_values, lax.axis_index("i"), len(shape))
    mine = take(mine, lax.axis_index("h"), len(shape) + 1)
    return mine.reshape(shape + (-1,))


def shards(
    tokens,
    cotangent,
    doc_lengths,
    input_gain,
    input_weight,
    step_weight,
    state_weight,
    conv_inner,
    conv_inner_bias,
    conv_state,
    conv_state_bias,
    step_bias,
    decay_log,
    skip_gain,
    gated_gain,
    output_weight,
):
    planes = lax.axis_size("o")
    head_count = lax.axis_size("h")
    plane = lax.axis_index("o")
    inner = lax.axis_index("i")
    head = lax.axis_index("h")
    here = jnp.stack([inner, head]).astype(jnp.int32)
    tok_rows, share = tokens.shape
    span = tok_rows * PLANE
    steps = span // CHUNK
    weight_rows, groups_all = input_weight.shape[:2]
    groups = groups_all // PLANE
    width = groups * P_SIZE
    wide_rows = groups_all * P_SIZE
    cols = output_weight.shape[2]
    own_planes = planes // head_count
    half = own_planes * cols
    pad = KERNEL - 1
    halo = 16
    fence = lax.optimization_barrier

    def token_block(*rest):
        return pl.BlockSpec((tok_rows,) + rest, lambda r, place: (r ^ place[0],) + (0,) * len(rest))

    def part_block(*rest):
        return pl.BlockSpec((1,) + rest, lambda r, place: (r,) + (0,) * len(rest))

    def whole_block(*shape):
        return pl.BlockSpec(shape, lambda r, place: (0,) * len(shape))

    def placed_call(kernel, in_specs, out_specs, out_shape, scratch, name):
        return pl.pallas_call(
            kernel,
            grid_spec=pltpu.PrefetchScalarGridSpec(
                num_scalar_prefetch=1,
                grid=(PLANE,),
                in_specs=in_specs,
                out_specs=out_specs,
                scratch_shapes=scratch,
            ),
            out_shape=out_shape,
            compiler_params=PARAMS,
            name=name,
        )

    def placed_call_once(kernel, out_shape, scratch, name):
        return pl.pallas_call(
            kernel,
            grid_spec=pltpu.PrefetchScalarGridSpec(
                num_scalar_prefetch=1,
                grid=(1,),
                in_specs=[pl.BlockSpec(memory_space=pltpu.VMEM)] * 2,
                out_specs=[pl.BlockSpec(memory_space=pltpu.VMEM)] * len(out_shape),
                scratch_shapes=scratch,
            ),
            out_shape=out_shape,
            compiler_params=PARAMS,
            name=name,
        )

    def unplaced(kernel):
        return lambda place_ref, *refs: kernel(*refs)

    def chunk_call(kernel, in_specs, out_specs, out_shape, scratch, name, ahead=0):
        return pl.pallas_call(
            spread(kernel, in_specs + out_specs, ahead=ahead),
            grid_spec=pltpu.PrefetchScalarGridSpec(
                num_scalar_prefetch=ahead,
                grid=(steps // SUB,),
                in_specs=[spec for _, spec in in_specs],
                out_specs=[spec for _, spec in out_specs],
                scratch_shapes=scratch,
            ),
            out_shape=out_shape,
            compiler_params=PARAMS,
            name=name,
        )

    pieces = input_weight.reshape(weight_rows, PLANE, groups, 2, P_SIZE)

    def head_pieces(side):
        return jnp.transpose(pieces[:, :, :, side, :], (1, 0, 2, 3)).reshape(
            PLANE, weight_rows, width
        )

    inner_pieces = exchange_inner(head_pieces(1))
    near = [swap(tokens, "h", q) if q else tokens for q in range(head_count)]
    far = swap(tokens, "i", 2)
    step_planes = stack_planes(step_weight.reshape(weight_rows, groups_all))
    before = shifted(tokens[tok_rows - halo :], "o", 1)
    before = jnp.where(inner == PLANE - 1, before, jnp.zeros_like(before))
    near, far, inner_pieces, step_planes, before = fence(
        (near, far, inner_pieces, step_planes, before)
    )
    weight_inner = lax.all_gather(
        inner_pieces.reshape(PLANE * weight_rows, width), "o", axis=0, tiled=True
    )
    sibling = [swap(b, "i", 1) for b in near]
    before = before + swap(before, "i", 2)
    before = before + swap(before, "i", 1)
    before = [swap(before, "h", q) if q else before for q in range(head_count)]
    weight_step = jnp.transpose(stack_inner(step_planes), (1, 0, 2, 3)).reshape(D, groups_all)
    weight_step = lax.dynamic_slice_in_dim(weight_step, inner * groups, groups, 1)
    weight_step_t = jnp.pad(jnp.transpose(weight_step), ((0, 16 - groups), (0, 0)))
    far = [swap(far, "h", q) if q else far for q in range(head_count)]
    gate_pieces, before, far, sibling, weight_step, weight_step_t = fence(
        (
            exchange_inner(fence((head_pieces(0), near))[0]),
            before,
            far,
            sibling,
            weight_step,
            weight_step_t,
        )
    )
    weight_gate = lax.all_gather(
        gate_pieces.reshape(PLANE * weight_rows, width), "o", axis=0, tiled=True
    )
    blocks = [near, sibling, far, [swap(b, "i", 1) for b in far]]
    normed, tok_share, state_value, step_raw, step_row, normed_halo, state_halo = placed_call(
        partial(norm_kernel, head_count, cols, own_planes),
        [
            whole_block(1, D),
            whole_block(D, 2 * STATE),
            whole_block(D, groups),
            whole_block(16, D),
        ]
        + [whole_block(tok_rows, share)] * (PLANE * head_count)
        + [whole_block(halo, share)] * head_count,
        [
            token_block(D),
            part_block(tok_rows, half),
            token_block(2 * STATE),
            token_block(groups),
            pl.BlockSpec((16, tok_rows), lambda r, place: (0, r ^ place[0])),
            whole_block(halo, D),
            whole_block(halo, 2 * STATE),
        ],
        [
            shaped((span, D), bf16),
            shaped((PLANE, tok_rows, half), bf16),
            shaped((span, 2 * STATE), bf16),
            shaped((span, groups)),
            shaped((16, span)),
            shaped((halo, D), bf16),
            shaped((halo, 2 * STATE), bf16),
        ],
        [],
        "norm",
    )(
        here,
        input_gain[None],
        state_weight,
        weight_step,
        weight_step_t,
        *[b for row in blocks for b in row],
        *before,
    )

    weight_out = lax.all_gather(output_weight.reshape(wide_rows, cols), "o")
    weight_out = weight_out.reshape(planes, PLANE, width, cols)

    cotangent_later, normed = fence((cotangent, normed))
    largest = jnp.max(jnp.abs(cotangent_later)).astype(f32)
    cot_parts = pl.pallas_call(
        partial(split_kernel, own_planes, cols),
        grid_spec=pltpu.PrefetchScalarGridSpec(
            num_scalar_prefetch=1,
            grid=(4,),
            in_specs=[pl.BlockSpec((1, tok_rows, share), lambda m, place: (m, 0, 0))],
            out_specs=[pl.BlockSpec((1, tok_rows, half), lambda m, place: (m, 0, 0))] * PLANE,
        ),
        out_shape=[shaped((4, tok_rows, half), bf16)] * PLANE,
        compiler_params=PARAMS,
        name="split",
    )(here, cotangent_later)
    cot_near = jnp.stack([cot_parts[0], swap(cot_parts[1], "i", 1)])
    cot_sent = [swap(cot_parts[2], "i", 2), swap(cot_parts[3], "i", 3)]
    cot_near = [swap(cot_near, "h", q) if q else cot_near for q in range(head_count)]

    starts = (jnp.cumsum(doc_lengths) - doc_lengths).astype(jnp.int32)
    base = (plane * span).astype(jnp.int32).reshape(1)

    def taps_of(kernel, bias):
        return jnp.concatenate([kernel, bias[None], jnp.zeros((3, bias.shape[0]), f32)], axis=0)

    taps_inner = taps_of(own_heads(conv_inner, P_SIZE), own_heads(conv_inner_bias, P_SIZE))
    taps_state = taps_of(conv_state, conv_state_bias)
    gain_wide = own_heads(gated_gain, P_SIZE)
    step_shift = own_heads(step_bias, 1)
    rate_log = own_heads(decay_log, 1)
    skip_wide = jnp.repeat(own_heads(skip_gain, 1), P_SIZE)
    wide = jnp.concatenate([skip_wide[None], gain_wide[None], jnp.zeros((6, width), f32)], axis=0)
    group_number = inner * groups + jnp.arange(groups)
    level_limit = jnp.array([groups_all >> m for m in range(4)] + [0] * 4)
    level_mask = jnp.repeat(
        (group_number[None, :] < level_limit[:, None]).astype(bf16), P_SIZE, axis=1
    )

    rate = jnp.exp(rate_log)
    head_row = jnp.concatenate([step_shift[None], rate[None], jnp.zeros((6, groups), f32)], axis=0)
    head_col = jnp.stack([step_shift, rate], axis=1)
    col_width = 4 * groups + 7
    row_height = 2 * groups + 1

    pre_state, state_act, state_act_t, col_pack, row_pack, decay_wide = chunk_call(
        partial(vectors_kernel, groups),
        [
            per_chunk(2 * STATE),
            fixed(halo, 2 * STATE),
            per_chunk(groups),
            across(16),
            fixed(8, 2 * STATE),
            fixed(1, starts.shape[0]),
            fixed(starts.shape[0], 1),
            fixed(8, groups),
            fixed(groups, 2),
        ],
        [
            per_chunk(2 * STATE),
            per_chunk(2 * STATE),
            across(2 * STATE),
            per_chunk(col_width),
            across(row_height),
            fixed(8, width),
        ],
        [
            shaped((span, 2 * STATE)),
            shaped((span, 2 * STATE), bf16),
            shaped((2 * STATE, span), bf16),
            shaped((span, col_width)),
            shaped((row_height, span)),
            shaped((8, width)),
        ],
        [pltpu.VMEM((8, 2 * STATE), f32), pltpu.VMEM((8, groups), f32)],
        "vectors",
        ahead=1,
    )(
        base,
        state_value,
        state_halo,
        step_raw,
        step_row,
        taps_state,
        starts[None, :],
        starts[:, None],
        head_row,
        head_col,
    )
    decay_whole = decay_wide[0:1]

    wide_out = shaped((span, width))
    value = jnp.dot(normed, weight_inner, preferred_element_type=f32).astype(bf16)
    inner_halo = jnp.dot(normed_halo, weight_inner, preferred_element_type=f32).astype(bf16)
    pre_inner, x, own_state = chunk_call(
        partial(convolve_kernel, groups),
        [
            per_chunk(width),
            fixed(halo, width),
            across(2 * STATE),
            per_chunk(col_width),
            fixed(8, width),
        ],
        [per_chunk(width), per_chunk(width), fixed(STATE, width)],
        [wide_out, shaped((span, width), bf16), shaped((STATE, width))],
        [pltpu.VMEM((8, width), f32)],
        "convolve",
    )(value, inner_halo, state_act_t, col_pack, taps_inner)
    x, cot_near, cot_sent = fence((x, cot_near, cot_sent))
    cot_first = [swap(cot_sent[0], "h", q) if q else cot_sent[0] for q in range(head_count)]
    cot_second = [swap(cot_sent[1], "h", q) if q else cot_sent[1] for q in range(head_count)]
    incoming = chain(own_state, decay_whole, 1)
    (y_local,) = chunk_call(
        partial(within_kernel, groups),
        [per_chunk(width), per_chunk(2 * STATE), per_chunk(col_width), across(row_height)],
        [per_chunk(width)],
        [wide_out],
        [],
        "within",
    )(x, state_act, col_pack, row_pack)
    y_local, cot_first = fence((y_local, cot_first))
    gate_z = jnp.dot(normed, weight_gate, preferred_element_type=f32).astype(bf16)
    v, scaled_u, squares, entering = chunk_call(
        partial(carry_kernel, groups),
        [
            per_chunk(width),
            per_chunk(2 * STATE),
            across(2 * STATE),
            per_chunk(col_width),
            per_chunk(width),
            per_chunk(width),
            fixed(STATE, width),
            fixed(8, width),
            fixed(8, width),
        ],
        [per_chunk(width), per_chunk(width), across(8), per_chunk(width)],
        [
            wide_out,
            shaped((span, width), bf16),
            shaped((8, span)),
            shaped((steps * STATE, width)),
        ],
        [pltpu.VMEM((STATE, width), f32)],
        "carry",
    )(x, state_act, state_act_t, col_pack, y_local, gate_z, incoming, wide, level_mask)

    scaled_u, cot_second = fence((scaled_u, cot_second))
    cots = list(cot_near) + list(cot_first) + list(cot_second)

    squares = jnp.concatenate(
        [squares[:4], jnp.full((1, span), largest, f32), jnp.zeros((3, span), f32)], axis=0
    )
    squares = add_inner(add_all(add_inner(squares, 2), ("h",)), 1)
    scaled_u, squares = fence((scaled_u, squares))
    u_far = swap(scaled_u, "i", 2)
    u_parts = [scaled_u, swap(scaled_u, "i", 1), u_far, swap(u_far, "i", 1)]
    scales_row, scales = pl.pallas_call(
        scale_kernel,
        out_shape=[shaped((8, span)), shaped((span, 8))],
        compiler_params=pltpu.CompilerParams(vmem_limit_bytes=8 * 1024 * 1024),
        name="scales",
    )(squares)
    u_bound = squares[4, 0] * jnp.sum(jnp.max(scales_row[:4], axis=1))
    u_bound = u_bound * (0.1875 * 2.0 * head_count * half)
    scales, u_parts = fence((scales, u_parts))
    cot_block = part_block(4, tok_rows, half)
    weight_block = whole_block(planes, PLANE, width, cols)
    cot_near_block = pl.BlockSpec(
        (1, 4, tok_rows, half), lambda r, place: (jnp.minimum(r, 1), 0, 0, 0)
    )
    cot_blocks = [cot_near_block] * head_count
    cot_blocks += [whole_block(4, tok_rows, half)] * (2 * head_count)
    cot_scratch = pltpu.VMEM((head_count, 4, tok_rows, half), bf16)
    cot_shape = shaped((PLANE, 4, tok_rows, half), bf16)
    *parts, sums = placed_call(
        partial(out_back_kernel, head_count),
        [token_block(8), weight_block] + cot_blocks,
        [token_block(width)] * PLANE
        + [
            pl.BlockSpec((4, tok_rows, head_count * half), lambda r, place: (0, r ^ place[0], 0)),
        ],
        [wide_out] * PLANE + [shaped((4, span, head_count * half), bf16)],
        [pltpu.VMEM((4, tok_rows, head_count * half), bf16), cot_scratch],
        "out_back",
    )(here, scales, weight_out, *cots)
    u_scale = jnp.exp2(jnp.ceil(jnp.log2(jnp.clip(u_bound, 1e-30, 1e30))))
    out_grad = placed_call(
        partial(out_weight_kernel, head_count, own_planes, cols),
        [whole_block(4, span, head_count * half)] + [whole_block(span, width)] * PLANE,
        pl.BlockSpec((planes, width, cols), lambda r, place: (0, r ^ place[0], 0)),
        shaped((planes, wide_rows, cols), bf16),
        [],
        "out_weight_back",
    )(here, sums, *u_parts)

    parts_far = swap(parts[3], "i", 1)
    parts_far, out_grad_sent = fence((parts_far, out_grad))
    out_grad = lax.psum_scatter(out_grad_sent, "o", scatter_dimension=0, tiled=False)
    sent_across = ((parts[2] + parts_far) * (HALF_TOP / u_scale)).astype(jnp.float16)
    u_parts, sent_across = fence((u_parts, sent_across))
    got_across = swap(sent_across, "i", 2).astype(f32) * (u_scale / HALF_TOP)
    u_grad = parts[0] + swap(parts[1], "i", 1) + got_across
    dots, own_product, *sent_products = placed_call(
        partial(product_kernel, head_count),
        [weight_block]
        + [token_block(width)] * PLANE
        + cot_blocks,
        [pl.BlockSpec((8, tok_rows), lambda r, place: (0, r ^ place[0]))]
        + [cot_block] * head_count,
        [shaped((8, span)), shaped(cot_shape.shape)] + [cot_shape] * (head_count - 1),
        [pltpu.VMEM((4, tok_rows, head_count * half), f32), cot_scratch],
        "products",
    )(here, weight_out, *u_parts, *cots)
    dots = add_all(add_inner(dots, 1), ("h",))
    sent_products, dots = fence((sent_products, dots))
    dots = add_inner(dots, 2)
    y_grad, z_grad, wide_sums, leaving = chunk_call(
        partial(gate_back_kernel, groups),
        [
            per_chunk(width),
            per_chunk(width),
            per_chunk(width),
            per_chunk(width),
            across(2 * STATE),
            per_chunk(col_width),
            across(8),
            across(8),
            fixed(8, width),
            fixed(8, width),
        ],
        [per_chunk(width), per_chunk(width), fixed(8, width), fixed(STATE, width)],
        [wide_out, shaped((span, width), bf16), shaped((8, width)), shaped((STATE, width))],
        [],
        "gate_back",
    )(u_grad, v, gate_z, x, state_act_t, col_pack, dots, scales_row, wide, level_mask)
    lam = chain(leaving, decay_whole, -1)

    dx_local, dbc_local, ds_local = chunk_call(
        partial(within_back_kernel, groups),
        [
            per_chunk(width),
            per_chunk(2 * STATE),
            per_chunk(col_width),
            across(row_height),
            per_chunk(width),
        ],
        [per_chunk(width), per_chunk(2 * STATE), per_chunk(2 * groups)],
        [wide_out, shaped((span, 2 * STATE)), shaped((span, 2 * groups))],
        [],
        "within_back",
    )(x, state_act, col_pack, row_pack, y_grad)
    gate_z_grad, dx_local = fence((z_grad, dx_local))
    gate_part = contract(normed, gate_z_grad, 0, 0).astype(bf16)
    got_products = [swap(sent_products[q - 1], "h", q) for q in range(1, head_count)]
    lam, got_products, gate_part, out_grad = fence((lam, got_products, gate_part, out_grad))
    mixed_parts = placed_call(
        unplaced(partial(mix_kernel, head_count)),
        [token_block(8), part_block(tok_rows, half)] + [cot_block] * head_count,
        [whole_block(4, tok_rows, half)] * PLANE,
        [shaped((4, tok_rows, half), bf16)] * PLANE,
        [],
        "mix",
    )(here, scales, tok_share, own_product, *got_products)
    gate_grad = lax.psum_scatter(gate_part, "o", scatter_dimension=0, tiled=True)
    lam, mixed_parts = fence((lam, mixed_parts))
    mixed_parts = [mixed_parts[0]] + [swap(mixed_parts[r], "i", r) for r in range(1, PLANE)]
    turns = steps // SUB

    def back_rows(shape):
        return "rows", pl.BlockSpec(
            (SUB * CHUNK, shape), lambda c: (jnp.maximum(turns - 1 - c, 0), 0)
        )

    def back_cols(shape):
        return "cols", pl.BlockSpec(
            (shape, SUB * CHUNK), lambda c: (0, jnp.maximum(turns - 1 - c, 0))
        )

    back_wide = back_rows(width)
    back_state = back_rows(2 * STATE)
    both = width + 2 * STATE
    back_in = [
        back_wide,
        back_state,
        back_cols(2 * STATE),
        back_rows(col_width),
        back_cols(row_height),
        back_wide,
        back_wide,
        back_state,
        back_rows(2 * groups),
        back_wide,
        fixed(STATE, width),
        fixed(8, width),
        back_wide,
        back_wide,
        fixed(halo, width),
        fixed(8, width),
        back_state,
        back_state,
        fixed(halo, 2 * STATE),
        fixed(8, 2 * STATE),
        fixed(8, groups),
        fixed(8, width),
    ]
    back_out = [
        back_wide,
        fixed(16, both),
        fixed(8, both),
        fixed(8, D),
        back_state,
        ("cols", pl.BlockSpec((2 * STATE, SUB * CHUNK), lambda c: (0, turns - c))),
        back_rows(groups),
    ]
    inner_grad, tails, edges, narrow, state_grad, state_sum, step_grad_low = pl.pallas_call(
        spread(
            partial(carry_back_kernel, groups, steps), back_in + back_out, reverse=True
        ),
        grid=(turns + 1,),
        in_specs=[spec for _, spec in back_in],
        out_specs=[spec for _, spec in back_out],
        out_shape=[
            shaped((span, width), bf16),
            shaped((16, both)),
            shaped((8, both)),
            shaped((8, D)),
            shaped((span, 2 * STATE), bf16),
            shaped((2 * STATE, SUB * CHUNK + span)),
            shaped((span, groups), bf16),
        ],
        scratch_shapes=[
            pltpu.VMEM((STATE, width), f32),
            pltpu.VMEM((24, width), f32),
            pltpu.VMEM((24, 2 * STATE), f32),
        ],
        compiler_params=PARAMS,
        name="carry_back",
    )(
        x,
        state_act,
        state_act_t,
        col_pack,
        row_pack,
        y_grad,
        dx_local,
        dbc_local,
        ds_local,
        entering,
        lam,
        wide,
        pre_inner,
        value,
        inner_halo,
        taps_inner,
        pre_state,
        state_value,
        state_halo,
        taps_state,
        head_row,
        wide_sums,
    )
    edges, state_sum, narrow, mixed_parts = fence((edges, state_sum, narrow, mixed_parts))
    edges = shifted(edges, "o", -1)

    def state_half(values, axis, bit):
        halves = values.reshape((2, values.shape[0] // 2, values.shape[1]))
        side = jnp.where((lax.axis_index(axis) & bit) != 0, 1, 0)
        return take(halves, side) + swap(take(halves, 1 - side), axis, bit)

    for axis, bit in (("i", 1), ("i", 2)) + tuple(("h", b) for b in reversed(bits_of("h"))):
        state_sum = state_half(state_sum, axis, bit)
    edges, state_sum, gate_grad = fence((edges, state_sum, gate_grad))
    state_rows = state_sum.shape[0]
    state_low = state_sum.astype(bf16)
    edge_at = (SUB - 1) * CHUNK
    state_part = jnp.dot(
        state_low[:, SUB * CHUNK :], normed, preferred_element_type=f32
    ) + jnp.dot(
        state_low[:, edge_at : edge_at + 8], normed_halo[8:], preferred_element_type=f32
    )
    step_part = contract(step_grad_low, normed, 0, 0)
    sum_rows = 8 + groups

    def packed_rows(sums, state):
        return jnp.concatenate([state.astype(bf16), *split_rows(sums)], axis=0)

    def unpacked_rows(rows):
        upper = rows[..., state_rows : state_rows + sum_rows, :].astype(f32)
        return upper + rows[..., state_rows + sum_rows :, :].astype(f32), rows[..., :state_rows, :]

    def plus_plane(sums, state, bit):
        got, got_state = unpacked_rows(swap(packed_rows(sums, state), "o", bit))
        return sums + got, state + got_state.astype(f32)

    small = jnp.concatenate([narrow, step_part], axis=0)
    tails = (tails + jnp.pad(edges, ((8, 0), (0, 0)))).astype(bf16)
    inner_grad = lax.dynamic_update_slice_in_dim(inner_grad, tails[:, :width], span - 16, 0)
    state_grad = lax.dynamic_update_slice_in_dim(state_grad, tails[:, width:], span - 16, 0)

    small, state_part = plus_plane(small, state_part, 1)
    part = D // 8

    def columns_of(rows):
        return pl.BlockSpec((rows, part), lambda c, place: (0, c))

    def rows_of(width):
        return pl.BlockSpec((part, width), lambda c, place: (c, 0))

    normed_own, normed_across, normed_core, gain_part = pl.pallas_call(
        normed_back_kernel,
        grid_spec=pltpu.PrefetchScalarGridSpec(
            num_scalar_prefetch=1,
            grid=(8,),
            in_specs=[
                whole_block(span, width),
                whole_block(span, width),
                whole_block(span, groups),
                whole_block(span, 2 * STATE),
                columns_of(span),
                rows_of(width),
                rows_of(width),
                rows_of(groups),
                rows_of(2 * STATE),
            ],
            out_specs=[
                columns_of(tok_rows),
                columns_of(tok_rows),
                pl.BlockSpec((2, tok_rows, part), lambda c, place: (0, 0, c)),
                columns_of(8),
            ],
            scratch_shapes=[pltpu.VMEM((span, part), f32)],
        ),
        out_shape=[
            shaped((tok_rows, D)),
            shaped((tok_rows, D)),
            shaped((2, tok_rows, D), bf16),
            shaped((8, D)),
        ],
        compiler_params=PARAMS,
        name="normed_back",
    )(
        here,
        z_grad,
        inner_grad,
        step_grad_low,
        state_grad,
        normed,
        weight_gate,
        weight_inner,
        weight_step,
        state_weight,
    )
    inner_grad, normed_core, small, state_part = fence((inner_grad, normed_core, small, state_part))

    inner_part = contract(normed, inner_grad, 0, 0).astype(bf16)
    got_core = swap(normed_core, "i", 1)
    gain_sum = add_inner(gain_part[0].reshape(8, -1), 1)
    for bit in bits_of("o")[1:]:
        small, state_part = plus_plane(small, state_part, bit)
    gate_back = scattered_inner(gate_grad.reshape(PLANE, weight_rows, width))
    inner_part, got_core, gain_sum = fence((inner_part, got_core, gain_sum))
    got_core, small, state_part, gate_back = fence((got_core, small, state_part, gate_back))
    inner_part = lax.psum_scatter(inner_part, "o", scatter_dimension=0, tiled=True)

    got_across = swap((normed_across + got_core[1].astype(f32)).astype(bf16), "i", 2)
    small = packed_rows(small, state_part)
    shape = small.shape
    for bit in bits_of("h"):
        small = stack_over(small, "h", bit, 0)
        small = small.reshape((-1,) + shape)
    gain_sum = add_all(gain_sum, ("h",))
    output_weight_grad = out_grad.astype(f32).reshape(groups_all, P_SIZE, cols)
    mixed = placed_call(
        partial(join_kernel, own_planes, cols),
        [part_block(tok_rows, half)] * PLANE,
        part_block(tok_rows, share),
        shaped((4, tok_rows, share), bf16),
        [],
        "join",
    )(here, *mixed_parts)
    got_across, gain_sum, small, mixed, output_weight_grad = fence(
        (got_across, gain_sum, small, mixed, output_weight_grad)
    )

    full_grad = scatter_heads(
        normed_own + got_core[0].astype(f32) + got_across.astype(f32), 1
    )
    small = stack_over(small, "i", 2, 0)
    gain_sum = gain_sum + swap(gain_sum, "o", 1)
    full_grad, gain_sum, small, inner_part = fence((full_grad, gain_sum, small, inner_part))

    own_wide = [near[q].astype(f32) for q in range(head_count)]
    square = sum(jnp.sum(a * a, axis=1, keepdims=True) for a in own_wide)
    inverse = lax.rsqrt(square / D + eps)
    gain_share = lax.dynamic_slice_in_dim(input_gain, head * share, share, 0)
    unit = own_wide[0] * inverse
    resid = jnp.sum(cotangent.astype(f32), axis=0)

    def weighted_of(values):
        return values * gain_share[None, :]

    def norm_row_sum(values):
        sums = jnp.sum(weighted_of(values) * unit, axis=1).reshape(-1, CHUNK)
        return add_all(sums, ("h",)).reshape(-1, 1)

    inner_back = scattered_inner(inner_part.reshape(PLANE, weight_rows, width))
    small = small.reshape((2, head_count) + shape)
    small_core = swap(small, "i", 1)
    for bit in bits_of("o")[1:]:
        gain_sum = gain_sum + swap(gain_sum, "o", bit)
    row_sum = norm_row_sum(full_grad)
    small_core, gain_sum, row_sum = fence((small_core, gain_sum, row_sum))
    gain_sum = add_inner(gain_sum, 2)
    heads_all = groups_all * head_count
    row_of = [shaped((1, INNER)), shaped((1, 2 * STATE)), shaped((1, heads_all))]
    state_weight_grad, *rows, step_rows = placed_call_once(
        partial(unpack_kernel, groups, state_rows),
        [
            shaped((D, 2 * STATE)),
            shaped((KERNEL, INNER)),
            row_of[0],
            row_of[0],
            shaped((KERNEL, 2 * STATE)),
            row_of[1],
            row_of[2],
            row_of[2],
            row_of[2],
            shaped((groups_all, D)),
        ],
        [pltpu.VMEM((8, D), f32)],
        "unpack",
    )(here, small, small_core)
    inner_back, step_rows = fence((inner_back, step_rows))
    taps_grad, bias_grad, gated_grad, state_taps_grad, *rows = rows
    state_bias_grad, shift_grad, rate_grad, skip_grad = rows
    input_gain_grad = gain_sum.reshape(D) / input_gain
    step_weight_grad = lax.dynamic_slice_in_dim(
        step_rows, (plane * PLANE + inner) * weight_rows, weight_rows, 1
    )
    step_weight_grad = jnp.transpose(step_weight_grad)[:, None, :]
    if groups % 8 == 0:
        input_weight_grad = placed_call(
            partial(weight_kernel, groups),
            [whole_block(weight_rows, width)] * (2 * PLANE),
            pl.BlockSpec((weight_rows, groups, 2 * P_SIZE), lambda r, place: (0, r ^ place[0], 0)),
            shaped((weight_rows, groups_all, 2 * P_SIZE)),
            [],
            "weight_grad",
        )(here, *gate_back, *inner_back)
    else:
        sides = []
        for back in (gate_back, inner_back):
            whole = jnp.zeros((PLANE, weight_rows, groups, P_SIZE), bf16)
            for r in range(PLANE):
                whole = put(whole, back[r].reshape(weight_rows, groups, P_SIZE), inner ^ r)
            sides.append(jnp.transpose(whole, (1, 0, 2, 3)))
        input_weight_grad = jnp.concatenate(sides, axis=3).astype(f32)
        input_weight_grad = input_weight_grad.reshape(weight_rows, groups_all, 2 * P_SIZE)

    tokens_grad = resid + inverse * (weighted_of(full_grad) - unit * (row_sum / D))
    return (
        mixed,
        tokens_grad,
        input_gain_grad,
        input_weight_grad,
        step_weight_grad,
        state_weight_grad,
        taps_grad,
        bias_grad.reshape(INNER),
        state_taps_grad,
        state_bias_grad.reshape(2 * STATE),
        shift_grad.reshape(heads_all),
        rate_grad.reshape(heads_all),
        skip_grad.reshape(heads_all),
        gated_grad.reshape(INNER),
        output_weight_grad,
    )


def solution(mesh):
    rows, heads = mesh.devices.shape
    cut = Mesh(mesh.devices.reshape(rows // PLANE, PLANE, heads), ("o", "i", "h"))
    both = ("o", "i")
    placed = (
        P(both, "h"),
        P(None, both, "h"),
        P(),
        P(),
        P(both, None, "h"),
        P(both, "h", None),
        P(),
        P(),
        P(),
        P(),
        P(),
        P(),
        P(),
        P(),
        P(),
        P(None, "h", both),
    )
    return jax.shard_map(
        shards,
        mesh=cut,
        in_specs=placed,
        out_specs=(
            P(None, both, "h"),
            P(both, "h"),
            P(),
            P(both, None, "h"),
            P(both, "h", None),
            P(),
            P(),
            P(),
            P(),
            P(),
            P(),
            P(),
            P(),
            P(),
            P(None, "h", both),
        ),
        check_vma=False,
    )
```

```python
from functools import partial

import jax
import jax.numpy as jnp
from jax import lax
from jax.experimental import pallas as pl
from jax.experimental.pallas import tpu as pltpu
from jax.sharding import Mesh
from jax.sharding import PartitionSpec as P

D = 2048
P_SIZE = 64
STATE = 128
KERNEL = 4
INNER = 4096
CHUNK = 128
SUB = 2
PLANE = 4

HALF_TOP = 16384.0

eps = 1e-05
bf16 = jnp.bfloat16
f32 = jnp.float32
high = lax.Precision.HIGHEST
PARAMS = pltpu.CompilerParams(
    vmem_limit_bytes=58 * 1024 * 1024, dimension_semantics=("arbitrary",)
)


def swap(block, axis, bit):
    return lax.ppermute(block, axis, [(a, a ^ bit) for a in range(lax.axis_size(axis))])


def shifted(block, axis, distance):
    devices = range(lax.axis_size(axis))
    route = [(a - distance, a) for a in devices if a - distance in devices]
    return lax.ppermute(block, axis, route)


def scattered_inner(blocks):
    place = lax.axis_index("i")
    got = {0: take(blocks, place)}
    for bit in (2, 3, 1):
        got[bit] = swap(take(blocks, place ^ bit), "i", bit)
    return [got[r] for r in range(PLANE)]


def bits_of(axis):
    count = lax.axis_size(axis)
    return [1 << b for b in range(count.bit_length() - 1)]


def take(values, index, axis=0):
    return lax.dynamic_index_in_dim(values, index, axis, keepdims=False)


def put(buffer, piece, index):
    return lax.dynamic_update_index_in_dim(buffer, piece, index, 0)


def add_all(value, axes):
    for axis in axes:
        for bit in bits_of(axis):
            value = value + swap(value, axis, bit)
    return value


def add_inner(value, bit):
    return value + swap(value, "i", bit)


def stack_over(value, axis, bit, at):
    other = swap(value, axis, bit)
    upper = (lax.axis_index(axis) & bit) != 0
    return jnp.where(
        upper, jnp.stack([other, value], axis=at), jnp.stack([value, other], axis=at)
    )


def stack_plane(value):
    shape = value.shape
    count = lax.axis_size("h")
    for bit in bits_of("h"):
        value = stack_over(value, "h", bit, 0)
        value = value.reshape((-1,) + shape) if bit > 1 else value
    value = value.reshape((count,) + shape)
    value = stack_over(value, "i", 2, 0)
    value = stack_over(value, "i", 1, 1)
    return value.reshape((PLANE, count) + shape)


def stack_planes(value):
    shape = value.shape
    for bit in bits_of("o"):
        value = stack_over(value, "o", bit, 0)
        value = value.reshape((-1,) + shape)
    return value


def stack_inner(value):
    shape = value.shape
    value = stack_over(value, "i", 2, 0)
    return stack_over(value, "i", 1, 1).reshape((PLANE,) + shape)


def exchange_inner(blocks):
    place = lax.axis_index("i")
    out = blocks
    for bit in (2, 3, 1):
        out = put(out, swap(take(blocks, place ^ bit), "i", bit), place ^ bit)
    return out


def scatter_heads(values, axis):
    count = lax.axis_size("h")
    if count != 2:
        return lax.psum_scatter(values, "h", scatter_dimension=axis, tiled=True)
    place = lax.axis_index("h")
    width = values.shape[axis] // 2
    sent = lax.dynamic_slice_in_dim(values, (1 - place) * width, width, axis)
    kept = lax.dynamic_slice_in_dim(values, place * width, width, axis)
    return kept + swap(sent.astype(bf16), "h", 1).astype(f32)


def column_power(values):
    largest = jnp.max(jnp.abs(values), axis=0, keepdims=True)
    exponent = jnp.ceil(jnp.log2(jnp.clip(largest, 1e-30, 1e30)))
    return jnp.exp2(exponent), exponent


def split_rows(values):
    upper = lax.reduce_precision(values, 8, 7)
    return upper.astype(bf16), (values - upper).astype(bf16)


def pack_half(values, extra=()):
    power, exponent = column_power(values)
    rows = [exponent]
    for row in extra:
        first = lax.reduce_precision(row, 5, 10)
        rows += [first, (row - first) * 2048.0]
    rows.append(jnp.zeros((16 - len(rows), values.shape[1]), f32))
    return jnp.concatenate([values * (HALF_TOP / power)] + rows, axis=0).astype(jnp.float16)


def unpack_half(packed):
    rows = packed.shape[0] - 16
    tail = packed[rows:].astype(f32)
    values = packed[:rows].astype(f32) * (jnp.exp2(tail[0:1]) / HALF_TOP)
    return values, tail[1:2] + tail[2:3] / 2048.0


def chain(state, decay_wide, direction):
    packed = pack_half(state, (decay_wide,))
    total = None
    for distance in range(lax.axis_size("o") - 1, 0, -1):
        own, decay = unpack_half(shifted(packed, "o", direction * distance))
        total = own if total is None else own + decay * total
    return total


def mm(a, b):
    return jnp.dot(a, b, preferred_element_type=f32)


def mm_two(a, b):
    upper, lower = split_two(b)
    return mm(a, upper) + mm(a, lower)


def mm_three(a, b):
    a_up, a_low = split_two(a)
    b_up, b_low = split_two(b)
    return mm_t(a_up, b_up) + mm_t(a_up, b_low) + mm_t(a_low, b_up)


def mm_t(a, b):
    return lax.dot_general(a, b, (((1,), (1,)), ((), ())), preferred_element_type=f32)


def t_mm(a, b):
    return lax.dot_general(a, b, (((0,), (0,)), ((), ())), preferred_element_type=f32)


def head_mask(groups, width):
    head = lax.broadcasted_iota(jnp.int32, (groups, width), 0)
    lane = lax.broadcasted_iota(jnp.int32, (groups, width), 1)
    return (lane // P_SIZE == head).astype(f32).astype(bf16)


def split_two(values):
    upper = values.astype(bf16)
    return upper, (values - upper.astype(f32)).astype(bf16)


def widen(values, mask):
    upper, lower = split_two(values)
    return mm(upper, mask) + mm(lower, mask)


def fold(values, mask):
    upper, lower = split_two(values)
    return mm_t(upper, mask) + mm_t(lower, mask)


def pair_masks():
    lane = lax.broadcasted_iota(jnp.int32, (1, 2 * P_SIZE), 1)
    lower = (lane < P_SIZE).astype(f32)
    return lower.astype(bf16), (1.0 - lower).astype(bf16)


def rows_cols():
    row = lax.broadcasted_iota(jnp.int32, (CHUNK, CHUNK), 0)
    col = lax.broadcasted_iota(jnp.int32, (CHUNK, CHUNK), 1)
    return row, col


def within_kernel(groups, turn, x_ref, st_ref, col_ref, row_ref, y_ref):
    b_in = st_ref[:, :STATE]
    c_out = st_ref[:, STATE:]
    scores = mm_t(c_out, b_in)
    doc_col = col_ref[:, 3 * groups : 3 * groups + 1]
    doc_row = row_ref[2 * groups : 2 * groups + 1, :]
    row, col = rows_cols()
    bias = jnp.where((doc_col == doc_row) & (row >= col), 0.0, -1e30)
    masks = pair_masks()
    for pair in range(groups // 2):
        lanes = slice(pair * 2 * P_SIZE, (pair + 1) * 2 * P_SIZE)
        x_pair = x_ref[:, lanes]
        weights, values = [], []
        for side in range(2):
            h = 2 * pair + side
            spread = jnp.exp(col_ref[:, h : h + 1] - row_ref[h : h + 1, :] + bias)
            weights.append(split_two(scores * spread * row_ref[groups + h : groups + h + 1, :]))
            values.append(x_pair * masks[side])
        value = jnp.concatenate(values, axis=0)
        y_ref[:, lanes] = mm(
            jnp.concatenate([weights[0][0], weights[1][0]], axis=1), value
        ) + mm(jnp.concatenate([weights[0][1], weights[1][1]], axis=1), value)


def carry_kernel(
    groups, turn,
    x_ref,
    st_ref,
    stt_ref,
    col_ref,
    yl_ref,
    gz_ref,
    inc_ref,
    wide_ref,
    level_ref,
    v_ref,
    u_ref,
    sq_ref,
    enter_ref,
    state,
):
    @pl.when(turn == 0)
    def _():
        state[...] = inc_ref[...]

    width = x_ref.shape[1]
    mask = head_mask(groups, width)
    cum = col_ref[:, :groups]
    step = col_ref[:, groups : 2 * groups]
    from_start = col_ref[:, 3 * groups + 1 : 3 * groups + 2]
    to_end = col_ref[:, 3 * groups + 2 : 3 * groups + 3]
    cum_last = cum[CHUNK - 1 : CHUNK, :]
    entry = jnp.exp(cum) * from_start
    ending = jnp.exp(cum_last - cum) * to_end * step
    entry_wide = widen(entry, mask)
    ending_wide = widen(ending, mask)
    held = state[...]
    enter_ref[...] = held
    carried = mm_two(st_ref[:, STATE:], held)
    x_wide = x_ref[...].astype(f32)
    v = yl_ref[...] + entry_wide * carried + wide_ref[0:1, :] * x_wide
    v_ref[...] = v
    z = gz_ref[...].astype(f32)
    gated = v * (z * jax.nn.sigmoid(z))
    u_ref[...] = (gated * wide_ref[1:2, :]).astype(bf16)
    upper, lower = split_two(gated * gated)
    sq_ref[...] = mm_t(level_ref[...], upper) + mm_t(level_ref[...], lower)
    added = mm_two(stt_ref[:STATE, :], x_wide * ending_wide)
    state[...] = entry_wide[CHUNK - 1 : CHUNK, :] * held + added


def gate_back_kernel(
    groups, turn,
    ug_ref,
    v_ref,
    gz_ref,
    x_ref,
    stt_ref,
    col_ref,
    dot_ref,
    scale_ref,
    wide_ref,
    level_ref,
    yg_ref,
    zg_ref,
    acc_ref,
    lam_ref,
):
    @pl.when(turn == 0)
    def _():
        acc_ref[...] = jnp.zeros_like(acc_ref)
        lam_ref[...] = jnp.zeros_like(lam_ref)

    mask = head_mask(groups, x_ref.shape[1])
    v = v_ref[...]
    z = gz_ref[...].astype(f32)
    sig = jax.nn.sigmoid(z)
    silu = z * sig
    gated = v * silu
    ug = ug_ref[...]
    level = lax.broadcasted_iota(jnp.int32, dot_ref.shape, 0)
    factor = jnp.zeros(dot_ref.shape, f32)
    for m in range(4):
        factor = jnp.where(level == m, -0.5 / (INNER >> m), factor)
    scale = scale_ref[...]
    upper, lower = split_two(dot_ref[...] * scale * scale * scale * factor)
    stat = t_mm(upper, level_ref[...]) + t_mm(lower, level_ref[...])
    gated_grad = ug * wide_ref[1:2, :] + 2.0 * gated * stat
    y_grad = gated_grad * silu
    yg_ref[...] = y_grad
    zg_ref[...] = (gated_grad * v * (sig * (1.0 + z * (1.0 - sig)))).astype(bf16)
    acc_ref[0:1, :] += jnp.sum(ug * gated, axis=0, keepdims=True)
    acc_ref[1:2, :] += jnp.sum(y_grad * x_ref[...].astype(f32), axis=0, keepdims=True)
    whole_entry = widen(col_ref[:, 2 * groups : 3 * groups], mask)
    lam_ref[...] += mm_two(stt_ref[STATE:, :], y_grad * whole_entry)


def within_back_kernel(groups, turn, x_ref, st_ref, col_ref, row_ref, yg_ref, dx_ref, dbc_ref, ds_ref):
    b_in = st_ref[:, :STATE]
    c_out = st_ref[:, STATE:]
    scores = mm_t(b_in, c_out)
    doc_col = col_ref[:, 3 * groups : 3 * groups + 1]
    doc_row = row_ref[2 * groups : 2 * groups + 1, :]
    row, col = rows_cols()
    same = doc_col == doc_row
    bias = jnp.where(same & (row <= col), 0.0, -1e30)
    masks = pair_masks()
    total = jnp.zeros((CHUNK, CHUNK), f32)
    head_lane = lax.broadcasted_iota(jnp.int32, (CHUNK, groups), 1)
    head_row = lax.broadcasted_iota(jnp.int32, (groups, CHUNK), 0)
    size_part = jnp.zeros((CHUNK, groups), f32)
    out_part = jnp.zeros((groups, CHUNK), f32)
    for pair in range(groups // 2):
        lanes = slice(pair * 2 * P_SIZE, (pair + 1) * 2 * P_SIZE)
        x_pair = x_ref[:, lanes]
        y_pair, y_rest = split_two(yg_ref[:, lanes])
        weights, values = [], []
        for side in range(2):
            h = 2 * pair + side
            step = col_ref[:, groups + h : groups + h + 1]
            spread = jnp.exp(row_ref[h : h + 1, :] - col_ref[:, h : h + 1] + bias)
            y_side = y_pair * masks[side]
            paired = spread * (mm_t(x_pair, y_side) + mm_t(x_pair, y_rest * masks[side]))
            total = total + step * paired
            product = scores * paired
            size_part = jnp.where(
                head_lane == h, jnp.sum(product, axis=1, keepdims=True), size_part
            )
            out_part = jnp.where(
                head_row == h, jnp.sum(step * product, axis=0, keepdims=True), out_part
            )
            weights.append((scores * spread).astype(bf16))
            values.append(y_side)
        dx_ref[:, lanes] = mm(jnp.concatenate(weights, axis=1), jnp.concatenate(values, axis=0))
    upper, lower = split_two(total)
    dbc_ref[:, :STATE] = mm(upper, c_out) + mm(lower, c_out)
    dbc_ref[:, STATE:] = t_mm(upper, b_in) + t_mm(lower, b_in)
    later = (same & (row <= col)).astype(f32)
    step_all = col_ref[:, groups : 2 * groups]
    ds_ref[:, :groups] = size_part
    ds_ref[:, groups:] = lax.dot_general(
        later, out_part, (((1,), (1,)), ((), ())), precision=high, preferred_element_type=f32
    ) - jnp.dot(later, step_all * size_part, precision=high, preferred_element_type=f32)


def conv_back_step(act_grad, pre, value, taps_ref, match, next_ref, sum_ref):
    sig = jax.nn.sigmoid(pre)
    slope = act_grad * (sig * (1.0 + pre * (1.0 - sig)))
    sum_ref[4:5, :] += jnp.sum(slope, axis=0, keepdims=True)
    sum_ref[3:4, :] += jnp.sum(slope * value, axis=0, keepdims=True)
    grad = taps_ref[3:4, :] * slope
    row = lax.broadcasted_iota(jnp.int32, (8, pre.shape[1]), 0)
    for k in range(KERNEL - 1):
        reach = KERNEL - 1 - k
        rolled = pltpu.roll(slope * match[k], CHUNK - reach, 0)
        last = rolled[CHUNK - 8 :]
        keep = row < 8 - reach
        after = next_ref[k * 8 : k * 8 + 8, :]
        moved = jnp.concatenate([rolled[: CHUNK - 8], jnp.where(keep, last, after)], axis=0)
        next_ref[k * 8 : k * 8 + 8, :] = jnp.where(keep, 0.0, last)
        grad = grad + taps_ref[k : k + 1, :] * moved
        sum_ref[k : k + 1, :] += jnp.sum(value * moved, axis=0, keepdims=True)
    return grad


def conv_back_edge(halo_ref, taps_ref, next_ref, sum_ref, edge_ref):
    value = halo_ref[...].astype(f32)[8:]
    edge = 0.0
    for k in range(KERNEL - 1):
        after = next_ref[k * 8 : k * 8 + 8, :]
        edge = edge + taps_ref[k : k + 1, :] * after
        sum_ref[k : k + 1, :] += jnp.sum(value * after, axis=0, keepdims=True)
    edge_ref[...] = edge


def carry_back_kernel(
    groups,
    turns,
    step_index,
    x_ref,
    st_ref,
    stt_ref,
    col_ref,
    row_ref,
    yg_ref,
    dxl_ref,
    dbcl_ref,
    dsl_ref,
    enter_ref,
    lam_ref,
    wide_ref,
    pre_ref,
    value_ref,
    halo_ref,
    taps_ref,
    pre_state_ref,
    value_state_ref,
    halo_state_ref,
    taps_state_ref,
    rate_ref,
    wide_sum_ref,
    grad_ref,
    tail_ref,
    edge_ref,
    sum_ref,
    grad_state_ref,
    grad_state_t_ref,
    step_grad_ref,
    adjoint,
    next_ref,
    next_state_ref,
):
    width = x_ref.shape[1]
    state_at = 2 * width
    step_at = state_at + 2 * STATE
    sum_inner_ref = sum_ref.at[:, :width]
    sum_state_ref = sum_ref.at[:, state_at:step_at]

    @pl.when(step_index == turns)
    def _():
        sum_ref[:, width:state_at] = wide_sum_ref[...]
        conv_back_edge(halo_ref, taps_ref, next_ref, sum_inner_ref, edge_ref.at[:, :width])
        edge_state_ref = edge_ref.at[:, width:]
        conv_back_edge(halo_state_ref, taps_state_ref, next_state_ref, sum_state_ref, edge_state_ref)
        edge = edge_state_ref[...]
        edge = jnp.concatenate([edge, jnp.zeros((CHUNK - 8, edge.shape[1]), f32)], axis=0)
        grad_state_t_ref[...] = jnp.transpose(edge)

    @pl.when(step_index == 0)
    def _():
        adjoint[...] = lam_ref[...]
        next_ref[...] = jnp.zeros_like(next_ref)
        next_state_ref[...] = jnp.zeros_like(next_state_ref)
        sum_ref[...] = jnp.zeros_like(sum_ref)

    @pl.when(step_index < turns)
    def _():
        mask = head_mask(groups, width)
        cum = col_ref[:, :groups]
        step = col_ref[:, groups : 2 * groups]
        from_start = col_ref[:, 3 * groups + 1 : 3 * groups + 2]
        to_end = col_ref[:, 3 * groups + 2 : 3 * groups + 3]
        inside = col_ref[:, 3 * groups + 3 : 3 * groups + 4]
        match = [col_ref[:, 3 * groups + 4 + k : 3 * groups + 5 + k] for k in range(KERNEL - 1)]
        cum_last = cum[CHUNK - 1 : CHUNK, :]
        entry = jnp.exp(cum) * from_start
        ending = jnp.exp(cum_last - cum) * to_end
        entry_wide = widen(entry, mask)
        ending_wide = widen(ending, mask)
        step_wide = widen(step, mask)
        y_grad = yg_ref[...]
        entered = enter_ref[...]
        held = adjoint[...]
        y_entry = y_grad * entry_wide
        out_grad = dbcl_ref[:, STATE:] + mm_three(y_entry, entered)
        out_carry = fold(y_entry * mm_two(st_ref[:, STATE:], entered), mask)
        x_wide = x_ref[...].astype(f32)
        back = ending_wide * mm_two(st_ref[:, :STATE], held)
        act_grad = step_wide * (dxl_ref[...] + back) + wide_ref[0:1, :] * y_grad
        in_grad = dbcl_ref[:, :STATE] + mm_three(x_wide * ending_wide * step_wide, held)
        size_carry = fold(x_wide * back, mask)
        both = jnp.sum(held * entered, axis=0, keepdims=True)
        crossing = fold(jnp.broadcast_to(both, (8, width)), mask)[0:1, :] * entry[CHUNK - 1 : CHUNK, :]
        doc_col = col_ref[:, 3 * groups : 3 * groups + 1]
        doc_row = row_ref[2 * groups : 2 * groups + 1, :]
        row, col = rows_cols()
        same = doc_col == doc_row
        later = (same & (row <= col)).astype(f32)
        earlier = (same & (row > col)).astype(f32)
        decayed = (
            dsl_ref[:, groups:]
            + jnp.dot(later, out_carry, precision=high, preferred_element_type=f32)
            + jnp.dot(earlier, step * size_carry, precision=high, preferred_element_type=f32)
            + crossing
        )
        decay_grad = decayed * inside
        size_grad = dsl_ref[:, :groups] + size_carry
        rate = rate_ref[1:2, :]
        step_grad = (size_grad - rate * decay_grad) * col_ref[:, 3 * groups + 7 :]
        step_grad_ref[...] = step_grad.astype(bf16)
        sum_ref[0:1, step_at : step_at + groups] += jnp.sum(step_grad, axis=0, keepdims=True)
        sum_ref[0:1, step_at + groups : step_at + 2 * groups] -= jnp.sum(
            decay_grad * step * rate, axis=0, keepdims=True
        )
        adjoint[...] = entry_wide[CHUNK - 1 : CHUNK, :] * held + mm_two(stt_ref[STATE:, :], y_entry)

        grad = conv_back_step(
            act_grad, pre_ref[...], value_ref[...].astype(f32), taps_ref, match, next_ref, sum_inner_ref
        )
        grad_ref[...] = grad.astype(bf16)
        grad_state = conv_back_step(
            jnp.concatenate([in_grad, out_grad], axis=1),
            pre_state_ref[...],
            value_state_ref[...].astype(f32),
            taps_state_ref,
            match,
            next_state_ref,
            sum_state_ref,
        )
        grad_state_ref[...] = grad_state.astype(bf16)
        grad_state_t_ref[...] = jnp.transpose(grad_state)

        @pl.when(step_index == 0)
        def _():
            tail_ref[:, :width] = grad[CHUNK - 16 :]
            tail_ref[:, width:] = grad_state[CHUNK - 16 :]


def norm_kernel(count, cols, planes_each, place_ref, gain_ref, wt_ref, ws_ref, ws_t_ref, *refs):
    pieces = refs[: PLANE * count]
    before_refs = refs[PLANE * count : (PLANE + 1) * count]
    out_ref, share_ref, value_ref, raw_ref, raw_row_ref, halo_ref, halo_value_ref = refs[
        (PLANE + 1) * count :
    ]
    place = place_ref[0]
    head = place_ref[1]
    share = pieces[0].shape[1]

    @pl.when(pl.program_id(0) == 0)
    def _():
        wide = [ref[...].astype(f32) for ref in before_refs]
        total = 0.0
        for q in range(count):
            total = total + jnp.sum(wide[q] * wide[q], axis=1, keepdims=True)
        inverse = lax.rsqrt(total / D + eps)
        for q in range(count):
            lanes = pl.ds(pl.multiple_of((head ^ q) * share, 128), share)
            halo_ref[:, lanes] = (wide[q] * inverse * gain_ref[:, lanes]).astype(bf16)
        halo_value_ref[...] = mm(halo_ref[...], wt_ref[...]).astype(bf16)

    for r in range(PLANE):

        @pl.when(pl.program_id(0) == r)
        def _():
            wide = [pieces[r * count + q][...].astype(f32) for q in range(count)]
            total = 0.0
            for q in range(count):
                total = total + jnp.sum(wide[q] * wide[q], axis=1, keepdims=True)
            inverse = lax.rsqrt(total / D + eps)
            for q in range(count):
                lanes = pl.ds(pl.multiple_of((head ^ q) * share, 128), share)
                out_ref[:, lanes] = (wide[q] * inverse * gain_ref[:, lanes]).astype(bf16)
            for t in range(PLANE):

                @pl.when(place == t)
                def _():
                    for z in range(planes_each):
                        share_ref[0, :, z * cols : (z + 1) * cols] = pieces[r * count][
                            :, (z * PLANE + t) * cols : (z * PLANE + t + 1) * cols
                        ]

    normed = out_ref[...]
    value_ref[...] = mm(normed, wt_ref[...]).astype(bf16)
    raw_ref[...] = mm(normed, ws_ref[...])
    raw_row_ref[...] = mm_t(ws_t_ref[...], normed)


def shift_in(value, last, reach, row):
    rolled = pltpu.roll(value, reach, 0)
    top = jnp.where(row < reach, pltpu.roll(last, reach, 0), rolled[:8])
    return jnp.concatenate([top, rolled[8:]], axis=0)


def conv_step(value, last_ref, taps_ref, match):
    row = lax.broadcasted_iota(jnp.int32, (8, value.shape[1]), 0)
    last = last_ref[...]
    pre = taps_ref[4:5, :] + taps_ref[3:4, :] * value
    for k in range(KERNEL - 1):
        moved = shift_in(value, last, KERNEL - 1 - k, row)
        pre = pre + taps_ref[k : k + 1, :] * moved * match[k]
    last_ref[...] = value[value.shape[0] - 8 :]
    return pre


def softplus(a):
    return jnp.maximum(a, 0.0) + jnp.log1p(jnp.exp(-jnp.abs(a)))


def vectors_kernel(
    groups, turn,
    base_ref,
    value_ref,
    halo_ref,
    raw_ref,
    raw_row_ref,
    taps_ref,
    starts_ref,
    starts_t_ref,
    head_row_ref,
    head_col_ref,
    pre_ref,
    act_ref,
    act_t_ref,
    col_ref,
    row_ref,
    decay_ref,
    last_ref,
    total_ref,
):
    chunk = turn

    @pl.when(chunk == 0)
    def _():
        last_ref[...] = halo_ref[...].astype(f32)[8:]
        total_ref[...] = jnp.zeros_like(total_ref)

    base = base_ref[0]
    first = base + chunk * CHUNK

    def doc_of(position):
        return jnp.sum((position >= starts_ref[...]).astype(f32), axis=1, keepdims=True)

    place = first + lax.broadcasted_iota(jnp.int32, (CHUNK, 1), 0)
    corner = jnp.zeros((1, 1), jnp.int32)
    doc = doc_of(place)
    match = [(doc_of(place - (KERNEL - 1) + k) == doc).astype(f32) for k in range(KERNEL - 1)]
    from_start = (doc == doc_of(corner + (first - 1))).astype(f32)
    to_end = (doc == doc_of(corner + (first + CHUNK - 1))).astype(f32)
    whole_start = (doc == doc_of(corner + (base - 1))).astype(f32)
    place_row = first + lax.broadcasted_iota(jnp.int32, (1, CHUNK), 1)
    row_ref[2 * groups : 2 * groups + 1, :] = jnp.sum(
        (place_row >= starts_t_ref[...]).astype(f32), axis=0, keepdims=True
    )

    pre = conv_step(value_ref[...].astype(f32), last_ref, taps_ref, match)
    pre_ref[...] = pre
    act = pre * jax.nn.sigmoid(pre)
    act_ref[...] = act.astype(bf16)
    act_t_ref[...] = jnp.transpose(act).astype(bf16)

    shifted_raw = raw_ref[...] + head_row_ref[0:1, :]
    step = softplus(shifted_raw)
    col_ref[:, 3 * groups + 7 :] = jax.nn.sigmoid(shifted_raw)
    row, col = rows_cols()
    lower = (row >= col).astype(f32)
    cum = jnp.dot(
        lower, -step * head_row_ref[1:2, :], precision=high, preferred_element_type=f32
    )
    whole = cum + total_ref[0:1, :]
    total_ref[...] = jnp.broadcast_to(whole[CHUNK - 1 : CHUNK, :], total_ref.shape)
    entry_whole = jnp.exp(whole) * whole_start
    col_ref[:, :groups] = cum
    col_ref[:, groups : 2 * groups] = step
    col_ref[:, 2 * groups : 3 * groups] = entry_whole
    for n, column in enumerate([doc, from_start, to_end, match[2]] + match):
        col_ref[:, 3 * groups + n : 3 * groups + n + 1] = column
    step_row = softplus(raw_row_ref[:groups, :] + head_col_ref[:, 0:1])
    row_ref[:groups, :] = lax.dot_general(
        -step_row * head_col_ref[:, 1:2],
        lower,
        (((1,), (1,)), ((), ())),
        precision=high,
        preferred_element_type=f32,
    )
    row_ref[groups : 2 * groups, :] = step_row
    decay_ref[...] = widen(
        jnp.broadcast_to(entry_whole[CHUNK - 1 : CHUNK, :], (8, groups)),
        head_mask(groups, decay_ref.shape[1]),
    )


def convolve_kernel(
    groups, turn, value_ref, halo_ref, stt_ref, col_ref, taps_ref, pre_ref, x_ref, state_ref, last_ref
):
    @pl.when(turn == 0)
    def _():
        last_ref[...] = halo_ref[...].astype(f32)[8:]
        state_ref[...] = jnp.zeros_like(state_ref)

    mask = head_mask(groups, x_ref.shape[1])
    match = [col_ref[:, 3 * groups + 4 + k : 3 * groups + 5 + k] for k in range(KERNEL - 1)]
    pre = conv_step(value_ref[...].astype(f32), last_ref, taps_ref, match)
    pre_ref[...] = pre
    x_low = (pre * jax.nn.sigmoid(pre)).astype(bf16)
    x_ref[...] = x_low
    cum = col_ref[:, :groups]
    cum_last = cum[CHUNK - 1 : CHUNK, :]
    from_start = col_ref[CHUNK - 1 : CHUNK, 3 * groups + 1 : 3 * groups + 2]
    to_end = col_ref[:, 3 * groups + 2 : 3 * groups + 3]
    ending = widen(jnp.exp(cum_last - cum) * to_end * col_ref[:, groups : 2 * groups], mask)
    kept = widen(jnp.broadcast_to(jnp.exp(cum_last) * from_start, (8, groups)), mask)
    state_ref[...] = kept[0:1, :] * state_ref[...] + mm_two(
        stt_ref[:STATE, :], x_low.astype(f32) * ending
    )


def weight_kernel(groups, *refs):
    refs = refs[1:]
    out_ref = refs[2 * PLANE]
    for r in range(PLANE):

        @pl.when(pl.program_id(0) == r)
        def _():
            for g in range(groups):
                lanes = slice(g * P_SIZE, (g + 1) * P_SIZE)
                both = [refs[r][:, lanes].astype(f32), refs[PLANE + r][:, lanes].astype(f32)]
                out_ref[:, g, :] = jnp.concatenate(both, axis=1)


def unpack_kernel(groups, state_rows, place_ref, *refs):
    small_refs = refs[:2]
    (
        state_ref,
        taps_ref,
        bias_ref,
        gated_ref,
        state_taps_ref,
        state_bias_ref,
        shift_ref,
        rate_ref,
        skip_ref,
        step_ref,
        total_ref,
    ) = refs[2:]
    head = place_ref[1]
    core = place_ref[0] & 1
    width = groups * P_SIZE
    sums = 8 + groups
    heads = small_refs[0].shape[1]
    state_at = 2 * width
    step_at = state_at + 2 * STATE
    total_ref[...] = jnp.zeros_like(total_ref)
    for side in range(2):
        for near in range(2):

            @pl.when(core == side ^ near)
            def _():
                for y in range(2):
                    for h in range(heads):
                        rows = small_refs[near]
                        state = rows[y, h, :state_rows, :].astype(f32)
                        at = (side * 2 + y) * (STATE // 2) + h * state_rows
                        state_ref[:, at : at + state_rows] = jnp.transpose(state)
                        value = (
                            rows[y, h, state_rows : state_rows + sums, :].astype(f32)
                            + rows[y, h, state_rows + sums :, :].astype(f32)
                        )
                        total_ref[...] += value[:8]
                        inner = y * 2 + side
                        for g in range(groups):
                            number = (inner * groups + g) * heads + h
                            here = slice(number * P_SIZE, (number + 1) * P_SIZE)
                            lanes = slice(g * P_SIZE, (g + 1) * P_SIZE)
                            taps_ref[:, here] = value[:KERNEL, lanes]
                            bias_ref[:, here] = value[KERNEL : KERNEL + 1, lanes]
                            lanes = slice(width + g * P_SIZE, width + (g + 1) * P_SIZE)
                            gated_ref[:, here] = value[0:1, lanes]
                            skip_ref[:, number : number + 1] = jnp.sum(
                                value[1:2, lanes], axis=1, keepdims=True
                            )
                            lane = step_at + g
                            shift_ref[:, number : number + 1] = value[0:1, lane : lane + 1]
                            lane = step_at + groups + g
                            rate_ref[:, number : number + 1] = value[0:1, lane : lane + 1]

                        @pl.when(head == h)
                        def _():
                            step_ref[inner * groups : (inner + 1) * groups, :] = value[8:]

    state_taps_ref[...] = total_ref[:KERNEL, state_at:step_at]
    state_bias_ref[...] = total_ref[KERNEL : KERNEL + 1, state_at:step_at]


def normed_back_kernel(
    place_ref,
    z_ref,
    inner_ref,
    step_ref,
    state_ref,
    normed_ref,
    wg_ref,
    wi_ref,
    ws_ref,
    wt_ref,
    own_ref,
    across_ref,
    core_ref,
    gain_ref,
    total_ref,
):
    total = (
        mm_t(z_ref[...], wg_ref[...])
        + mm_t(inner_ref[...], wi_ref[...])
        + mm_t(step_ref[...], ws_ref[...])
        + mm_t(state_ref[...], wt_ref[...])
    )
    total_ref[...] = total
    gain = jnp.sum(total * normed_ref[...].astype(f32), axis=0, keepdims=True)
    gain_ref[...] = jnp.broadcast_to(gain, gain_ref.shape)
    rows = own_ref.shape[0]
    place = place_ref[0]

    def block(r):
        return total_ref[pl.ds(pl.multiple_of((place ^ r) * rows, rows), rows), :]

    own_ref[...] = block(0)
    core_ref[0] = block(1).astype(bf16)
    across_ref[...] = block(2)
    core_ref[1] = block(3).astype(bf16)


def level_of(place, half):
    return jnp.where(place == 0, 3 - half, jnp.where(place == 1, 1, 0))


def split_kernel(count, cols, place_ref, whole_ref, *out_refs):
    place = place_ref[0]
    for r in range(PLANE):
        for t in range(PLANE):

            @pl.when(place == t ^ r)
            def _():
                for z in range(count):
                    out_refs[r][0, :, z * cols : (z + 1) * cols] = whole_ref[
                        0, :, (z * PLANE + t) * cols : (z * PLANE + t + 1) * cols
                    ]


def join_kernel(count, cols, place_ref, *refs):
    place = place_ref[0]
    out_ref = refs[PLANE]
    for r in range(PLANE):
        for t in range(PLANE):

            @pl.when(place == t ^ r)
            def _():
                for z in range(count):
                    out_ref[0, :, (z * PLANE + t) * cols : (z * PLANE + t + 1) * cols] = refs[r][
                        0, :, z * cols : (z + 1) * cols
                    ]


def pick_part(near_refs, first_refs, second_refs, cot_ref):
    step = pl.program_id(0) % PLANE

    @pl.when(step < 2)
    def _():
        for q, near in enumerate(near_refs):
            cot_ref[q] = near[0]

    @pl.when(step == 2)
    def _():
        for q, first in enumerate(first_refs):
            cot_ref[q] = first[...]

    @pl.when(step == 3)
    def _():
        for q, second in enumerate(second_refs):
            cot_ref[q] = second[...]


def weight_rows_of(weight_ref, count, head, owner, span):
    each = weight_ref.shape[0] // count
    return jnp.concatenate(
        [weight_ref[(head ^ q) * each + z, owner, span, :] for q in range(count) for z in range(each)],
        axis=1,
    )


def scale_kernel(sum_ref, row_ref, col_ref):
    level = lax.broadcasted_iota(jnp.int32, sum_ref.shape, 0)
    width = jnp.zeros(sum_ref.shape, f32) + 1.0
    for m in range(4):
        width = jnp.where(level == m, float(INNER >> m), width)
    scale = lax.rsqrt(sum_ref[...] / width + eps)
    row_ref[...] = scale
    col_ref[...] = jnp.transpose(scale)


def out_back_kernel(count, place_ref, scale_ref, weight_ref, *refs):
    part_refs = refs[3 * count : 3 * count + PLANE]
    sum_ref, cot_ref, up_ref, low_ref, part_ref, sems = refs[3 * count + PLANE :]
    step = pl.program_id(0)
    place = place_ref[0]
    half = cot_ref.shape[3]
    rows = weight_ref.shape[2] // 2
    tokens = sum_ref.shape[1]

    @pl.when(step < PLANE)
    def _():
        pick_part(refs[:count], refs[count : 2 * count], refs[2 * count : 3 * count], cot_ref)
        here = pl.ds(pl.multiple_of((step ^ place) * tokens, tokens), tokens)
        for q in range(count):
            lanes = slice(q * half, (q + 1) * half)
            total = None
            for m in range(4):
                grad = (scale_ref[:, m : m + 1] * cot_ref[q, m].astype(f32)).astype(bf16)
                total = grad.astype(f32) if m == 0 else total + grad.astype(f32)
                upper, lower = split_two(total)
                sum_ref[m, :, lanes] = upper
                up_ref[m, here, lanes] = upper
                if m:
                    low_ref[m - 1, here, lanes] = lower

    for r in range(PLANE):

        @pl.when(step == PLANE + r)
        def _():
            owner = place ^ r
            for side in range(2):
                level = level_of(owner, side)
                span = slice(side * rows, (side + 1) * rows)
                weight = weight_rows_of(weight_ref, count, place_ref[1], owner, span)
                part_ref[r, :, span] = mm_t(up_ref[level], weight)

                @pl.when(owner < 2)
                def _():
                    part_ref[r, :, span] += mm_t(low_ref[level - 1], weight)

            pltpu.make_async_copy(part_ref.at[r], part_refs[r], sems.at[r]).start()

    @pl.when(step == 2 * PLANE - 1)
    def _():
        for r in range(PLANE):
            pltpu.make_async_copy(part_ref.at[r], part_refs[r], sems.at[r]).wait()


def product_kernel(count, place_ref, weight_ref, *refs):
    u_refs = refs[:PLANE]
    cot_refs = refs[PLANE : PLANE + 3 * count]
    refs = refs[PLANE + 3 * count :]
    dot_ref, own_ref = refs[:2]
    send_refs = refs[2 : count + 1]
    block_ref, cot_ref = refs[count + 1 :]
    pick_part(cot_refs[:count], cot_refs[count : 2 * count], cot_refs[2 * count :], cot_ref)
    place = place_ref[0]
    half = cot_ref.shape[3]
    rows = weight_ref.shape[2] // 2
    block_ref[...] = jnp.zeros_like(block_ref)
    for r in range(PLANE):
        owner = place ^ r
        for side in range(2):
            span = slice(side * rows, (side + 1) * rows)
            weight = weight_rows_of(weight_ref, count, place_ref[1], owner, span)
            block_ref[level_of(owner, side)] += mm(u_refs[r][:, span], weight)
    running = None
    ones = jnp.ones((8, half), bf16)
    dot_ref[4:8, :] = jnp.zeros((4, dot_ref.shape[1]), f32)
    for m in (3, 2, 1, 0):
        running = block_ref[m] if running is None else running + block_ref[m]
        dots = 0.0
        for q in range(count):
            part = running[:, q * half : (q + 1) * half]
            dots = dots + cot_ref[q, m].astype(f32) * part
            if q == 0:
                own_ref[0, m] = part
            else:
                send_refs[q - 1][0, m] = part.astype(bf16)
        upper, lower = split_two(dots)
        dot_ref[m : m + 1, :] = (mm_t(ones, upper) + mm_t(ones, lower))[0:1, :]


def mix_kernel(count, scale_ref, tok_ref, own_ref, *refs):
    got_refs = refs[: count - 1]
    out_refs = refs[count - 1 :]
    for r in range(PLANE):

        @pl.when(pl.program_id(0) == r)
        def _():
            for m in range(4):
                total = own_ref[0, m]
                for got in got_refs:
                    total = total + got[0, m].astype(f32)
                out_refs[r][m] = (
                    tok_ref[0].astype(f32) + scale_ref[:, m : m + 1] * total
                ).astype(bf16)


def out_weight_kernel(count, planes_each, cols, place_ref, sum_ref, *refs):
    u_refs = refs[:PLANE]
    out_ref = refs[PLANE]
    place = place_ref[0]
    head = place_ref[1]
    rows = u_refs[0].shape[1] // 2
    for r in range(PLANE):

        @pl.when(pl.program_id(0) == r)
        def _():
            owner = place ^ r
            for side in range(2):
                span = slice(side * rows, (side + 1) * rows)
                grad = t_mm(u_refs[r][:, span], sum_ref[level_of(owner, side)])
                for q in range(count):
                    for z in range(planes_each):
                        lanes = slice((q * planes_each + z) * cols, (q * planes_each + z + 1) * cols)
                        out_ref[(head ^ q) * planes_each + z, span, :] = grad[:, lanes].astype(bf16)


def per_chunk(width):
    return "rows", pl.BlockSpec((SUB * CHUNK, width), lambda c, *rest: (c, 0))


def across(height):
    return "cols", pl.BlockSpec((height, SUB * CHUNK), lambda c, *rest: (0, c))


def fixed(*shape):
    return "fixed", pl.BlockSpec(shape, lambda c, *rest: (0,) * len(shape))


def spread(kernel, specs, reverse=False, ahead=0):
    def view(kind, ref, sub):
        part = pl.ds(sub * CHUNK, CHUNK)
        if kind == "rows":
            return ref.at[part, :]
        return ref.at[:, part] if kind == "cols" else ref

    def run(*refs):
        first, refs = refs[:ahead], refs[ahead:]
        for n in range(SUB):
            sub = SUB - 1 - n if reverse else n
            views = [view(kind, ref, sub) for (kind, _), ref in zip(specs, refs)]
            kernel(pl.program_id(0) * SUB + n, *first, *views, *refs[len(specs) :])

    return run


def shaped(shape, kind=f32):
    return jax.ShapeDtypeStruct(shape, kind)


def contract(left_side, right_side, left_dim, right_dim):
    return lax.dot_general(
        left_side,
        right_side,
        (((left_dim,), (right_dim,)), ((), ())),
        preferred_element_type=f32,
    )


def own_heads(values, heads):
    shape = values.shape[:-1]
    shaped_values = values.reshape(shape + (PLANE, -1, lax.axis_size("h"), heads))
    mine = take(shaped_values, lax.axis_index("i"), len(shape))
    mine = take(mine, lax.axis_index("h"), len(shape) + 1)
    return mine.reshape(shape + (-1,))


def shards(
    tokens,
    cotangent,
    doc_lengths,
    input_gain,
    input_weight,
    step_weight,
    state_weight,
    conv_inner,
    conv_inner_bias,
    conv_state,
    conv_state_bias,
    step_bias,
    decay_log,
    skip_gain,
    gated_gain,
    output_weight,
):
    planes = lax.axis_size("o")
    head_count = lax.axis_size("h")
    plane = lax.axis_index("o")
    inner = lax.axis_index("i")
    head = lax.axis_index("h")
    here = jnp.stack([inner, head]).astype(jnp.int32)
    tok_rows, share = tokens.shape
    span = tok_rows * PLANE
    steps = span // CHUNK
    weight_rows, groups_all = input_weight.shape[:2]
    groups = groups_all // PLANE
    width = groups * P_SIZE
    wide_rows = groups_all * P_SIZE
    cols = output_weight.shape[2]
    own_planes = planes // head_count
    half = own_planes * cols
    pad = KERNEL - 1
    halo = 16
    fence = lax.optimization_barrier

    def token_block(*rest):
        return pl.BlockSpec((tok_rows,) + rest, lambda r, place: (r ^ place[0],) + (0,) * len(rest))

    def part_block(*rest):
        return pl.BlockSpec((1,) + rest, lambda r, place: (r,) + (0,) * len(rest))

    def whole_block(*shape):
        return pl.BlockSpec(shape, lambda r, place: (0,) * len(shape))

    def placed_call(kernel, in_specs, out_specs, out_shape, scratch, name, turns=PLANE):
        return pl.pallas_call(
            kernel,
            grid_spec=pltpu.PrefetchScalarGridSpec(
                num_scalar_prefetch=1,
                grid=(turns,),
                in_specs=in_specs,
                out_specs=out_specs,
                scratch_shapes=scratch,
            ),
            out_shape=out_shape,
            compiler_params=PARAMS,
            name=name,
        )

    def placed_call_once(kernel, out_shape, scratch, name):
        return pl.pallas_call(
            kernel,
            grid_spec=pltpu.PrefetchScalarGridSpec(
                num_scalar_prefetch=1,
                grid=(1,),
                in_specs=[pl.BlockSpec(memory_space=pltpu.VMEM)] * 2,
                out_specs=[pl.BlockSpec(memory_space=pltpu.VMEM)] * len(out_shape),
                scratch_shapes=scratch,
            ),
            out_shape=out_shape,
            compiler_params=PARAMS,
            name=name,
        )

    def unplaced(kernel):
        return lambda place_ref, *refs: kernel(*refs)

    def chunk_call(kernel, in_specs, out_specs, out_shape, scratch, name, ahead=0):
        return pl.pallas_call(
            spread(kernel, in_specs + out_specs, ahead=ahead),
            grid_spec=pltpu.PrefetchScalarGridSpec(
                num_scalar_prefetch=ahead,
                grid=(steps // SUB,),
                in_specs=[spec for _, spec in in_specs],
                out_specs=[spec for _, spec in out_specs],
                scratch_shapes=scratch,
            ),
            out_shape=out_shape,
            compiler_params=PARAMS,
            name=name,
        )

    pieces = input_weight.reshape(weight_rows, PLANE, groups, 2, P_SIZE)

    def head_pieces(side):
        return jnp.transpose(pieces[:, :, :, side, :], (1, 0, 2, 3)).reshape(
            PLANE, weight_rows, width
        )

    inner_pieces = exchange_inner(head_pieces(1))
    near = [swap(tokens, "h", q) if q else tokens for q in range(head_count)]
    far = swap(tokens, "i", 2)
    step_planes = stack_planes(step_weight.reshape(weight_rows, groups_all))
    before = shifted(tokens[tok_rows - halo :], "o", 1)
    before = jnp.where(inner == PLANE - 1, before, jnp.zeros_like(before))
    near, far, inner_pieces, step_planes, before = fence(
        (near, far, inner_pieces, step_planes, before)
    )
    weight_inner = lax.all_gather(
        inner_pieces.reshape(PLANE * weight_rows, width), "o", axis=0, tiled=True
    )
    sibling = [swap(b, "i", 1) for b in near]
    before = before + swap(before, "i", 2)
    before = before + swap(before, "i", 1)
    before = [swap(before, "h", q) if q else before for q in range(head_count)]
    weight_step = jnp.transpose(stack_inner(step_planes), (1, 0, 2, 3)).reshape(D, groups_all)
    weight_step = lax.dynamic_slice_in_dim(weight_step, inner * groups, groups, 1)
    weight_step_t = jnp.pad(jnp.transpose(weight_step), ((0, 16 - groups), (0, 0)))
    far = [swap(far, "h", q) if q else far for q in range(head_count)]
    gate_pieces, before, far, sibling, weight_step, weight_step_t = fence(
        (
            exchange_inner(fence((head_pieces(0), near))[0]),
            before,
            far,
            sibling,
            weight_step,
            weight_step_t,
        )
    )
    weight_gate = lax.all_gather(
        gate_pieces.reshape(PLANE * weight_rows, width), "o", axis=0, tiled=True
    )
    blocks = [near, sibling, far, [swap(b, "i", 1) for b in far]]
    normed, tok_share, state_value, step_raw, step_row, normed_halo, state_halo = placed_call(
        partial(norm_kernel, head_count, cols, own_planes),
        [
            whole_block(1, D),
            whole_block(D, 2 * STATE),
            whole_block(D, groups),
            whole_block(16, D),
        ]
        + [whole_block(tok_rows, share)] * (PLANE * head_count)
        + [whole_block(halo, share)] * head_count,
        [
            token_block(D),
            part_block(tok_rows, half),
            token_block(2 * STATE),
            token_block(groups),
            pl.BlockSpec((16, tok_rows), lambda r, place: (0, r ^ place[0])),
            whole_block(halo, D),
            whole_block(halo, 2 * STATE),
        ],
        [
            shaped((span, D), bf16),
            shaped((PLANE, tok_rows, half), bf16),
            shaped((span, 2 * STATE), bf16),
            shaped((span, groups)),
            shaped((16, span)),
            shaped((halo, D), bf16),
            shaped((halo, 2 * STATE), bf16),
        ],
        [],
        "norm",
    )(
        here,
        input_gain[None],
        state_weight,
        weight_step,
        weight_step_t,
        *[b for row in blocks for b in row],
        *before,
    )

    weight_out = lax.all_gather(output_weight.reshape(wide_rows, cols), "o")
    weight_out = weight_out.reshape(planes, PLANE, width, cols)

    cotangent_later, normed = fence((cotangent, normed))
    largest = jnp.max(jnp.abs(cotangent_later)).astype(f32)
    cot_parts = pl.pallas_call(
        partial(split_kernel, own_planes, cols),
        grid_spec=pltpu.PrefetchScalarGridSpec(
            num_scalar_prefetch=1,
            grid=(4,),
            in_specs=[pl.BlockSpec((1, tok_rows, share), lambda m, place: (m, 0, 0))],
            out_specs=[pl.BlockSpec((1, tok_rows, half), lambda m, place: (m, 0, 0))] * PLANE,
        ),
        out_shape=[shaped((4, tok_rows, half), bf16)] * PLANE,
        compiler_params=PARAMS,
        name="split",
    )(here, cotangent_later)
    cot_near = jnp.stack([cot_parts[0], swap(cot_parts[1], "i", 1)])
    cot_sent = [swap(cot_parts[2], "i", 2), swap(cot_parts[3], "i", 3)]
    cot_near = [swap(cot_near, "h", q) if q else cot_near for q in range(head_count)]

    starts = (jnp.cumsum(doc_lengths) - doc_lengths).astype(jnp.int32)
    base = (plane * span).astype(jnp.int32).reshape(1)

    def taps_of(kernel, bias):
        return jnp.concatenate([kernel, bias[None], jnp.zeros((3, bias.shape[0]), f32)], axis=0)

    taps_inner = taps_of(own_heads(conv_inner, P_SIZE), own_heads(conv_inner_bias, P_SIZE))
    taps_state = taps_of(conv_state, conv_state_bias)
    gain_wide = own_heads(gated_gain, P_SIZE)
    step_shift = own_heads(step_bias, 1)
    rate_log = own_heads(decay_log, 1)
    skip_wide = jnp.repeat(own_heads(skip_gain, 1), P_SIZE)
    wide = jnp.concatenate([skip_wide[None], gain_wide[None], jnp.zeros((6, width), f32)], axis=0)
    group_number = inner * groups + jnp.arange(groups)
    level_limit = jnp.array([groups_all >> m for m in range(4)] + [0] * 4)
    level_mask = jnp.repeat(
        (group_number[None, :] < level_limit[:, None]).astype(bf16), P_SIZE, axis=1
    )

    rate = jnp.exp(rate_log)
    head_row = jnp.concatenate([step_shift[None], rate[None], jnp.zeros((6, groups), f32)], axis=0)
    head_col = jnp.stack([step_shift, rate], axis=1)
    col_width = 4 * groups + 7
    row_height = 2 * groups + 1

    pre_state, state_act, state_act_t, col_pack, row_pack, decay_wide = chunk_call(
        partial(vectors_kernel, groups),
        [
            per_chunk(2 * STATE),
            fixed(halo, 2 * STATE),
            per_chunk(groups),
            across(16),
            fixed(8, 2 * STATE),
            fixed(1, starts.shape[0]),
            fixed(starts.shape[0], 1),
            fixed(8, groups),
            fixed(groups, 2),
        ],
        [
            per_chunk(2 * STATE),
            per_chunk(2 * STATE),
            across(2 * STATE),
            per_chunk(col_width),
            across(row_height),
            fixed(8, width),
        ],
        [
            shaped((span, 2 * STATE)),
            shaped((span, 2 * STATE), bf16),
            shaped((2 * STATE, span), bf16),
            shaped((span, col_width)),
            shaped((row_height, span)),
            shaped((8, width)),
        ],
        [pltpu.VMEM((8, 2 * STATE), f32), pltpu.VMEM((8, groups), f32)],
        "vectors",
        ahead=1,
    )(
        base,
        state_value,
        state_halo,
        step_raw,
        step_row,
        taps_state,
        starts[None, :],
        starts[:, None],
        head_row,
        head_col,
    )
    decay_whole = decay_wide[0:1]

    wide_out = shaped((span, width))
    value = jnp.dot(normed, weight_inner, preferred_element_type=f32).astype(bf16)
    inner_halo = jnp.dot(normed_halo, weight_inner, preferred_element_type=f32).astype(bf16)
    pre_inner, x, own_state = chunk_call(
        partial(convolve_kernel, groups),
        [
            per_chunk(width),
            fixed(halo, width),
            across(2 * STATE),
            per_chunk(col_width),
            fixed(8, width),
        ],
        [per_chunk(width), per_chunk(width), fixed(STATE, width)],
        [wide_out, shaped((span, width), bf16), shaped((STATE, width))],
        [pltpu.VMEM((8, width), f32)],
        "convolve",
    )(value, inner_halo, state_act_t, col_pack, taps_inner)
    x, cot_near, cot_sent = fence((x, cot_near, cot_sent))
    cot_first = [swap(cot_sent[0], "h", q) if q else cot_sent[0] for q in range(head_count)]
    cot_second = [swap(cot_sent[1], "h", q) if q else cot_sent[1] for q in range(head_count)]
    incoming = chain(own_state, decay_whole, 1)
    (y_local,) = chunk_call(
        partial(within_kernel, groups),
        [per_chunk(width), per_chunk(2 * STATE), per_chunk(col_width), across(row_height)],
        [per_chunk(width)],
        [wide_out],
        [],
        "within",
    )(x, state_act, col_pack, row_pack)
    y_local, cot_first = fence((y_local, cot_first))
    gate_z = jnp.dot(normed, weight_gate, preferred_element_type=f32).astype(bf16)
    v, scaled_u, squares, entering = chunk_call(
        partial(carry_kernel, groups),
        [
            per_chunk(width),
            per_chunk(2 * STATE),
            across(2 * STATE),
            per_chunk(col_width),
            per_chunk(width),
            per_chunk(width),
            fixed(STATE, width),
            fixed(8, width),
            fixed(8, width),
        ],
        [per_chunk(width), per_chunk(width), across(8), per_chunk(width)],
        [
            wide_out,
            shaped((span, width), bf16),
            shaped((8, span)),
            shaped((steps * STATE, width)),
        ],
        [pltpu.VMEM((STATE, width), f32)],
        "carry",
    )(x, state_act, state_act_t, col_pack, y_local, gate_z, incoming, wide, level_mask)

    scaled_u, cot_second = fence((scaled_u, cot_second))
    cots = list(cot_near) + list(cot_first) + list(cot_second)

    squares = jnp.concatenate(
        [squares[:4], jnp.full((1, span), largest, f32), jnp.zeros((3, span), f32)], axis=0
    )
    squares = add_inner(add_all(add_inner(squares, 2), ("h",)), 1)
    scaled_u, squares = fence((scaled_u, squares))
    u_far = swap(scaled_u, "i", 2)
    u_parts = [scaled_u, swap(scaled_u, "i", 1), u_far, swap(u_far, "i", 1)]
    scales_row, scales = pl.pallas_call(
        scale_kernel,
        out_shape=[shaped((8, span)), shaped((span, 8))],
        compiler_params=pltpu.CompilerParams(vmem_limit_bytes=8 * 1024 * 1024),
        name="scales",
    )(squares)
    u_bound = squares[4, 0] * jnp.sum(jnp.max(scales_row[:4], axis=1))
    u_bound = u_bound * (0.1875 * 2.0 * head_count * half)
    scales, u_parts = fence((scales, u_parts))
    cot_block = part_block(4, tok_rows, half)
    weight_block = whole_block(planes, PLANE, width, cols)
    cot_near_block = pl.BlockSpec(
        (1, 4, tok_rows, half), lambda r, place: (jnp.minimum(r, 1), 0, 0, 0)
    )
    first_turns = pl.BlockSpec((tok_rows, 8), lambda r, place: (jnp.minimum(r, PLANE - 1) ^ place[0], 0))
    cot_blocks = [cot_near_block] * head_count
    cot_blocks += [whole_block(4, tok_rows, half)] * (2 * head_count)
    cot_scratch = pltpu.VMEM((head_count, 4, tok_rows, half), bf16)
    cot_shape = shaped((PLANE, 4, tok_rows, half), bf16)
    *parts, sums = placed_call(
        partial(out_back_kernel, head_count),
        [first_turns, weight_block] + cot_blocks,
        [pl.BlockSpec(memory_space=pl.ANY)] * PLANE
        + [
            pl.BlockSpec(
                (4, tok_rows, head_count * half),
                lambda r, place: (0, jnp.minimum(r, PLANE - 1) ^ place[0], 0),
            ),
        ],
        [wide_out] * PLANE + [shaped((4, span, head_count * half), bf16)],
        [
            cot_scratch,
            pltpu.VMEM((4, span, head_count * half), bf16),
            pltpu.VMEM((3, span, head_count * half), bf16),
            pltpu.VMEM((PLANE, span, width), f32),
            pltpu.SemaphoreType.DMA((PLANE,)),
        ],
        "out_back",
        2 * PLANE,
    )(here, scales, weight_out, *cots)
    u_scale = jnp.exp2(jnp.ceil(jnp.log2(jnp.clip(u_bound, 1e-30, 1e30))))
    out_grad = placed_call(
        partial(out_weight_kernel, head_count, own_planes, cols),
        [whole_block(4, span, head_count * half)] + [whole_block(span, width)] * PLANE,
        pl.BlockSpec((planes, width, cols), lambda r, place: (0, r ^ place[0], 0)),
        shaped((planes, wide_rows, cols), bf16),
        [],
        "out_weight_back",
    )(here, sums, *u_parts)

    parts_far = swap(parts[3], "i", 1)
    parts_far, out_grad_sent = fence((parts_far, out_grad))
    out_grad = lax.psum_scatter(out_grad_sent, "o", scatter_dimension=0, tiled=False)
    sent_across = ((parts[2] + parts_far) * (HALF_TOP / u_scale)).astype(jnp.float16)
    u_parts, sent_across = fence((u_parts, sent_across))
    got_across = swap(sent_across, "i", 2).astype(f32) * (u_scale / HALF_TOP)
    u_grad = parts[0] + swap(parts[1], "i", 1) + got_across
    dots, own_product, *sent_products = placed_call(
        partial(product_kernel, head_count),
        [weight_block]
        + [token_block(width)] * PLANE
        + cot_blocks,
        [pl.BlockSpec((8, tok_rows), lambda r, place: (0, r ^ place[0]))]
        + [cot_block] * head_count,
        [shaped((8, span)), shaped(cot_shape.shape)] + [cot_shape] * (head_count - 1),
        [pltpu.VMEM((4, tok_rows, head_count * half), f32), cot_scratch],
        "products",
    )(here, weight_out, *u_parts, *cots)
    dots = add_all(add_inner(dots, 1), ("h",))
    sent_products, dots = fence((sent_products, dots))
    dots = add_inner(dots, 2)
    y_grad, z_grad, wide_sums, leaving = chunk_call(
        partial(gate_back_kernel, groups),
        [
            per_chunk(width),
            per_chunk(width),
            per_chunk(width),
            per_chunk(width),
            across(2 * STATE),
            per_chunk(col_width),
            across(8),
            across(8),
            fixed(8, width),
            fixed(8, width),
        ],
        [per_chunk(width), per_chunk(width), fixed(8, width), fixed(STATE, width)],
        [wide_out, shaped((span, width), bf16), shaped((8, width)), shaped((STATE, width))],
        [],
        "gate_back",
    )(u_grad, v, gate_z, x, state_act_t, col_pack, dots, scales_row, wide, level_mask)
    lam = chain(leaving, decay_whole, -1)

    dx_local, dbc_local, ds_local = chunk_call(
        partial(within_back_kernel, groups),
        [
            per_chunk(width),
            per_chunk(2 * STATE),
            per_chunk(col_width),
            across(row_height),
            per_chunk(width),
        ],
        [per_chunk(width), per_chunk(2 * STATE), per_chunk(2 * groups)],
        [wide_out, shaped((span, 2 * STATE)), shaped((span, 2 * groups))],
        [],
        "within_back",
    )(x, state_act, col_pack, row_pack, y_grad)
    gate_z_grad, dx_local = fence((z_grad, dx_local))
    gate_part = contract(normed, gate_z_grad, 0, 0).astype(bf16)
    got_products = [swap(sent_products[q - 1], "h", q) for q in range(1, head_count)]
    lam, got_products, gate_part, out_grad = fence((lam, got_products, gate_part, out_grad))
    mixed_parts = placed_call(
        unplaced(partial(mix_kernel, head_count)),
        [token_block(8), part_block(tok_rows, half)] + [cot_block] * head_count,
        [whole_block(4, tok_rows, half)] * PLANE,
        [shaped((4, tok_rows, half), bf16)] * PLANE,
        [],
        "mix",
    )(here, scales, tok_share, own_product, *got_products)
    gate_grad = lax.psum_scatter(gate_part, "o", scatter_dimension=0, tiled=True)
    lam, mixed_parts = fence((lam, mixed_parts))
    mixed_parts = [mixed_parts[0]] + [swap(mixed_parts[r], "i", r) for r in range(1, PLANE)]
    turns = steps // SUB

    def back_rows(shape):
        return "rows", pl.BlockSpec(
            (SUB * CHUNK, shape), lambda c: (jnp.maximum(turns - 1 - c, 0), 0)
        )

    def back_cols(shape):
        return "cols", pl.BlockSpec(
            (shape, SUB * CHUNK), lambda c: (0, jnp.maximum(turns - 1 - c, 0))
        )

    back_wide = back_rows(width)
    back_state = back_rows(2 * STATE)
    both = width + 2 * STATE
    back_in = [
        back_wide,
        back_state,
        back_cols(2 * STATE),
        back_rows(col_width),
        back_cols(row_height),
        back_wide,
        back_wide,
        back_state,
        back_rows(2 * groups),
        back_wide,
        fixed(STATE, width),
        fixed(8, width),
        back_wide,
        back_wide,
        fixed(halo, width),
        fixed(8, width),
        back_state,
        back_state,
        fixed(halo, 2 * STATE),
        fixed(8, 2 * STATE),
        fixed(8, groups),
        fixed(8, width),
    ]
    back_out = [
        back_wide,
        fixed(16, both),
        fixed(8, both),
        fixed(8, D),
        back_state,
        ("cols", pl.BlockSpec((2 * STATE, SUB * CHUNK), lambda c: (0, turns - c))),
        back_rows(groups),
    ]
    inner_grad, tails, edges, narrow, state_grad, state_sum, step_grad_low = pl.pallas_call(
        spread(
            partial(carry_back_kernel, groups, steps), back_in + back_out, reverse=True
        ),
        grid=(turns + 1,),
        in_specs=[spec for _, spec in back_in],
        out_specs=[spec for _, spec in back_out],
        out_shape=[
            shaped((span, width), bf16),
            shaped((16, both)),
            shaped((8, both)),
            shaped((8, D)),
            shaped((span, 2 * STATE), bf16),
            shaped((2 * STATE, SUB * CHUNK + span)),
            shaped((span, groups), bf16),
        ],
        scratch_shapes=[
            pltpu.VMEM((STATE, width), f32),
            pltpu.VMEM((24, width), f32),
            pltpu.VMEM((24, 2 * STATE), f32),
        ],
        compiler_params=PARAMS,
        name="carry_back",
    )(
        x,
        state_act,
        state_act_t,
        col_pack,
        row_pack,
        y_grad,
        dx_local,
        dbc_local,
        ds_local,
        entering,
        lam,
        wide,
        pre_inner,
        value,
        inner_halo,
        taps_inner,
        pre_state,
        state_value,
        state_halo,
        taps_state,
        head_row,
        wide_sums,
    )
    edges, state_sum, narrow, mixed_parts = fence((edges, state_sum, narrow, mixed_parts))
    edges = shifted(edges, "o", -1)

    def state_half(values, axis, bit):
        halves = values.reshape((2, values.shape[0] // 2, values.shape[1]))
        side = jnp.where((lax.axis_index(axis) & bit) != 0, 1, 0)
        return take(halves, side) + swap(take(halves, 1 - side), axis, bit)

    for axis, bit in (("i", 1), ("i", 2)) + tuple(("h", b) for b in reversed(bits_of("h"))):
        state_sum = state_half(state_sum, axis, bit)
    edges, state_sum, gate_grad = fence((edges, state_sum, gate_grad))
    state_rows = state_sum.shape[0]
    state_low = state_sum.astype(bf16)
    edge_at = (SUB - 1) * CHUNK
    state_part = jnp.dot(
        state_low[:, SUB * CHUNK :], normed, preferred_element_type=f32
    ) + jnp.dot(
        state_low[:, edge_at : edge_at + 8], normed_halo[8:], preferred_element_type=f32
    )
    step_part = contract(step_grad_low, normed, 0, 0)
    sum_rows = 8 + groups

    def packed_rows(sums, state):
        return jnp.concatenate([state.astype(bf16), *split_rows(sums)], axis=0)

    def unpacked_rows(rows):
        upper = rows[..., state_rows : state_rows + sum_rows, :].astype(f32)
        return upper + rows[..., state_rows + sum_rows :, :].astype(f32), rows[..., :state_rows, :]

    def plus_plane(sums, state, bit):
        got, got_state = unpacked_rows(swap(packed_rows(sums, state), "o", bit))
        return sums + got, state + got_state.astype(f32)

    small = jnp.concatenate([narrow, step_part], axis=0)
    tails = (tails + jnp.pad(edges, ((8, 0), (0, 0)))).astype(bf16)
    inner_grad = lax.dynamic_update_slice_in_dim(inner_grad, tails[:, :width], span - 16, 0)
    state_grad = lax.dynamic_update_slice_in_dim(state_grad, tails[:, width:], span - 16, 0)

    small, state_part = plus_plane(small, state_part, 1)
    part = D // 8

    def columns_of(rows):
        return pl.BlockSpec((rows, part), lambda c, place: (0, c))

    def rows_of(width):
        return pl.BlockSpec((part, width), lambda c, place: (c, 0))

    normed_own, normed_across, normed_core, gain_part = pl.pallas_call(
        normed_back_kernel,
        grid_spec=pltpu.PrefetchScalarGridSpec(
            num_scalar_prefetch=1,
            grid=(8,),
            in_specs=[
                whole_block(span, width),
                whole_block(span, width),
                whole_block(span, groups),
                whole_block(span, 2 * STATE),
                columns_of(span),
                rows_of(width),
                rows_of(width),
                rows_of(groups),
                rows_of(2 * STATE),
            ],
            out_specs=[
                columns_of(tok_rows),
                columns_of(tok_rows),
                pl.BlockSpec((2, tok_rows, part), lambda c, place: (0, 0, c)),
                columns_of(8),
            ],
            scratch_shapes=[pltpu.VMEM((span, part), f32)],
        ),
        out_shape=[
            shaped((tok_rows, D)),
            shaped((tok_rows, D)),
            shaped((2, tok_rows, D), bf16),
            shaped((8, D)),
        ],
        compiler_params=PARAMS,
        name="normed_back",
    )(
        here,
        z_grad,
        inner_grad,
        step_grad_low,
        state_grad,
        normed,
        weight_gate,
        weight_inner,
        weight_step,
        state_weight,
    )
    inner_grad, normed_core, small, state_part = fence((inner_grad, normed_core, small, state_part))

    inner_part = contract(normed, inner_grad, 0, 0).astype(bf16)
    got_core = swap(normed_core, "i", 1)
    gain_sum = add_inner(gain_part[0].reshape(8, -1), 1)
    for bit in bits_of("o")[1:]:
        small, state_part = plus_plane(small, state_part, bit)
    gate_back = scattered_inner(gate_grad.reshape(PLANE, weight_rows, width))
    inner_part, got_core, gain_sum = fence((inner_part, got_core, gain_sum))
    got_core, small, state_part, gate_back = fence((got_core, small, state_part, gate_back))
    inner_part = lax.psum_scatter(inner_part, "o", scatter_dimension=0, tiled=True)

    got_across = swap((normed_across + got_core[1].astype(f32)).astype(bf16), "i", 2)
    small = packed_rows(small, state_part)
    shape = small.shape
    for bit in bits_of("h"):
        small = stack_over(small, "h", bit, 0)
        small = small.reshape((-1,) + shape)
    gain_sum = add_all(gain_sum, ("h",))
    output_weight_grad = out_grad.astype(f32).reshape(groups_all, P_SIZE, cols)
    mixed = placed_call(
        partial(join_kernel, own_planes, cols),
        [part_block(tok_rows, half)] * PLANE,
        part_block(tok_rows, share),
        shaped((4, tok_rows, share), bf16),
        [],
        "join",
    )(here, *mixed_parts)
    got_across, gain_sum, small, mixed, output_weight_grad = fence(
        (got_across, gain_sum, small, mixed, output_weight_grad)
    )

    full_grad = scatter_heads(
        normed_own + got_core[0].astype(f32) + got_across.astype(f32), 1
    )
    small = stack_over(small, "i", 2, 0)
    gain_sum = gain_sum + swap(gain_sum, "o", 1)
    full_grad, gain_sum, small, inner_part = fence((full_grad, gain_sum, small, inner_part))

    own_wide = [near[q].astype(f32) for q in range(head_count)]
    square = sum(jnp.sum(a * a, axis=1, keepdims=True) for a in own_wide)
    inverse = lax.rsqrt(square / D + eps)
    gain_share = lax.dynamic_slice_in_dim(input_gain, head * share, share, 0)
    unit = own_wide[0] * inverse
    resid = jnp.sum(cotangent.astype(f32), axis=0)

    def weighted_of(values):
        return values * gain_share[None, :]

    def norm_row_sum(values):
        sums = jnp.sum(weighted_of(values) * unit, axis=1).reshape(-1, CHUNK)
        return add_all(sums, ("h",)).reshape(-1, 1)

    inner_back = scattered_inner(inner_part.reshape(PLANE, weight_rows, width))
    small = small.reshape((2, head_count) + shape)
    small_core = swap(small, "i", 1)
    for bit in bits_of("o")[1:]:
        gain_sum = gain_sum + swap(gain_sum, "o", bit)
    row_sum = norm_row_sum(full_grad)
    small_core, gain_sum, row_sum = fence((small_core, gain_sum, row_sum))
    gain_sum = add_inner(gain_sum, 2)
    heads_all = groups_all * head_count
    row_of = [shaped((1, INNER)), shaped((1, 2 * STATE)), shaped((1, heads_all))]
    state_weight_grad, *rows, step_rows = placed_call_once(
        partial(unpack_kernel, groups, state_rows),
        [
            shaped((D, 2 * STATE)),
            shaped((KERNEL, INNER)),
            row_of[0],
            row_of[0],
            shaped((KERNEL, 2 * STATE)),
            row_of[1],
            row_of[2],
            row_of[2],
            row_of[2],
            shaped((groups_all, D)),
        ],
        [pltpu.VMEM((8, D), f32)],
        "unpack",
    )(here, small, small_core)
    inner_back, step_rows = fence((inner_back, step_rows))
    taps_grad, bias_grad, gated_grad, state_taps_grad, *rows = rows
    state_bias_grad, shift_grad, rate_grad, skip_grad = rows
    input_gain_grad = gain_sum.reshape(D) / input_gain
    step_weight_grad = lax.dynamic_slice_in_dim(
        step_rows, (plane * PLANE + inner) * weight_rows, weight_rows, 1
    )
    step_weight_grad = jnp.transpose(step_weight_grad)[:, None, :]
    if groups % 8 == 0:
        input_weight_grad = placed_call(
            partial(weight_kernel, groups),
            [whole_block(weight_rows, width)] * (2 * PLANE),
            pl.BlockSpec((weight_rows, groups, 2 * P_SIZE), lambda r, place: (0, r ^ place[0], 0)),
            shaped((weight_rows, groups_all, 2 * P_SIZE)),
            [],
            "weight_grad",
        )(here, *gate_back, *inner_back)
    else:
        sides = []
        for back in (gate_back, inner_back):
            whole = jnp.zeros((PLANE, weight_rows, groups, P_SIZE), bf16)
            for r in range(PLANE):
                whole = put(whole, back[r].reshape(weight_rows, groups, P_SIZE), inner ^ r)
            sides.append(jnp.transpose(whole, (1, 0, 2, 3)))
        input_weight_grad = jnp.concatenate(sides, axis=3).astype(f32)
        input_weight_grad = input_weight_grad.reshape(weight_rows, groups_all, 2 * P_SIZE)

    tokens_grad = resid + inverse * (weighted_of(full_grad) - unit * (row_sum / D))
    return (
        mixed,
        tokens_grad,
        input_gain_grad,
        input_weight_grad,
        step_weight_grad,
        state_weight_grad,
        taps_grad,
        bias_grad.reshape(INNER),
        state_taps_grad,
        state_bias_grad.reshape(2 * STATE),
        shift_grad.reshape(heads_all),
        rate_grad.reshape(heads_all),
        skip_grad.reshape(heads_all),
        gated_grad.reshape(INNER),
        output_weight_grad,
    )


def solution(mesh):
    rows, heads = mesh.devices.shape
    cut = Mesh(mesh.devices.reshape(rows // PLANE, PLANE, heads), ("o", "i", "h"))
    both = ("o", "i")
    placed = (
        P(both, "h"),
        P(None, both, "h"),
        P(),
        P(),
        P(both, None, "h"),
        P(both, "h", None),
        P(),
        P(),
        P(),
        P(),
        P(),
        P(),
        P(),
        P(),
        P(),
        P(None, "h", both),
    )
    return jax.shard_map(
        shards,
        mesh=cut,
        in_specs=placed,
        out_specs=(
            P(None, both, "h"),
            P(both, "h"),
            P(),
            P(both, None, "h"),
            P(both, "h", None),
            P(),
            P(),
            P(),
            P(),
            P(),
            P(),
            P(),
            P(),
            P(),
            P(None, "h", both),
        ),
        check_vma=False,
    )
```
